256 devices in a mesh: blk: 64 (over x, z_hi, y, core), rep: 4 (over z_lo).
Axes of the slice: x: 4, y: 4, z: 8 (z_hi: 2, z_lo: 4; z = z_hi * 4 + z_lo), core: 2. Of those that a mesh axis runs over, the one named last changes fastest.
Arguments:
- src_points: bfloat16 [131072, 256], P(('blk', 'rep')), may hold values from -0.75 to 0.75
- src_log_mass: float32 [131072], P(('blk', 'rep')), may hold values from -3 to 3
- tgt_points: bfloat16 [65536, 256], P('blk'), may hold values from -0.75 to 0.75
- tgt_log_mass: float32 [65536], P('blk'), may hold values from -3 to 3
- initial_potential: float32 [65536], P('blk'), may hold values from -61 to 61
- pair_list: int32 [64, 7], replicated, may hold values from -1 to 63, as said below
- pair_count: int32 [64], replicated, may hold values from 1 to 7, as said below
Outputs:
- source_potential: float32 [131072], P(('blk', 'rep'))
- target_potential: float32 [65536], P('blk')
The draws below stay inside these ranges and needn't reach their ends.
Inputs may be any that keep to these rules, and one draw needn't show every extreme that they name: Row s of pair_list lists the target blocks kept by source block s: entry 0 is s itself, the next pair_count[s] - 1 entries are distinct blocks (s + o) mod 64 with 1 <= |o| <= 3, and the remaining entries are -1. `pair_count`: some block has 7 kept target blocks and some other block has 1.
All inputs are finite; a program needn't handle non-finite values.
Results may differ from the reference program's by a relative error of at most 0.0003.
Values may be sent and summed in bfloat16 or wider, within the bound.
No kernel may reach another device: no remote copies, remote signals or barrier semaphores. Data moves between devices by JAX's collectives and lax.ppermute only.
A program may use at most 64 MiB of HBM per device.

```python
import jax
import jax.numpy as jnp
from jax import lax

D = 256
T_BLK = 1024
REACH = 3
ITERS = 2
KMAX = 7
BLOCKS = 64
SRC_BLK = 2048
SOURCES = 131072
TARGETS = 65536


def kept_pairs(key):
    count_key, richest_key, order_key = jax.random.split(key, 3)
    block_ids = jnp.arange(BLOCKS, dtype=jnp.int32)
    counts = jax.random.randint(count_key, (BLOCKS,), 1, 4).astype(jnp.int32)
    richest = jax.random.randint(richest_key, (), 0, BLOCKS).astype(jnp.int32)
    counts = jnp.where(block_ids == richest, KMAX, counts)
    counts = jnp.where(block_ids == (richest + 1) % BLOCKS, 1, counts)
    row_keys = jax.random.split(order_key, BLOCKS)
    shuffled = jax.vmap(lambda one_key: jax.random.permutation(one_key, 2 * REACH))(row_keys).astype(jnp.int32)
    offsets = jnp.where(shuffled < REACH, shuffled - REACH, shuffled - REACH + 1)
    offsets = jnp.concatenate([jnp.zeros((BLOCKS, 1), jnp.int32), offsets], axis=1)
    targets = (block_ids[:, None] + offsets) % BLOCKS
    in_use = jnp.arange(KMAX, dtype=jnp.int32)[None, :] < counts[:, None]
    return (jnp.where(in_use, targets, -1).astype(jnp.int32), counts.astype(jnp.int32))


def draw_pair_list(key, part):
    return kept_pairs(key)[0]


def draw_pair_count(key, part):
    return kept_pairs(key)[1]


def draw_initial_potential(key, part):
    key = jax.random.fold_in(key, 11)
    rough_key = jax.random.fold_in(key, 1)
    return jax.random.uniform(rough_key, (TARGETS,), jnp.float32, -2.0, 2.0)


def shard_levels(key, extent, cuts, smallest, high):
    level = 1.0
    for position, shards_of in cuts:
        heights = jax.random.uniform(jax.random.fold_in(jax.random.fold_in(key, 6), position), (shards_of,), jnp.float32, smallest / len(cuts), high / len(cuts))
        level = level * jnp.repeat(jnp.exp(heights), extent[position] // shards_of).reshape((-1,) + (1,) * (len(extent) - 1 - position))
    return level


def gaussian(stream_key, dims, spread, most, cuts=(), held_as=jnp.bfloat16):
    array = spread * jax.random.normal(stream_key, dims, jnp.float32)
    if cuts:
        array = array * shard_levels(stream_key, dims, cuts, -0.22, 0.18)
    return jnp.clip(array, -most, most).astype(held_as)


def setup_inputs(seed: int = 0) -> dict:
    streams_of = jax.random.split(jax.random.key(seed), 8)
    return {
        "src_points": gaussian(streams_of[0], (SOURCES, D), 0.125, 0.75, ((0, 256),)),
        "src_log_mass": jnp.clip(jax.random.uniform(streams_of[1], (SOURCES,), jnp.float32, -3.0, 3.0) * shard_levels(streams_of[1], (SOURCES,), ((0, 256),), -0.4, 0.0), -3.0, 3.0),
        "tgt_points": gaussian(streams_of[2], (TARGETS, D), 0.125, 0.75, ((0, 64),)),
        "tgt_log_mass": jnp.clip(jax.random.uniform(streams_of[3], (TARGETS,), jnp.float32, -3.0, 3.0) * shard_levels(streams_of[3], (TARGETS,), ((0, 64),), -0.4, 0.0), -3.0, 3.0),
        "initial_potential": draw_initial_potential(jax.random.fold_in(streams_of[7], 71), 0),
        "pair_list": draw_pair_list(jax.random.fold_in(streams_of[7], 71), 0),
        "pair_count": draw_pair_count(jax.random.fold_in(streams_of[7], 71), 0),
    }


EPS_START = 0.5


def half_norms(points):
    widened = points.astype(jnp.float32)
    return 0.5 * jnp.sum(widened * widened, axis=1)


def scaled_cost(src, src_half, tgt, tgt_half, inv_eps):
    cross = lax.dot_general(src, tgt, (((1,), (1,)), ((), ())), preferred_element_type=jnp.float32)
    return (src_half[:, None] + tgt_half[None, :] - cross) * inv_eps


def log_sum(scores, axis):
    top = jnp.max(scores, axis=axis, keepdims=True)
    return jnp.squeeze(top, axis) + jnp.log(jnp.sum(jnp.exp(scores - top), axis=axis))


def keep_matrix(pair_list, pair_count):
    named = pair_list[:, :, None] == jnp.arange(BLOCKS, dtype=jnp.int32)[None, None, :]
    in_use = jnp.arange(KMAX, dtype=jnp.int32)[None, :, None] < pair_count[:, None, None]
    return jnp.any(named & in_use, axis=1)


def reference(src_points, src_log_mass, tgt_points, tgt_log_mass, initial_potential, pair_list, pair_count):
    keep_table = keep_matrix(pair_list, pair_count)
    src_blocks = src_points.reshape(BLOCKS, SRC_BLK, D)
    src_half = half_norms(src_points).reshape(BLOCKS, SRC_BLK)
    src_mass = src_log_mass.reshape(BLOCKS, SRC_BLK)
    tgt_blocks = tgt_points.reshape(BLOCKS, T_BLK, D)
    tgt_half = half_norms(tgt_points).reshape(BLOCKS, T_BLK)
    tgt_mass = tgt_log_mass.reshape(BLOCKS, T_BLK)
    offsets = jnp.arange(-REACH, REACH + 1, dtype=jnp.int32)
    block_ids = jnp.arange(BLOCKS, dtype=jnp.int32)
    source_pot = jnp.zeros((BLOCKS, SRC_BLK), jnp.float32)
    target_pot = initial_potential.reshape(BLOCKS, T_BLK)
    for sweep_index in range(ITERS):
        epsilon = EPS_START * 0.5 ** sweep_index
        inv_eps = 1.0 / epsilon
        shifted = tgt_mass + target_pot * inv_eps

        def row_update(block):
            window = (block + offsets) % BLOCKS
            cost = scaled_cost(src_blocks[block], src_half[block], tgt_blocks[window].reshape(KMAX * T_BLK, D), tgt_half[window].reshape(KMAX * T_BLK), inv_eps)
            scores = shifted[window].reshape(KMAX * T_BLK)[None, :] - cost
            allowed = jnp.repeat(keep_table[block, window], T_BLK, total_repeat_length=KMAX * T_BLK)
            scores = jnp.where(allowed[None, :], scores, -jnp.inf)
            return -epsilon * log_sum(scores, 1)

        source_pot = lax.map(row_update, block_ids)
        weighted = src_mass + source_pot * inv_eps

        def column_update(block):
            window = (block + offsets) % BLOCKS
            cost = scaled_cost(src_blocks[window].reshape(KMAX * SRC_BLK, D), src_half[window].reshape(KMAX * SRC_BLK), tgt_blocks[block], tgt_half[block], inv_eps)
            scores = weighted[window].reshape(KMAX * SRC_BLK)[:, None] - cost
            allowed = jnp.repeat(keep_table[window, block], SRC_BLK, total_repeat_length=KMAX * SRC_BLK)
            scores = jnp.where(allowed[:, None], scores, -jnp.inf)
            return -epsilon * log_sum(scores, 0)

        target_pot = lax.map(column_update, block_ids)
    return source_pot.reshape(SOURCES), target_pot.reshape(TARGETS)
```

```python
import functools
import math

import jax
import jax.numpy as jnp
from jax import lax
from jax.experimental import pallas as pl
from jax.experimental.pallas import tpu as pltpu
from jax.sharding import PartitionSpec as P

ITERS = 2
EPS_START = 0.5
NEG_FILL = -1e30
LOG2E = math.log2(math.e)
LN2 = math.log(2.0)
REPS = 4
SEGMENT = 8
TAIL = 16


def send(value, place, blocks):
    pairs = []
    for block in range(blocks):
        for rep in range(REPS):
            to_block, to_rep = place(block, rep)
            pairs.append((block * REPS + rep, to_block % blocks * REPS + to_rep))
    return lax.ppermute(value, ("blk", "rep"), pairs)


def along(steps, blocks):
    def place(block, rep):
        target = (block + steps) % blocks
        return target, rep if (target // SEGMENT - block // SEGMENT) % 2 == 0 else REPS - 1 - rep

    return place


def by_core(even_steps, odd_steps, blocks):
    even, odd = along(even_steps, blocks), along(odd_steps, blocks)
    return lambda block, rep: even(block, rep) if block % 2 == 0 else odd(block, rep)


def sibling(block, rep):
    return block ^ 1, rep


def rep_xor(k):
    return lambda block, rep: (block, rep ^ k)


def half_norms(points):
    widened = points.astype(jnp.float32)
    return 0.5 * jnp.sum(widened * widened, axis=1)


def terms(vector):
    first = lax.reduce_precision(vector, 8, 7)
    rest = vector - first
    second = lax.reduce_precision(rest, 8, 7)
    third = lax.reduce_precision(rest - second, 8, 7)
    return [part.astype(jnp.bfloat16) for part in (first, second, third)]


def from_terms(rows):
    widened = rows.astype(jnp.float32)
    return widened[..., 0:2, :] + widened[..., 2:4, :] + widened[..., 4:6, :]


def log2_merge(*parts):
    top = functools.reduce(jnp.maximum, parts)
    return top + jnp.log2(sum(jnp.exp2(part - top) for part in parts))


def spread_rows(vector_ref, index, bias_ref):
    count = bias_ref.shape[0] // 128
    for q in range(count):
        row = vector_ref[index, q : q + 1, :]
        bias_ref[q * 128 : (q + 1) * 128, :] = jnp.broadcast_to(row, (128, 128)).T


def fold(value, combine):
    rows = value.shape[0]
    while rows > 8:
        rows //= 2
        value = combine(value[:rows], value[rows:])
    return value


def scores_into(score_ref, bias_ref, left_ref, left_at, left_rows, right_ref, right_rows, lane_at, scale):
    tops = []
    for c in range(0, right_rows, 256):
        right = right_ref[c : c + 256, :]
        top = None
        for r in range(0, left_rows, 256):
            cross = lax.dot_general(
                left_ref[r : r + 256, :], right, (((1,), (1,)), ((), ())), preferred_element_type=jnp.float32
            )
            bias = bias_ref[left_at + r : left_at + r + 256, :]
            scores = cross * scale + jnp.concatenate([bias, bias], axis=1)
            score_ref[left_at + r : left_at + r + 256, lane_at + c : lane_at + c + 256] = scores
            part = fold(scores, jnp.maximum)
            top = part if top is None else jnp.maximum(top, part)
        tops.append(top)
    return tops


def totals_of(score_ref, rows, lane_at, top):
    total = jnp.zeros_like(top)
    for r in range(0, rows, 64):
        scores = score_ref[r : r + 64, lane_at : lane_at + 256].reshape(8, 8, 256)
        total = total + jnp.sum(jnp.exp2(scores - top[None]), axis=0)
    return total


def row_kernel(scale, flags, own, mate, *refs):
    targets, (bias_in, out, bias, score, top_ref, total_ref) = refs[:7], refs[7:]
    top_ref[...] = jnp.full(top_ref.shape, NEG_FILL, jnp.float32)
    total_ref[...] = jnp.zeros(total_ref.shape, jnp.float32)
    half = own.shape[0]
    columns = bias.shape[0]
    for n in range(7):

        @pl.when(flags[n] != 0)
        def _(n=n):
            spread_rows(bias_in, n, bias)
            for side, src in enumerate((own, mate)):
                tops = scores_into(score, bias, targets[n], 0, columns, src, half, side * half, scale)
                for i, block_top in enumerate(tops):
                    at = side * half + i * 256
                    old = top_ref[:, at : at + 256]
                    top = jnp.maximum(old, block_top)
                    total = totals_of(score, columns, at, top)
                    total_ref[:, at : at + 256] = total_ref[:, at : at + 256] * jnp.exp2(old - top) + total
                    top_ref[:, at : at + 256] = top

    top = top_ref[...]
    greatest = jnp.max(top, axis=0, keepdims=True)
    total = jnp.sum(total_ref[...] * jnp.exp2(top - greatest), axis=0, keepdims=True)
    out[...] = greatest + jnp.log2(total)


def column_kernel(scale, flags, own, mate, *refs):
    targets, (bias_in, out, bias, score) = refs[:7], refs[7:]
    out[...] = jnp.full(out.shape, NEG_FILL, jnp.float32)
    spread_rows(bias_in, 0, bias)
    half = own.shape[0]
    for n in range(7):

        @pl.when(flags[n] != 0)
        def _(n=n):
            columns = out.shape[1]
            first = scores_into(score, bias, own, 0, half, targets[n], columns, 0, scale)
            second = scores_into(score, bias, mate, half, half, targets[n], columns, 0, scale)
            for i, (a, b) in enumerate(zip(first, second)):
                top = jnp.max(jnp.maximum(a, b), axis=0, keepdims=True)
                total = totals_of(score, 2 * half, i * 256, jnp.broadcast_to(top, (8, 256)))
                total = jnp.sum(total, axis=0, keepdims=True)
                out[pl.ds(flags[7 + n], 1), i * 256 : (i + 1) * 256] = top + jnp.log2(total)


def call_rows(scale, flags, own, mate, targets, bias):
    half, columns = own.shape[0], targets[0].shape[0] - TAIL
    whole = pl.BlockSpec(memory_space=pltpu.VMEM)
    return pl.pallas_call(
        functools.partial(row_kernel, scale),
        out_shape=jax.ShapeDtypeStruct((1, 2 * half), jnp.float32),
        in_specs=[pl.BlockSpec(memory_space=pltpu.SMEM)] + [whole] * 10,
        out_specs=whole,
        scratch_shapes=[
            pltpu.VMEM((columns, 128), jnp.float32),
            pltpu.VMEM((columns, 2 * half), jnp.float32),
            pltpu.VMEM((8, 2 * half), jnp.float32),
            pltpu.VMEM((8, 2 * half), jnp.float32),
        ],
        compiler_params=pltpu.CompilerParams(vmem_limit_bytes=32 * 2**20),
        name="rows",
    )(flags, own, mate, *targets, bias)


def call_columns(scale, flags, own, mate, targets, bias):
    half, columns = own.shape[0], targets[0].shape[0] - TAIL
    whole = pl.BlockSpec(memory_space=pltpu.VMEM)
    return pl.pallas_call(
        functools.partial(column_kernel, scale),
        out_shape=jax.ShapeDtypeStruct((8, columns), jnp.float32),
        in_specs=[pl.BlockSpec(memory_space=pltpu.SMEM)] + [whole] * 10,
        out_specs=whole,
        scratch_shapes=[
            pltpu.VMEM((2 * half, 128), jnp.float32),
            pltpu.VMEM((2 * half, columns), jnp.float32),
        ],
        compiler_params=pltpu.CompilerParams(vmem_limit_bytes=32 * 2**20),
        name="columns",
    )(flags, own, mate, *targets, bias)


def fill_rows(value, before, after):
    return jnp.pad(value, ((before, after), (0, 0)), constant_values=NEG_FILL)


def local(src_points, src_log_mass, tgt_points, tgt_log_mass, initial_potential, pair_list, pair_count):
    block = lax.axis_index("blk")
    rep = lax.axis_index("rep")
    blocks = lax.axis_size("blk")
    core = block % 2
    half_index = (rep % 2) ^ ((block // SEGMENT) % 2)
    rows = src_points.shape[0]
    width = tgt_points.shape[0]
    columns = width // 2

    def my_half(value):
        return lax.dynamic_slice_in_dim(value, half_index * columns, columns, 0)

    first_scale = LOG2E / EPS_START
    points = my_half(tgt_points)
    masses = my_half(tgt_log_mass) * LOG2E
    bias = masses + (my_half(initial_potential) - half_norms(points)) * first_scale
    tail = [part.reshape(-1, points.shape[1]) for part in terms(bias) + terms(masses)]
    tail.append(jnp.zeros((TAIL - 6 * columns // points.shape[1], points.shape[1]), jnp.bfloat16))
    message = jnp.concatenate([points] + tail, axis=0)

    before = send(message, along(2, blocks), blocks)
    after = send(message, along(-2, blocks), blocks)
    third = send(message, by_core(-3, 3, blocks), blocks)
    beside = send(message, sibling, blocks)
    mate = send(src_points, rep_xor(1), blocks)
    before_beside = send(before, sibling, blocks)
    after_beside = send(after, sibling, blocks)
    targets = [message, beside, before, before_beside, after, after_beside, third]

    even_slots = jnp.array([3, 4, 1, 2, 5, 6, 0], jnp.int32)
    odd_slots = jnp.array([4, 3, 2, 1, 6, 5, 7], jnp.int32)
    slots = jnp.where(core == 0, even_slots, odd_slots)
    names = (block - core - 3 + slots) % blocks
    row_names = pair_list[block]
    in_use = jnp.arange(row_names.shape[0], dtype=jnp.int32) < pair_count[block]
    kept = jnp.any((row_names[None, :] == names[:, None]) & in_use[None, :], axis=1)
    flags = jnp.concatenate([kept.astype(jnp.int32), slots])

    tails = jnp.stack([target[columns:] for target in targets])
    biases = from_terms(tails[:, 0:6]).reshape(7, columns // 128, 128)
    window_masses = from_terms(tails[:, 6:12]).reshape(7, columns // 128, 128)
    src_masses = src_log_mass * LOG2E

    for sweep in range(ITERS):
        epsilon = EPS_START * 0.5**sweep
        scale = LOG2E / epsilon
        part = call_rows(scale, flags, src_points, mate, targets, biases).reshape(-1)
        if sweep == 0:
            got = send(jnp.concatenate([part, src_masses]), rep_xor(1), blocks)
            both_masses = jnp.concatenate([src_masses, got[2 * rows :]])
        else:
            got = send(part, rep_xor(1), blocks)
        row_sums = log2_merge(part, jnp.concatenate([got[rows : 2 * rows], got[:rows]]))
        weighted = (both_masses - row_sums).reshape(1, 2 * rows // 128, 128)
        part = call_columns(scale, flags, src_points, mate, targets, weighted)
        chip = log2_merge(
            part,
            send(part, sibling, blocks),
            send(part, rep_xor(2), blocks),
            send(part, lambda b, r: (b ^ 1, r ^ 2), blocks),
        )
        forward = core == 0
        if sweep + 1 < ITERS:
            got = []
            for n in (1, 2, 3):
                kept_rows = 8 - 2 * n
                out = jnp.where(forward, chip[2 * n :], chip[:kept_rows])
                out = send(out, by_core(2 * n, -2 * n, blocks), blocks)
                got.append(
                    jnp.where(forward, fill_rows(out, 0, 2 * n), fill_rows(out, 2 * n, 0))
                )
            side = log2_merge(*got)
            column_sums = log2_merge(chip, side, send(side, sibling, blocks))
            mine = jnp.where(
                core == 0,
                jnp.stack([column_sums[i] for i in (3, 4, 1, 2, 5, 6, 0)]),
                jnp.stack([column_sums[i] for i in (4, 3, 2, 1, 6, 5, 7)]),
            )
            biases = window_masses - 2.0 * mine.reshape(7, columns // 128, 128)
        else:
            near = jnp.where(forward, chip[5:7], chip[1:3])
            near = send(near, by_core(2, -2, blocks), blocks)
            far = jnp.where(forward, chip[7], chip[0])
            far = send(far, by_core(4, -4, blocks), blocks)
            empty = jnp.full_like(far, NEG_FILL)
            far = jnp.where(forward, jnp.stack([far, empty]), jnp.stack([empty, far]))
            side = log2_merge(near, far)
            column_sums = log2_merge(chip[3:5], side, send(side, sibling, blocks))
            mine = jnp.where(core == 0, column_sums[0], column_sums[1])
            other = send(mine, rep_xor(1), blocks)
            whole = jnp.where(
                half_index == 0, jnp.concatenate([mine, other]), jnp.concatenate([other, mine])
            )
            source_pot = half_norms(src_points) - (epsilon * LN2) * row_sums[:rows]
            target_pot = half_norms(tgt_points) - (epsilon * LN2) * whole
    return source_pot, target_pot


def solution(mesh):
    in_specs = (
        P(("blk", "rep"), None),
        P(("blk", "rep")),
        P("blk", None),
        P("blk"),
        P("blk"),
        P(),
        P(),
    )
    out_specs = (P(("blk", "rep")), P("blk"))
    return jax.shard_map(local, mesh=mesh, in_specs=in_specs, out_specs=out_specs, check_vma=False)
```

```python
import functools

import jax
import jax.numpy as jnp
from jax import lax
from jax.experimental import pallas as pl
from jax.experimental.pallas import tpu as pltpu
from jax.sharding import PartitionSpec as P

ITERS = 2
EPS_START = 0.5
NEG_FILL = -1e30
BUFFERS = 8
REPS = 4
SEGMENT = 8
TAIL = 16


def send(value, place, blocks):
    pairs = []
    for block in range(blocks):
        for rep in range(REPS):
            to_block, to_rep = place(block, rep)
            pairs.append((block * REPS + rep, to_block % blocks * REPS + to_rep))
    return lax.ppermute(value, ("blk", "rep"), pairs)


def along(steps, blocks):
    def place(block, rep):
        target = (block + steps) % blocks
        return target, rep if (target // SEGMENT - block // SEGMENT) % 2 == 0 else REPS - 1 - rep

    return place


def by_core(even_steps, odd_steps, blocks):
    even, odd = along(even_steps, blocks), along(odd_steps, blocks)
    return lambda block, rep: even(block, rep) if block % 2 == 0 else odd(block, rep)


def sibling(block, rep):
    return block ^ 1, rep


def diagonal(block, rep):
    return block ^ 1, rep ^ 1


def half_norms(points):
    widened = points.astype(jnp.float32)
    return 0.5 * jnp.sum(widened * widened, axis=1)


def terms(vector):
    first = lax.reduce_precision(vector, 8, 7)
    rest = vector - first
    second = lax.reduce_precision(rest, 8, 7)
    third = lax.reduce_precision(rest - second, 8, 7)
    return [part.astype(jnp.bfloat16) for part in (first, second, third)]


def from_terms(rows, which):
    rows = rows[6 * which : 6 * which + 6]
    vector = rows[0:2] + rows[2:4] + rows[4:6]
    return [vector[q // 2 : q // 2 + 1, q % 2 * 128 : q % 2 * 128 + 128] for q in range(4)]


def log_merge(*parts):
    top = functools.reduce(jnp.maximum, parts)
    return top + jnp.log(sum(jnp.exp(part - top) for part in parts))


def spread_rows(vector_ref, bias_ref):
    for q in range(bias_ref.shape[0] // 128):
        row = vector_ref[q : q + 1, :]
        bias_ref[q * 128 : (q + 1) * 128, :] = jnp.broadcast_to(row, (128, 128)).T


def fold(value, combine):
    rows = value.shape[0]
    while rows > 8:
        rows //= 2
        value = combine(value[:rows], value[rows:])
    return value


def row_update(cross, bias, twice, side, half, top_ref, total_ref):
    step = 64
    for r in range(0, half, step):
        at = side * half + r
        scores = []
        for q, term in enumerate(bias):
            part = cross[at : at + step, q * 128 : (q + 1) * 128]
            scores.append((part + part if twice else part) + term)
        old = top_ref[at : at + step, :]
        top = jnp.maximum(old, functools.reduce(jnp.maximum, scores))
        total = functools.reduce(jnp.add, [jnp.exp(part - top) for part in scores])
        total_ref[at : at + step, :] = total_ref[at : at + step, :] * jnp.exp(old - top) + total
        top_ref[at : at + step, :] = top


def row_finish(top_ref, total_ref, out):
    for q in range(out.shape[0]):
        top = top_ref[q * 128 : (q + 1) * 128, :].T
        greatest = jnp.max(top, axis=0, keepdims=True)
        total = total_ref[q * 128 : (q + 1) * 128, :].T * jnp.exp(top - greatest)
        out[q : q + 1, :] = greatest + jnp.log(jnp.sum(total, axis=0, keepdims=True))


def first_kernel(numbers, first, last, flags, *refs):
    count = len(numbers)
    sources, targets = refs[:2], refs[2 : 2 + count]
    refs = refs[2 + count :]
    if not first:
        refs = refs[2:]
    cross, top_ref, total_ref, masses = refs[:4]
    if first:
        top_ref[...] = jnp.full(top_ref.shape, NEG_FILL, jnp.float32)
        total_ref[...] = jnp.zeros(total_ref.shape, jnp.float32)
    half = sources[0].shape[0]
    width = cross.shape[2]
    for k, number in enumerate(numbers):
        tail = targets[k][width:, :].astype(jnp.float32)
        for q, row in enumerate(from_terms(tail, 1)):
            masses[k, q : q + 1, :] = row
        bias = from_terms(tail, 0)
        for side, src in enumerate(sources):

            @pl.when(flags[side * BUFFERS + number] != 0)
            def _(k=k, side=side, src=src, bias=bias):
                for r in range(0, half, 256):
                    for c in range(0, width, 256):
                        cross[k, side * half + r : side * half + r + 256, c : c + 256] = lax.dot_general(
                            src[r : r + 256, :],
                            targets[k][c : c + 256, :],
                            (((1,), (1,)), ((), ())),
                            preferred_element_type=jnp.float32,
                        )
                row_update(cross.at[k], bias, False, side, half, top_ref, total_ref)

    if last:
        row_finish(top_ref, total_ref, refs[4])


def row_kernel(groups, flags, *refs):
    count = len(groups)
    crosses, masses, (sums, out, top_ref, total_ref) = refs[:count], refs[count : 2 * count], refs[2 * count :]
    top_ref[...] = jnp.full(top_ref.shape, NEG_FILL, jnp.float32)
    total_ref[...] = jnp.zeros(total_ref.shape, jnp.float32)
    half = top_ref.shape[0] // 2
    for numbers, cross, mass in zip(groups, crosses, masses):
        for k, number in enumerate(numbers):
            column_sums = sums[flags[2 * BUFFERS + number]]
            bias = [mass[k, q : q + 1, :] - 2.0 * column_sums[q : q + 1, :] for q in range(mass.shape[1])]
            for side in range(2):

                @pl.when(flags[side * BUFFERS + number] != 0)
                def _(k=k, side=side, cross=cross, bias=bias):
                    row_update(cross.at[k], bias, True, side, half, top_ref, total_ref)

    row_finish(top_ref, total_ref, out)


def column_kernel(groups, twice, flags, *refs):
    crosses, (weights, out, bias, top_ref, total_ref) = refs[: len(groups)], refs[len(groups) :]
    out[...] = jnp.full(out.shape, NEG_FILL, jnp.float32)
    spread_rows(weights, bias)
    half = bias.shape[0] // 2
    step = 128
    for numbers, cross in zip(groups, crosses):
        pieces = cross.shape[2] // 128
        for k, number in enumerate(numbers):
            top_ref[...] = jnp.full(top_ref.shape, NEG_FILL, jnp.float32)
            total_ref[...] = jnp.zeros(total_ref.shape, jnp.float32)
            for side in range(2):

                @pl.when(flags[side * BUFFERS + number] != 0)
                def _(k=k, side=side, cross=cross):
                    tops = [top_ref[:, q * 128 : (q + 1) * 128] for q in range(pieces)]
                    totals = [total_ref[:, q * 128 : (q + 1) * 128] for q in range(pieces)]
                    for r in range(side * half, (side + 1) * half, step):
                        weight = bias[r : r + step, :]
                        for q in range(pieces):
                            part = cross[k, r : r + step, q * 128 : (q + 1) * 128]
                            scores = (part + part if twice else part) + weight
                            top = jnp.maximum(tops[q], fold(scores, jnp.maximum))
                            total = jnp.sum(jnp.exp(scores.reshape(-1, 8, 128) - top[None]), axis=0)
                            totals[q] = totals[q] * jnp.exp(tops[q] - top) + total
                            tops[q] = top
                    for q in range(pieces):
                        top_ref[:, q * 128 : (q + 1) * 128] = tops[q]
                        total_ref[:, q * 128 : (q + 1) * 128] = totals[q]

            @pl.when((flags[number] | flags[BUFFERS + number]) != 0)
            def _(number=number):
                for q in range(pieces):
                    top = top_ref[:, q * 128 : (q + 1) * 128]
                    greatest = jnp.max(top, axis=0, keepdims=True)
                    total = total_ref[:, q * 128 : (q + 1) * 128] * jnp.exp(top - greatest)
                    out[flags[2 * BUFFERS + number], q : q + 1, :] = greatest + jnp.log(
                        jnp.sum(total, axis=0, keepdims=True)
                    )


WHOLE = pl.BlockSpec(memory_space=pltpu.VMEM)
SCALARS = pl.BlockSpec(memory_space=pltpu.SMEM)
PARAMS = pltpu.CompilerParams(vmem_limit_bytes=20 * 2**20)


def in_vmem(value):
    return pltpu.with_memory_space_constraint(value, pltpu.VMEM)


def call_first(numbers, first, last, flags, sources, targets, state):
    rows, columns = 2 * sources[0].shape[0], targets[0].shape[0] - TAIL
    out_shape = [pltpu.VMEM((len(numbers), rows, columns), jnp.float32)]
    out_shape += [pltpu.VMEM((rows, 128), jnp.float32)] * 2
    out_shape.append(jax.ShapeDtypeStruct((len(numbers), columns // 128, 128), jnp.float32))
    if last:
        out_shape.append(jax.ShapeDtypeStruct((rows // 128, 128), jnp.float32))
    operands = [flags, *sources, *targets]
    aliases = {}
    if not first:
        aliases = {len(operands): 1, len(operands) + 1: 2}
        operands += [in_vmem(value) for value in state]
    return pl.pallas_call(
        functools.partial(first_kernel, numbers, first, last),
        out_shape=out_shape,
        in_specs=[SCALARS] + [WHOLE] * (len(operands) - 1),
        out_specs=[WHOLE] * len(out_shape),
        input_output_aliases=aliases,
        compiler_params=PARAMS,
        cost_estimate=pl.CostEstimate(
            flops=2 * len(numbers) * rows * columns * sources[0].shape[1],
            bytes_accessed=len(numbers) * rows * columns,
            transcendentals=len(numbers) * rows * columns,
        ),
        name="first_rows",
    )(*operands)


def call_rows(groups, flags, crosses, masses, sums):
    rows = crosses[0].shape[1]
    return pl.pallas_call(
        functools.partial(row_kernel, groups),
        out_shape=jax.ShapeDtypeStruct((rows // 128, 128), jnp.float32),
        in_specs=[SCALARS] + [WHOLE] * (2 * len(crosses) + 1),
        out_specs=WHOLE,
        scratch_shapes=[pltpu.VMEM((rows, 128), jnp.float32)] * 2,
        compiler_params=PARAMS,
        name="rows",
    )(flags, *map(in_vmem, crosses), *masses, sums)


def call_columns(groups, twice, flags, crosses, weights):
    rows, columns = crosses[0].shape[1:]
    return pl.pallas_call(
        functools.partial(column_kernel, groups, twice),
        out_shape=jax.ShapeDtypeStruct((BUFFERS, columns // 128, 128), jnp.float32),
        in_specs=[SCALARS] + [WHOLE] * (len(crosses) + 1),
        out_specs=WHOLE,
        scratch_shapes=[pltpu.VMEM((rows, 128), jnp.float32)] + [pltpu.VMEM((8, columns), jnp.float32)] * 2,
        compiler_params=PARAMS,
        name="columns",
    )(flags, *map(in_vmem, crosses), weights)


def fill_rows(value, before, after):
    return jnp.pad(value, ((before, after), (0, 0), (0, 0)), constant_values=NEG_FILL)


def local(src_points, src_log_mass, tgt_points, tgt_log_mass, initial_potential, pair_list, pair_count):
    block = lax.axis_index("blk")
    rep = lax.axis_index("rep")
    blocks = lax.axis_size("blk")
    core = block % 2
    half_index = (rep % 2) ^ ((block // SEGMENT) % 2)
    rows = src_points.shape[0]
    width = tgt_points.shape[0]
    columns = width // 2

    def my_half(value):
        return lax.dynamic_slice_in_dim(value, half_index * columns, columns, 0)

    first_scale = 1.0 / EPS_START
    points = my_half(tgt_points)
    masses = my_half(tgt_log_mass)
    bias = masses + (my_half(initial_potential) - half_norms(points)) * first_scale
    tail = [part.reshape(-1, points.shape[1]) for part in terms(bias) + terms(masses)]
    tail.append(jnp.zeros((TAIL - 6 * columns // points.shape[1], points.shape[1]), jnp.bfloat16))
    message = jnp.concatenate([points * jnp.bfloat16(first_scale)] + tail, axis=0)

    before = send(message, along(2, blocks), blocks)
    after = send(message, along(-2, blocks), blocks)
    third = send(message, by_core(-3, 3, blocks), blocks)
    beside = send(message, sibling, blocks)
    mate = send(src_points, diagonal, blocks)
    sources = [src_points, mate]
    before_beside = send(before, sibling, blocks)
    after_beside = send(after, sibling, blocks)
    third_beside = send(third, sibling, blocks)
    targets = [message, beside, before, after, third, before_beside, after_beside, third_beside]
    groups = ((0, 1), (2, 3, 4), (5, 6, 7))

    even_slots = (3, 4, 1, 5, 0, 2, 6, 7)
    odd_slots = (4, 3, 2, 6, 7, 1, 5, 0)
    slots = jnp.where(core == 0, jnp.array(even_slots, jnp.int32), jnp.array(odd_slots, jnp.int32))
    names = (block - core - 3 + slots) % blocks

    def kept(source_block):
        row_names = pair_list[source_block]
        in_use = jnp.arange(row_names.shape[0], dtype=jnp.int32) < pair_count[source_block]
        return jnp.any((row_names[None, :] == names[:, None]) & in_use[None, :], axis=1).astype(jnp.int32)

    flags = jnp.concatenate([kept(block), kept(block + 1 - 2 * core), slots])

    window_masses, crosses, state = [], [], ()
    for numbers in groups:
        cross, top, total, masses, *sums = call_first(
            numbers,
            numbers is groups[0],
            numbers is groups[-1],
            flags,
            sources,
            [targets[n] for n in numbers],
            state,
        )
        state = (top, total)
        crosses.append(cross)
        window_masses.append(masses)
    part = sums[0].reshape(-1)

    for sweep in range(ITERS):
        epsilon = EPS_START * 0.5**sweep
        if sweep == 0:
            got = send(jnp.concatenate([part, src_log_mass]), diagonal, blocks)
            both_masses = jnp.concatenate([src_log_mass, got[2 * rows :]])
        else:
            part = call_rows(groups, flags, crosses, window_masses, column_sums).reshape(-1)
            got = send(part, diagonal, blocks)
        row_sums = log_merge(part, jnp.concatenate([got[rows : 2 * rows], got[:rows]]))
        weighted = (both_masses - row_sums).reshape(2 * rows // 128, 128)
        part = call_columns(groups, sweep > 0, flags, crosses, weighted)
        chip = log_merge(
            part,
            send(part, sibling, blocks),
            send(part, lambda b, r: (b, r ^ 2), blocks),
            send(part, lambda b, r: (b ^ 1, r ^ 2), blocks),
        )
        forward = core == 0
        if sweep + 1 < ITERS:
            got = []
            for n in (1, 2, 3):
                kept_rows = 8 - 2 * n
                out = jnp.where(forward, chip[2 * n :], chip[:kept_rows])
                out = send(out, by_core(2 * n, -2 * n, blocks), blocks)
                got.append(
                    jnp.where(forward, fill_rows(out, 0, 2 * n), fill_rows(out, 2 * n, 0))
                )
            side = log_merge(*got)
            column_sums = log_merge(chip, side, send(side, sibling, blocks))
        else:
            near = jnp.where(forward, chip[5:7], chip[1:3])
            near = send(near, by_core(2, -2, blocks), blocks)
            far = jnp.where(forward, chip[7], chip[0])
            far = send(far, by_core(4, -4, blocks), blocks)
            empty = jnp.full_like(far, NEG_FILL)
            far = jnp.where(forward, jnp.stack([far, empty]), jnp.stack([empty, far]))
            side = log_merge(near, far)
            column_sums = log_merge(chip[3:5], side, send(side, sibling, blocks))
            mine = jnp.where(core == 0, column_sums[0], column_sums[1]).reshape(columns)
            other = send(mine, lambda b, r: (b, r ^ 1), blocks)
            whole = jnp.where(
                half_index == 0, jnp.concatenate([mine, other]), jnp.concatenate([other, mine])
            )
            source_pot = half_norms(src_points) - epsilon * row_sums[:rows]
            target_pot = half_norms(tgt_points) - epsilon * whole
    return source_pot, target_pot


def solution(mesh):
    in_specs = (
        P(("blk", "rep"), None),
        P(("blk", "rep")),
        P("blk", None),
        P("blk"),
        P("blk"),
        P(),
        P(),
    )
    out_specs = (P(("blk", "rep")), P("blk"))
    return jax.shard_map(local, mesh=mesh, in_specs=in_specs, out_specs=out_specs, check_vma=False)
```

```python
import functools

import jax
import jax.numpy as jnp
from jax import lax
from jax.experimental import pallas as pl
from jax.experimental.pallas import tpu as pltpu
from jax.sharding import PartitionSpec as P

ITERS = 2
EPS_START = 0.5
NEG_FILL = -1e30
ROW_UNROLL = 8
COLUMN_UNROLL = 4
BUFFERS = 8
REPS = 4
SEGMENT = 8
TAIL = 16


def send(value, place, blocks):
    pairs = []
    for block in range(blocks):
        for rep in range(REPS):
            to_block, to_rep = place(block, rep)
            pairs.append((block * REPS + rep, to_block % blocks * REPS + to_rep))
    return lax.ppermute(value, ("blk", "rep"), pairs)


def along(steps, blocks):
    def place(block, rep):
        target = (block + steps) % blocks
        return target, rep if (target // SEGMENT - block // SEGMENT) % 2 == 0 else REPS - 1 - rep

    return place


def by_core(even_steps, odd_steps, blocks):
    even, odd = along(even_steps, blocks), along(odd_steps, blocks)
    return lambda block, rep: even(block, rep) if block % 2 == 0 else odd(block, rep)


def sibling(block, rep):
    return block ^ 1, rep


def diagonal(block, rep):
    return block ^ 1, rep ^ 1


def half_norms(points):
    widened = points.astype(jnp.float32)
    return 0.5 * jnp.sum(widened * widened, axis=1)


def terms(vector):
    first = lax.reduce_precision(vector, 8, 7)
    rest = vector - first
    second = lax.reduce_precision(rest, 8, 7)
    third = lax.reduce_precision(rest - second, 8, 7)
    return [part.astype(jnp.bfloat16) for part in (first, second, third)]


def from_terms(rows, which):
    rows = rows[6 * which : 6 * which + 6]
    vector = rows[0:2] + rows[2:4] + rows[4:6]
    return [vector[q // 2 : q // 2 + 1, q % 2 * 128 : q % 2 * 128 + 128] for q in range(4)]


def log_merge(*parts):
    top = functools.reduce(jnp.maximum, parts)
    return top + jnp.log(sum(jnp.exp(part - top) for part in parts))


def spread_rows(vector_ref, bias_ref):
    for q in range(bias_ref.shape[0] // 128):
        row = vector_ref[q : q + 1, :]
        bias_ref[q * 128 : (q + 1) * 128, :] = jnp.broadcast_to(row, (128, 128)).T


def fold(value, combine):
    rows = value.shape[0]
    while rows > 8:
        rows //= 2
        value = combine(value[:rows], value[rows:])
    return value


def row_update(cross_ref, index, bias, twice, side, half, top_ref, total_ref):
    step = 64

    def chunk(r, _):
        at = pl.ds(pl.multiple_of(side * half + r * step, step), step)
        scores = []
        for q, term in enumerate(bias):
            part = cross_ref[index, at, q * 128 : (q + 1) * 128]
            scores.append((part + part if twice else part) + term)
        old = top_ref[at, :]
        top = jnp.maximum(old, functools.reduce(jnp.maximum, scores))
        total = functools.reduce(jnp.add, [jnp.exp(part - top) for part in scores])
        total_ref[at, :] = total_ref[at, :] * jnp.exp(old - top) + total
        top_ref[at, :] = top
        return 0

    lax.fori_loop(0, half // step, chunk, 0, unroll=ROW_UNROLL)


def row_finish(top_ref, total_ref, out):
    for q in range(out.shape[0]):
        top = top_ref[q * 128 : (q + 1) * 128, :].T
        greatest = jnp.max(top, axis=0, keepdims=True)
        total = total_ref[q * 128 : (q + 1) * 128, :].T * jnp.exp(top - greatest)
        out[q : q + 1, :] = greatest + jnp.log(jnp.sum(total, axis=0, keepdims=True))


def each_kept(flags, first, count, body):
    def unit(u, _):
        number, side = first + lax.div(u, 2), lax.rem(u, 2)

        @pl.when(flags[side * BUFFERS + number] != 0)
        def _():
            body(number, side)

        return 0

    lax.fori_loop(0, 2 * count, unit, 0)


def first_kernel(numbers, first, last, flags, *refs):
    count = len(numbers)
    sources, targets = refs[:2], refs[2 : 2 + count]
    refs = refs[2 + count :]
    if not first:
        refs = refs[4:]
    cross, masses, top_ref, total_ref = refs[:4]
    src_ref, tgt_ref, bias_ref = refs[-3:]
    if first:
        top_ref[...] = jnp.full(top_ref.shape, NEG_FILL, jnp.float32)
        total_ref[...] = jnp.zeros(total_ref.shape, jnp.float32)
    half = sources[0].shape[0]
    width = cross.shape[2]
    for side, src in enumerate(sources):
        src_ref[side] = src[...]
    for k, number in enumerate(numbers):
        tgt_ref[k] = targets[k][:width, :]
        tail = targets[k][width:, :].astype(jnp.float32)
        for q, (row, mass) in enumerate(zip(from_terms(tail, 0), from_terms(tail, 1))):
            bias_ref[k, q : q + 1, :] = row
            masses[number, q : q + 1, :] = mass

    def body(number, side):
        k = number - numbers[0]
        for c in range(0, width, 256):
            for r in range(0, half, 256):
                at = pl.ds(pl.multiple_of(side * half + r, 256), 256)
                cross[number, at, c : c + 256] = lax.dot_general(
                    src_ref[side, r : r + 256, :],
                    tgt_ref[k, c : c + 256, :],
                    (((1,), (1,)), ((), ())),
                    preferred_element_type=jnp.float32,
                )
        bias = [bias_ref[k, q : q + 1, :] for q in range(width // 128)]
        row_update(cross, number, bias, False, side, half, top_ref, total_ref)

    each_kept(flags, numbers[0], count, body)
    if last:
        row_finish(top_ref, total_ref, refs[4])


def row_kernel(flags, cross, masses, sums, out, top_ref, total_ref):
    top_ref[...] = jnp.full(top_ref.shape, NEG_FILL, jnp.float32)
    total_ref[...] = jnp.zeros(total_ref.shape, jnp.float32)
    half = top_ref.shape[0] // 2

    def body(number, side):
        slot = flags[2 * BUFFERS + number]
        bias = [
            masses[number, q : q + 1, :] - 2.0 * sums[slot, q : q + 1, :] for q in range(masses.shape[1])
        ]
        row_update(cross, number, bias, True, side, half, top_ref, total_ref)

    each_kept(flags, 0, BUFFERS, body)
    row_finish(top_ref, total_ref, out)


def column_kernel(twice, flags, cross, weights, out, bias, top_ref, total_ref):
    out[...] = jnp.full(out.shape, NEG_FILL, jnp.float32)
    top_ref[...] = jnp.full(top_ref.shape, NEG_FILL, jnp.float32)
    total_ref[...] = jnp.zeros(total_ref.shape, jnp.float32)
    spread_rows(weights, bias)
    half = bias.shape[0] // 2
    pieces = cross.shape[2] // 128
    step = 128

    def body(number, side):
        def chunk(r, state):
            at = pl.ds(pl.multiple_of(side * half + r * step, step), step)
            weight = bias[at, :]
            tops, totals = [], []
            for q in range(pieces):
                part = cross[number, at, q * 128 : (q + 1) * 128]
                scores = (part + part if twice else part) + weight
                top = jnp.maximum(state[0][q], fold(scores, jnp.maximum))
                total = jnp.sum(jnp.exp(scores.reshape(-1, 8, 128) - top[None]), axis=0)
                totals.append(state[1][q] * jnp.exp(state[0][q] - top) + total)
                tops.append(top)
            return tuple(tops), tuple(totals)

        state = (
            tuple(top_ref[number, :, q * 128 : (q + 1) * 128] for q in range(pieces)),
            tuple(total_ref[number, :, q * 128 : (q + 1) * 128] for q in range(pieces)),
        )
        tops, totals = lax.fori_loop(0, half // step, chunk, state, unroll=COLUMN_UNROLL)
        for q in range(pieces):
            top_ref[number, :, q * 128 : (q + 1) * 128] = tops[q]
            total_ref[number, :, q * 128 : (q + 1) * 128] = totals[q]

    each_kept(flags, 0, BUFFERS, body)

    def finish(number, _):
        @pl.when((flags[number] | flags[BUFFERS + number]) != 0)
        def _():
            for q in range(pieces):
                top = top_ref[number, :, q * 128 : (q + 1) * 128]
                greatest = jnp.max(top, axis=0, keepdims=True)
                total = total_ref[number, :, q * 128 : (q + 1) * 128] * jnp.exp(top - greatest)
                out[flags[2 * BUFFERS + number], q : q + 1, :] = greatest + jnp.log(
                    jnp.sum(total, axis=0, keepdims=True)
                )

        return 0

    lax.fori_loop(0, BUFFERS, finish, 0)


WHOLE = pl.BlockSpec(memory_space=pltpu.VMEM)
SCALARS = pl.BlockSpec(memory_space=pltpu.SMEM)
PARAMS = pltpu.CompilerParams(vmem_limit_bytes=20 * 2**20)


def in_vmem(value):
    return pltpu.with_memory_space_constraint(value, pltpu.VMEM)


def call_first(numbers, first, last, flags, sources, targets, state):
    half, depth = sources[0].shape
    rows, columns, count = 2 * half, targets[0].shape[0] - TAIL, len(numbers)
    out_shape = [
        pltpu.VMEM((BUFFERS, rows, columns), jnp.float32),
        pltpu.VMEM((BUFFERS, columns // 128, 128), jnp.float32),
        pltpu.VMEM((rows, 128), jnp.float32),
        pltpu.VMEM((rows, 128), jnp.float32),
    ]
    if last:
        out_shape.append(jax.ShapeDtypeStruct((rows // 128, 128), jnp.float32))
    operands = [flags, *sources, *targets]
    aliases = {}
    if not first:
        aliases = {len(operands) + i: i for i in range(4)}
        operands += [in_vmem(value) for value in state]
    return pl.pallas_call(
        functools.partial(first_kernel, numbers, first, last),
        out_shape=out_shape,
        in_specs=[SCALARS] + [WHOLE] * (len(operands) - 1),
        out_specs=[WHOLE] * len(out_shape),
        scratch_shapes=[
            pltpu.VMEM((2, half, depth), jnp.bfloat16),
            pltpu.VMEM((count, columns, depth), jnp.bfloat16),
            pltpu.VMEM((count, columns // 128, 128), jnp.float32),
        ],
        input_output_aliases=aliases,
        compiler_params=PARAMS,
        cost_estimate=pl.CostEstimate(
            flops=2 * count * rows * columns * depth,
            bytes_accessed=count * rows * columns,
            transcendentals=count * rows * columns,
        ),
        name="first_rows",
    )(*operands)


def call_rows(flags, cross, masses, sums):
    rows = cross.shape[1]
    return pl.pallas_call(
        row_kernel,
        out_shape=jax.ShapeDtypeStruct((rows // 128, 128), jnp.float32),
        in_specs=[SCALARS] + [WHOLE] * 3,
        out_specs=WHOLE,
        scratch_shapes=[pltpu.VMEM((rows, 128), jnp.float32)] * 2,
        compiler_params=PARAMS,
        name="rows",
    )(flags, in_vmem(cross), in_vmem(masses), sums)


def call_columns(twice, flags, cross, weights):
    rows, columns = cross.shape[1:]
    return pl.pallas_call(
        functools.partial(column_kernel, twice),
        out_shape=jax.ShapeDtypeStruct((BUFFERS, columns // 128, 128), jnp.float32),
        in_specs=[SCALARS] + [WHOLE] * 2,
        out_specs=WHOLE,
        scratch_shapes=[pltpu.VMEM((rows, 128), jnp.float32)]
        + [pltpu.VMEM((BUFFERS, 8, columns), jnp.float32)] * 2,
        compiler_params=PARAMS,
        name="columns",
    )(flags, in_vmem(cross), weights)


def fill_rows(value, before, after):
    return jnp.pad(value, ((before, after), (0, 0), (0, 0)), constant_values=NEG_FILL)


def local(src_points, src_log_mass, tgt_points, tgt_log_mass, initial_potential, pair_list, pair_count):
    block = lax.axis_index("blk")
    rep = lax.axis_index("rep")
    blocks = lax.axis_size("blk")
    core = block % 2
    half_index = (rep % 2) ^ ((block // SEGMENT) % 2)
    rows = src_points.shape[0]
    width = tgt_points.shape[0]
    columns = width // 2

    def my_half(value):
        return lax.dynamic_slice_in_dim(value, half_index * columns, columns, 0)

    first_scale = 1.0 / EPS_START
    points = my_half(tgt_points)
    masses = my_half(tgt_log_mass)
    bias = masses + (my_half(initial_potential) - half_norms(points)) * first_scale
    tail = [part.reshape(-1, points.shape[1]) for part in terms(bias) + terms(masses)]
    tail.append(jnp.zeros((TAIL - 6 * columns // points.shape[1], points.shape[1]), jnp.bfloat16))
    message = jnp.concatenate([points * jnp.bfloat16(first_scale)] + tail, axis=0)

    before = send(message, along(2, blocks), blocks)
    after = send(message, along(-2, blocks), blocks)
    third = send(message, by_core(-3, 3, blocks), blocks)
    beside = send(message, sibling, blocks)
    mate = send(src_points, diagonal, blocks)
    sources = [src_points, mate]
    groups = ((0, 1), (2, 3, 4), (5, 6, 7))

    even_slots = (3, 4, 1, 5, 0, 2, 6, 7)
    odd_slots = (4, 3, 2, 6, 7, 1, 5, 0)
    slots = jnp.where(core == 0, jnp.array(even_slots, jnp.int32), jnp.array(odd_slots, jnp.int32))
    names = (block - core - 3 + slots) % blocks

    def kept(source_block):
        row_names = pair_list[source_block]
        in_use = jnp.arange(row_names.shape[0], dtype=jnp.int32) < pair_count[source_block]
        return jnp.any((row_names[None, :] == names[:, None]) & in_use[None, :], axis=1).astype(jnp.int32)

    flags = jnp.concatenate([kept(block), kept(block + 1 - 2 * core), slots])

    state = call_first(groups[0], True, False, flags, sources, [message, beside], ())
    state, arrived = lax.optimization_barrier((state, (before, after, third)))
    passed_on = [send(value, sibling, blocks) for value in arrived]
    state = call_first(groups[1], False, False, flags, sources, arrived, state)
    *state, last = call_first(groups[2], False, True, flags, sources, passed_on, state)
    cross, window_masses = state[:2]
    part = last.reshape(-1)

    for sweep in range(ITERS):
        epsilon = EPS_START * 0.5**sweep
        if sweep == 0:
            got = send(jnp.concatenate([part, src_log_mass]), diagonal, blocks)
            both_masses = jnp.concatenate([src_log_mass, got[2 * rows :]])
        else:
            part = call_rows(flags, cross, window_masses, column_sums).reshape(-1)
            got = send(part, diagonal, blocks)
        row_sums = log_merge(part, jnp.concatenate([got[rows : 2 * rows], got[:rows]]))
        weighted = (both_masses - row_sums).reshape(2 * rows // 128, 128)
        part = call_columns(sweep > 0, flags, cross, weighted)
        chip = log_merge(
            part,
            send(part, sibling, blocks),
            send(part, lambda b, r: (b, r ^ 2), blocks),
            send(part, lambda b, r: (b ^ 1, r ^ 2), blocks),
        )
        forward = core == 0
        if sweep + 1 < ITERS:
            got = []
            for n in (1, 2, 3):
                kept_rows = 8 - 2 * n
                out = jnp.where(forward, chip[2 * n :], chip[:kept_rows])
                out = send(out, by_core(2 * n, -2 * n, blocks), blocks)
                got.append(
                    jnp.where(forward, fill_rows(out, 0, 2 * n), fill_rows(out, 2 * n, 0))
                )
            side = log_merge(*got)
            column_sums = log_merge(chip, side, send(side, sibling, blocks))
        else:
            near = jnp.where(forward, chip[5:7], chip[1:3])
            near = send(near, by_core(2, -2, blocks), blocks)
            far = jnp.where(forward, chip[7], chip[0])
            far = send(far, by_core(4, -4, blocks), blocks)
            empty = jnp.full_like(far, NEG_FILL)
            far = jnp.where(forward, jnp.stack([far, empty]), jnp.stack([empty, far]))
            side = log_merge(near, far)
            column_sums = log_merge(chip[3:5], side, send(side, sibling, blocks))
            mine = jnp.where(core == 0, column_sums[0], column_sums[1]).reshape(columns)
            other = send(mine, lambda b, r: (b, r ^ 1), blocks)
            whole = jnp.where(
                half_index == 0, jnp.concatenate([mine, other]), jnp.concatenate([other, mine])
            )
            source_pot = half_norms(src_points) - epsilon * row_sums[:rows]
            target_pot = half_norms(tgt_points) - epsilon * whole
    return source_pot, target_pot


def solution(mesh):
    in_specs = (
        P(("blk", "rep"), None),
        P(("blk", "rep")),
        P("blk", None),
        P("blk"),
        P("blk"),
        P(),
        P(),
    )
    out_specs = (P(("blk", "rep")), P("blk"))
    return jax.shard_map(local, mesh=mesh, in_specs=in_specs, out_specs=out_specs, check_vma=False)
```

```python
import functools

import jax
import jax.numpy as jnp
from jax import lax
from jax.experimental import pallas as pl
from jax.experimental.pallas import tpu as pltpu
from jax.sharding import PartitionSpec as P

ITERS = 2
EPS_START = 0.5
NEG_FILL = -1e30
ROW_UNROLL = 8
COLUMN_UNROLL = 4
BUFFERS = 8
REPS = 4
SEGMENT = 8
TAIL = 16


def send(value, place, blocks):
    pairs = []
    for block in range(blocks):
        for rep in range(REPS):
            to_block, to_rep = place(block, rep)
            pairs.append((block * REPS + rep, to_block % blocks * REPS + to_rep))
    return lax.ppermute(value, ("blk", "rep"), pairs)


def along(steps, blocks):
    def place(block, rep):
        target = (block + steps) % blocks
        return target, rep if (target // SEGMENT - block // SEGMENT) % 2 == 0 else REPS - 1 - rep

    return place


def by_core(even_steps, odd_steps, blocks):
    even, odd = along(even_steps, blocks), along(odd_steps, blocks)
    return lambda block, rep: even(block, rep) if block % 2 == 0 else odd(block, rep)


def sibling(block, rep):
    return block ^ 1, rep


def diagonal(block, rep):
    return block ^ 1, rep ^ 1


def half_norms(points):
    widened = points.astype(jnp.float32)
    return 0.5 * jnp.sum(widened * widened, axis=1)


def terms(vector):
    parts = []
    for _ in range(3):
        parts.append(vector.astype(jnp.bfloat16).astype(jnp.float32))
        vector = vector - parts[-1]
    return parts


def log_merge(*parts):
    top = functools.reduce(jnp.maximum, parts)
    return top + jnp.log(sum(jnp.exp(part - top) for part in parts))


def spread_rows(vector_ref, bias_ref):
    for q in range(bias_ref.shape[0] // 128):
        row = vector_ref[q : q + 1, :]
        bias_ref[q * 128 : (q + 1) * 128, :] = jnp.broadcast_to(row, (128, 128)).T


def fold(value, combine):
    rows = value.shape[0]
    while rows > 8:
        rows //= 2
        value = combine(value[:rows], value[rows:])
    return value


def row_update(cross_ref, index, bias, twice, side, half, top_ref, total_ref):
    step = 64

    def chunk(r, _):
        at = pl.ds(pl.multiple_of(side * half + r * step, step), step)
        scores = []
        for q, term in enumerate(bias):
            part = cross_ref[index, at, q * 128 : (q + 1) * 128]
            scores.append((part + part if twice else part) + term)
        old = top_ref[at, :]
        top = jnp.maximum(old, functools.reduce(jnp.maximum, scores))
        total = functools.reduce(jnp.add, [jnp.exp(part - top) for part in scores])
        total_ref[at, :] = total_ref[at, :] * jnp.exp(old - top) + total
        top_ref[at, :] = top
        return 0

    lax.fori_loop(0, half // step, chunk, 0, unroll=ROW_UNROLL)


def row_finish(top_ref, total_ref, out):
    for q in range(out.shape[0]):
        top = top_ref[q * 128 : (q + 1) * 128, :].T
        greatest = jnp.max(top, axis=0, keepdims=True)
        total = total_ref[q * 128 : (q + 1) * 128, :].T * jnp.exp(top - greatest)
        out[q : q + 1, :] = greatest + jnp.log(jnp.sum(total, axis=0, keepdims=True))


def each_kept(flags, first, count, body):
    def unit(u, _):
        number, side = first + lax.div(u, 2), lax.rem(u, 2)

        @pl.when(flags[side * BUFFERS + number] != 0)
        def _():
            body(number, side)

        return 0

    lax.fori_loop(0, 2 * count, unit, 0)


def message_kernel(scale, half, points, masses, initial, src, out, src_out, block_ref, mass_ref, initial_ref, sems):
    columns, depth = block_ref.shape
    src_copy = pltpu.make_async_copy(src, src_out, sems.at[1])
    copy = pltpu.make_async_copy(
        points.at[pl.ds(pl.multiple_of(half[0] * columns, columns), columns), :], block_ref, sems.at[0]
    )
    small = [
        pltpu.make_async_copy(masses, mass_ref, sems.at[2]),
        pltpu.make_async_copy(initial, initial_ref, sems.at[3]),
    ]
    for start in (copy, *small, src_copy):
        start.start()
    copy.wait()
    value = block_ref[...].astype(jnp.float32)
    out[:columns, :] = (value * scale).astype(jnp.bfloat16)
    squares = value * value
    high = squares.astype(jnp.bfloat16)
    low = (squares - high.astype(jnp.float32)).astype(jnp.bfloat16)
    ones = jnp.ones((8, depth), jnp.bfloat16)
    norms = sum(
        lax.dot_general(ones, part, (((1,), (1,)), ((), ())), preferred_element_type=jnp.float32)
        for part in (high, low)
    )
    count = columns // 128
    norms = jnp.concatenate([norms[0:1, q * 128 : (q + 1) * 128] for q in range(count)], axis=0)

    def pick(ref):
        return jnp.where(half[0] == 0, ref[:count, :], ref[count:, :])

    for copy in small:
        copy.wait()
    mass = pick(mass_ref)
    bias = mass + (pick(initial_ref) - 0.5 * norms) * scale
    rows = [jnp.concatenate(pair, axis=1) for pair in zip(terms(bias), terms(mass))]
    rows.append(jnp.zeros((TAIL - 3 * count, 256), jnp.float32))
    out[columns:, :] = jnp.concatenate(rows, axis=0).astype(jnp.bfloat16)
    src_copy.wait()


def first_kernel(numbers, first, last, flags, *refs):
    sources, targets = refs[:2], refs[2 : 2 + len(numbers)]
    refs = refs[2 + len(numbers) :]
    if not first:
        refs = refs[4:]
    cross, masses, top_ref, total_ref = refs[:4]
    src_ref, tgt_ref, bias_ref = refs[-3:]
    if first:
        top_ref[...] = jnp.full(top_ref.shape, NEG_FILL, jnp.float32)
        total_ref[...] = jnp.zeros(total_ref.shape, jnp.float32)
    half = sources[0].shape[0]
    width = cross.shape[2]
    for side, src in enumerate(sources):
        src_ref[side] = src[...]
    for k, number in enumerate(numbers):
        tgt_ref[k] = targets[k][:width, :]
        tail = targets[k][width:, :].astype(jnp.float32)
        count = width // 128
        vectors = tail[:count] + tail[count : 2 * count] + tail[2 * count : 3 * count]
        bias_ref[k] = vectors[:, :128]
        masses[number] = vectors[:, 128:]

    def body(number, side):
        k = number - numbers[0]
        for c in range(0, width, 256):
            for r in range(0, half, 256):
                at = pl.ds(pl.multiple_of(side * half + r, 256), 256)
                cross[number, at, c : c + 256] = lax.dot_general(
                    src_ref[side, r : r + 256, :],
                    tgt_ref[k, c : c + 256, :],
                    (((1,), (1,)), ((), ())),
                    preferred_element_type=jnp.float32,
                )
        bias = [bias_ref[k, q : q + 1, :] for q in range(width // 128)]
        row_update(cross, number, bias, False, side, half, top_ref, total_ref)

    each_kept(flags, numbers[0], len(numbers), body)
    if last:
        row_finish(top_ref, total_ref, refs[4])


def row_kernel(flags, cross, masses, sums, out, top_ref, total_ref):
    top_ref[...] = jnp.full(top_ref.shape, NEG_FILL, jnp.float32)
    total_ref[...] = jnp.zeros(total_ref.shape, jnp.float32)
    half = top_ref.shape[0] // 2

    def body(number, side):
        slot = flags[2 * BUFFERS + number]
        bias = [
            masses[number, q : q + 1, :] - 2.0 * sums[slot, q : q + 1, :] for q in range(masses.shape[1])
        ]
        row_update(cross, number, bias, True, side, half, top_ref, total_ref)

    each_kept(flags, 0, BUFFERS, body)
    row_finish(top_ref, total_ref, out)


def column_kernel(twice, flags, cross, weights, out, bias, top_ref, total_ref):
    out[...] = jnp.full(out.shape, NEG_FILL, jnp.float32)
    top_ref[...] = jnp.full(top_ref.shape, NEG_FILL, jnp.float32)
    total_ref[...] = jnp.zeros(total_ref.shape, jnp.float32)
    spread_rows(weights, bias)
    half = bias.shape[0] // 2
    pieces = cross.shape[2] // 128
    step = 128

    def body(number, side):
        def chunk(r, state):
            at = pl.ds(pl.multiple_of(side * half + r * step, step), step)
            weight = bias[at, :]
            tops, totals = [], []
            for q in range(pieces):
                part = cross[number, at, q * 128 : (q + 1) * 128]
                scores = (part + part if twice else part) + weight
                top = jnp.maximum(state[0][q], fold(scores, jnp.maximum))
                total = jnp.sum(jnp.exp(scores.reshape(-1, 8, 128) - top[None]), axis=0)
                totals.append(state[1][q] * jnp.exp(state[0][q] - top) + total)
                tops.append(top)
            return tuple(tops), tuple(totals)

        state = (
            tuple(top_ref[number, :, q * 128 : (q + 1) * 128] for q in range(pieces)),
            tuple(total_ref[number, :, q * 128 : (q + 1) * 128] for q in range(pieces)),
        )
        tops, totals = lax.fori_loop(0, half // step, chunk, state, unroll=COLUMN_UNROLL)
        for q in range(pieces):
            top_ref[number, :, q * 128 : (q + 1) * 128] = tops[q]
            total_ref[number, :, q * 128 : (q + 1) * 128] = totals[q]

    each_kept(flags, 0, BUFFERS, body)

    def finish(number, _):
        @pl.when((flags[number] | flags[BUFFERS + number]) != 0)
        def _():
            for q in range(pieces):
                top = top_ref[number, :, q * 128 : (q + 1) * 128]
                greatest = jnp.max(top, axis=0, keepdims=True)
                total = total_ref[number, :, q * 128 : (q + 1) * 128] * jnp.exp(top - greatest)
                out[flags[2 * BUFFERS + number], q : q + 1, :] = greatest + jnp.log(
                    jnp.sum(total, axis=0, keepdims=True)
                )

        return 0

    lax.fori_loop(0, BUFFERS, finish, 0)


WHOLE = pl.BlockSpec(memory_space=pltpu.VMEM)
SCALARS = pl.BlockSpec(memory_space=pltpu.SMEM)
PARAMS = pltpu.CompilerParams(vmem_limit_bytes=20 * 2**20)


def in_vmem(value):
    return pltpu.with_memory_space_constraint(value, pltpu.VMEM)


def in_hbm(value):
    return pltpu.with_memory_space_constraint(value, pltpu.HBM)


def call_message(scale, half_index, points, masses, initial, src):
    columns, depth = points.shape[0] // 2, points.shape[1]
    return pl.pallas_call(
        functools.partial(message_kernel, scale),
        out_shape=[
            pltpu.VMEM((columns + TAIL, depth), jnp.bfloat16),
            pltpu.VMEM(src.shape, jnp.bfloat16),
        ],
        in_specs=[SCALARS] + [pl.BlockSpec(memory_space=pltpu.HBM)] * 4,
        out_specs=[WHOLE] * 2,
        scratch_shapes=[
            pltpu.VMEM((columns, depth), jnp.bfloat16),
            pltpu.VMEM((2 * columns // 128, 128), jnp.float32),
            pltpu.VMEM((2 * columns // 128, 128), jnp.float32),
            pltpu.SemaphoreType.DMA((4,)),
        ],
        compiler_params=PARAMS,
        name="message",
    )(half_index.reshape(1), *map(in_hbm, (points, masses.reshape(-1, 128), initial.reshape(-1, 128), src)))


def call_first(numbers, first, last, flags, sources, targets, state):
    half, depth = sources[0].shape
    rows, columns, count = 2 * half, targets[0].shape[0] - TAIL, len(numbers)
    out_shape = [
        pltpu.VMEM((BUFFERS, rows, columns), jnp.float32),
        pltpu.VMEM((BUFFERS, columns // 128, 128), jnp.float32),
        pltpu.VMEM((rows, 128), jnp.float32),
        pltpu.VMEM((rows, 128), jnp.float32),
    ]
    if last:
        out_shape.append(jax.ShapeDtypeStruct((rows // 128, 128), jnp.float32))
    operands = [flags, *sources, *targets]
    aliases = {}
    if not first:
        aliases = {len(operands) + i: i for i in range(4)}
        operands += [in_vmem(value) for value in state]
    return pl.pallas_call(
        functools.partial(first_kernel, numbers, first, last),
        out_shape=out_shape,
        in_specs=[SCALARS] + [WHOLE] * (len(operands) - 1),
        out_specs=[WHOLE] * len(out_shape),
        scratch_shapes=[
            pltpu.VMEM((2, half, depth), jnp.bfloat16),
            pltpu.VMEM((count, columns, depth), jnp.bfloat16),
            pltpu.VMEM((count, columns // 128, 128), jnp.float32),
        ],
        input_output_aliases=aliases,
        compiler_params=PARAMS,
        cost_estimate=pl.CostEstimate(
            flops=2 * count * rows * columns * depth,
            bytes_accessed=count * rows * columns,
            transcendentals=count * rows * columns,
        ),
        name="first_rows",
    )(*operands)


def call_rows(flags, cross, masses, sums):
    rows = cross.shape[1]
    return pl.pallas_call(
        row_kernel,
        out_shape=jax.ShapeDtypeStruct((rows // 128, 128), jnp.float32),
        in_specs=[SCALARS] + [WHOLE] * 3,
        out_specs=WHOLE,
        scratch_shapes=[pltpu.VMEM((rows, 128), jnp.float32)] * 2,
        compiler_params=PARAMS,
        name="rows",
    )(flags, in_vmem(cross), in_vmem(masses), sums)


def call_columns(twice, flags, cross, weights):
    rows, columns = cross.shape[1:]
    return pl.pallas_call(
        functools.partial(column_kernel, twice),
        out_shape=jax.ShapeDtypeStruct((BUFFERS, columns // 128, 128), jnp.float32),
        in_specs=[SCALARS] + [WHOLE] * 2,
        out_specs=WHOLE,
        scratch_shapes=[pltpu.VMEM((rows, 128), jnp.float32)]
        + [pltpu.VMEM((BUFFERS, 8, columns), jnp.float32)] * 2,
        compiler_params=PARAMS,
        name="columns",
    )(flags, in_vmem(cross), weights)


def fill_rows(value, before, after):
    return jnp.pad(value, ((before, after), (0, 0), (0, 0)), constant_values=NEG_FILL)


def local(src_points, src_log_mass, tgt_points, tgt_log_mass, initial_potential, pair_list, pair_count):
    block = lax.axis_index("blk")
    rep = lax.axis_index("rep")
    blocks = lax.axis_size("blk")
    core = block % 2
    half_index = (rep % 2) ^ ((block // SEGMENT) % 2)
    rows = src_points.shape[0]
    width = tgt_points.shape[0]
    columns = width // 2

    mate = send(src_points, diagonal, blocks)
    message, own = call_message(
        1.0 / EPS_START, half_index, tgt_points, tgt_log_mass, initial_potential, src_points
    )

    before = send(message, along(2, blocks), blocks)
    after = send(message, along(-2, blocks), blocks)
    tied, mate = lax.optimization_barrier((message, mate))
    third = send(tied, by_core(-3, 3, blocks), blocks)
    beside = send(message, sibling, blocks)
    sources = [own, mate]
    groups = ((0, 1), (2, 3, 4), (5, 6, 7))

    even_slots = (3, 4, 1, 5, 0, 2, 6, 7)
    odd_slots = (4, 3, 2, 6, 7, 1, 5, 0)
    slots = jnp.where(core == 0, jnp.array(even_slots, jnp.int32), jnp.array(odd_slots, jnp.int32))
    names = (block - core - 3 + slots) % blocks

    def kept(source_block):
        row_names = pair_list[source_block]
        in_use = jnp.arange(row_names.shape[0], dtype=jnp.int32) < pair_count[source_block]
        return jnp.any((row_names[None, :] == names[:, None]) & in_use[None, :], axis=1).astype(jnp.int32)

    flags = jnp.concatenate([kept(block), kept(block + 1 - 2 * core), slots])

    state = call_first(groups[0], True, False, flags, sources, [message, beside], ())
    state, arrived = lax.optimization_barrier((state, (before, after, third)))
    passed_on = [send(value, sibling, blocks) for value in arrived]
    state = call_first(groups[1], False, False, flags, sources, arrived, state)
    *state, last = call_first(groups[2], False, True, flags, sources, passed_on, state)
    cross, window_masses = state[:2]
    part = last.reshape(-1)

    for sweep in range(ITERS):
        epsilon = EPS_START * 0.5**sweep
        if sweep == 0:
            got = send(jnp.concatenate([part, src_log_mass]), diagonal, blocks)
            both_masses = jnp.concatenate([src_log_mass, got[2 * rows :]])
        else:
            part = call_rows(flags, cross, window_masses, column_sums).reshape(-1)
            got = send(part, diagonal, blocks)
        row_sums = log_merge(part, jnp.concatenate([got[rows : 2 * rows], got[:rows]]))
        weighted = (both_masses - row_sums).reshape(2 * rows // 128, 128)
        part = call_columns(sweep > 0, flags, cross, weighted)
        chip = log_merge(
            part,
            send(part, sibling, blocks),
            send(part, lambda b, r: (b, r ^ 2), blocks),
            send(part, lambda b, r: (b ^ 1, r ^ 2), blocks),
        )
        forward = core == 0
        if sweep + 1 < ITERS:
            got = []
            for n in (1, 2, 3):
                kept_rows = 8 - 2 * n
                out = jnp.where(forward, chip[2 * n :], chip[:kept_rows])
                out = send(out, by_core(2 * n, -2 * n, blocks), blocks)
                got.append(
                    jnp.where(forward, fill_rows(out, 0, 2 * n), fill_rows(out, 2 * n, 0))
                )
            side = log_merge(*got)
            column_sums = log_merge(chip, side, send(side, sibling, blocks))
        else:
            near = jnp.where(forward, chip[5:7], chip[1:3])
            near = send(near, by_core(2, -2, blocks), blocks)
            far = jnp.where(forward, chip[7], chip[0])
            far = send(far, by_core(4, -4, blocks), blocks)
            empty = jnp.full_like(far, NEG_FILL)
            far = jnp.where(forward, jnp.stack([far, empty]), jnp.stack([empty, far]))
            side = log_merge(near, far)
            column_sums = log_merge(chip[3:5], side, send(side, sibling, blocks))
            mine = jnp.where(core == 0, column_sums[0], column_sums[1]).reshape(columns)
            other = send(mine, lambda b, r: (b, r ^ 1), blocks)
            whole = jnp.where(
                half_index == 0, jnp.concatenate([mine, other]), jnp.concatenate([other, mine])
            )
            source_pot = half_norms(src_points) - epsilon * row_sums[:rows]
            target_pot = half_norms(tgt_points) - epsilon * whole
    return source_pot, target_pot


def solution(mesh):
    in_specs = (
        P(("blk", "rep"), None),
        P(("blk", "rep")),
        P("blk", None),
        P("blk"),
        P("blk"),
        P(),
        P(),
    )
    out_specs = (P(("blk", "rep")), P("blk"))
    return jax.shard_map(local, mesh=mesh, in_specs=in_specs, out_specs=out_specs, check_vma=False)
```

```python
import functools

import jax
import jax.numpy as jnp
from jax import lax
from jax.experimental import pallas as pl
from jax.experimental.pallas import tpu as pltpu
from jax.sharding import PartitionSpec as P

ITERS = 2
EPS_START = 0.5
NEG_FILL = -1e30
ROW_UNROLL = 8
COLUMN_UNROLL = 4
BUFFERS = 8
REPS = 4
SEGMENT = 8
TAIL = 16


def send(value, place, blocks):
    pairs = []
    for block in range(blocks):
        for rep in range(REPS):
            to_block, to_rep = place(block, rep)
            pairs.append((block * REPS + rep, to_block % blocks * REPS + to_rep))
    return lax.ppermute(value, ("blk", "rep"), pairs)


def along(steps, blocks):
    def place(block, rep):
        target = (block + steps) % blocks
        return target, rep if (target // SEGMENT - block // SEGMENT) % 2 == 0 else REPS - 1 - rep

    return place


def by_core(even_steps, odd_steps, blocks):
    even, odd = along(even_steps, blocks), along(odd_steps, blocks)
    return lambda block, rep: even(block, rep) if block % 2 == 0 else odd(block, rep)


def sibling(block, rep):
    return block ^ 1, rep


def diagonal(block, rep):
    return block ^ 1, rep ^ 1


def half_norms(points):
    widened = points.astype(jnp.float32)
    return 0.5 * jnp.sum(widened * widened, axis=1)


def terms(vector):
    parts = []
    for _ in range(3):
        parts.append(vector.astype(jnp.bfloat16).astype(jnp.float32))
        vector = vector - parts[-1]
    return parts


def log_merge(*parts):
    top = functools.reduce(jnp.maximum, parts)
    return top + jnp.log(sum(jnp.exp(part - top) for part in parts))


def spread_rows(vector_ref, bias_ref):
    for q in range(bias_ref.shape[0] // 128):
        row = vector_ref[q : q + 1, :]
        bias_ref[q * 128 : (q + 1) * 128, :] = jnp.broadcast_to(row, (128, 128)).T


def fold(value, combine):
    rows = value.shape[0]
    while rows > 8:
        rows //= 2
        value = combine(value[:rows], value[rows:])
    return value


def row_update(cross_ref, index, bias, twice, side, half, top_ref, total_ref):
    step = 64

    def chunk(r, _):
        at = pl.ds(pl.multiple_of(side * half + r * step, step), step)
        scores = []
        for q, term in enumerate(bias):
            part = cross_ref[index, at, q * 128 : (q + 1) * 128]
            scores.append((part + part if twice else part) + term)
        old = top_ref[at, :]
        top = jnp.maximum(old, functools.reduce(jnp.maximum, scores))
        total = functools.reduce(jnp.add, [jnp.exp(part - top) for part in scores])
        total_ref[at, :] = total_ref[at, :] * jnp.exp(old - top) + total
        top_ref[at, :] = top
        return 0

    lax.fori_loop(0, half // step, chunk, 0, unroll=ROW_UNROLL)


def row_finish(top_ref, total_ref, out):
    for q in range(out.shape[0]):
        top = top_ref[q * 128 : (q + 1) * 128, :].T
        greatest = jnp.max(top, axis=0, keepdims=True)
        total = total_ref[q * 128 : (q + 1) * 128, :].T * jnp.exp(top - greatest)
        out[q : q + 1, :] = greatest + jnp.log(jnp.sum(total, axis=0, keepdims=True))


def each_listed(flags, body):
    def unit(u, _):
        entry = flags[4 * BUFFERS + u]
        body(lax.div(entry, 2), lax.rem(entry, 2))
        return 0

    lax.fori_loop(0, flags[3 * BUFFERS], unit, 0)


def each_kept(flags, first, count, body):
    def unit(u, _):
        number, side = first + lax.div(u, 2), lax.rem(u, 2)

        @pl.when(flags[side * BUFFERS + number] != 0)
        def _():
            body(number, side)

        return 0

    lax.fori_loop(0, 2 * count, unit, 0)


def message_kernel(scale, half, points, masses, initial, src, out, src_out, block_ref, mass_ref, initial_ref, sems):
    columns, depth = block_ref.shape
    src_copy = pltpu.make_async_copy(src, src_out, sems.at[1])
    copy = pltpu.make_async_copy(
        points.at[pl.ds(pl.multiple_of(half[0] * columns, columns), columns), :], block_ref, sems.at[0]
    )
    small = [
        pltpu.make_async_copy(masses, mass_ref, sems.at[2]),
        pltpu.make_async_copy(initial, initial_ref, sems.at[3]),
    ]
    for start in (copy, *small, src_copy):
        start.start()
    copy.wait()
    value = block_ref[...].astype(jnp.float32)
    out[:columns, :] = (value * scale).astype(jnp.bfloat16)
    squares = value * value
    high = squares.astype(jnp.bfloat16)
    low = (squares - high.astype(jnp.float32)).astype(jnp.bfloat16)
    ones = jnp.ones((8, depth), jnp.bfloat16)
    norms = sum(
        lax.dot_general(ones, part, (((1,), (1,)), ((), ())), preferred_element_type=jnp.float32)
        for part in (high, low)
    )
    count = columns // 128
    norms = jnp.concatenate([norms[0:1, q * 128 : (q + 1) * 128] for q in range(count)], axis=0)

    def pick(ref):
        return jnp.where(half[0] == 0, ref[:count, :], ref[count:, :])

    for copy in small:
        copy.wait()
    mass = pick(mass_ref)
    bias = mass + (pick(initial_ref) - 0.5 * norms) * scale
    rows = [jnp.concatenate(pair, axis=1) for pair in zip(terms(bias), terms(mass))]
    rows.append(jnp.zeros((TAIL - 3 * count, 256), jnp.float32))
    out[columns:, :] = jnp.concatenate(rows, axis=0).astype(jnp.bfloat16)
    src_copy.wait()


def first_kernel(numbers, first, last, flags, *refs):
    sources, targets = refs[:2], refs[2 : 2 + len(numbers)]
    refs = refs[2 + len(numbers) :]
    if not first:
        refs = refs[4:]
    cross, masses, top_ref, total_ref = refs[:4]
    src_ref, tgt_ref, bias_ref = refs[-3:]
    if first:
        top_ref[...] = jnp.full(top_ref.shape, NEG_FILL, jnp.float32)
        total_ref[...] = jnp.zeros(total_ref.shape, jnp.float32)
    half = sources[0].shape[0]
    width = cross.shape[2]
    for side, src in enumerate(sources):
        src_ref[side] = src[...]
    for k, number in enumerate(numbers):
        tgt_ref[k] = targets[k][:width, :]
        tail = targets[k][width:, :].astype(jnp.float32)
        count = width // 128
        vectors = tail[:count] + tail[count : 2 * count] + tail[2 * count : 3 * count]
        bias_ref[k] = vectors[:, :128]
        masses[number] = vectors[:, 128:]

    def body(number, side):
        k = number - numbers[0]
        for c in range(0, width, 256):
            for r in range(0, half, 256):
                at = pl.ds(pl.multiple_of(side * half + r, 256), 256)
                cross[number, at, c : c + 256] = lax.dot_general(
                    src_ref[side, r : r + 256, :],
                    tgt_ref[k, c : c + 256, :],
                    (((1,), (1,)), ((), ())),
                    preferred_element_type=jnp.float32,
                )
        bias = [bias_ref[k, q : q + 1, :] for q in range(width // 128)]
        row_update(cross, number, bias, False, side, half, top_ref, total_ref)

    each_kept(flags, numbers[0], len(numbers), body)
    if last:
        row_finish(top_ref, total_ref, refs[4])


def row_kernel(flags, cross, masses, sums, out, top_ref, total_ref):
    top_ref[...] = jnp.full(top_ref.shape, NEG_FILL, jnp.float32)
    total_ref[...] = jnp.zeros(total_ref.shape, jnp.float32)
    half = top_ref.shape[0] // 2

    def body(number, side):
        slot = flags[2 * BUFFERS + number]
        bias = [
            masses[number, q : q + 1, :] - 2.0 * sums[slot, q : q + 1, :] for q in range(masses.shape[1])
        ]
        row_update(cross, number, bias, True, side, half, top_ref, total_ref)

    each_listed(flags, body)
    row_finish(top_ref, total_ref, out)


def column_kernel(twice, flags, cross, weights, out, bias, top_ref, total_ref):
    out[...] = jnp.full(out.shape, NEG_FILL, jnp.float32)
    spread_rows(weights, bias)
    half = bias.shape[0] // 2
    pieces = cross.shape[2] // 128
    step = 128

    def body(number, side):
        def chunk(r, state):
            at = pl.ds(pl.multiple_of(side * half + r * step, step), step)
            weight = bias[at, :]
            tops, totals = [], []
            for q in range(pieces):
                part = cross[number, at, q * 128 : (q + 1) * 128]
                scores = (part + part if twice else part) + weight
                top = jnp.maximum(state[0][q], fold(scores, jnp.maximum))
                total = jnp.sum(jnp.exp(scores.reshape(-1, 8, 128) - top[None]), axis=0)
                totals.append(state[1][q] * jnp.exp(state[0][q] - top) + total)
                tops.append(top)
            return tuple(tops), tuple(totals)

        going = (side == 1) & (flags[number] != 0)
        cuts = [slice(q * 128, (q + 1) * 128) for q in range(pieces)]
        state = (
            tuple(jnp.where(going, top_ref[:, cut], NEG_FILL) for cut in cuts),
            tuple(jnp.where(going, total_ref[:, cut], 0.0) for cut in cuts),
        )
        tops, totals = lax.fori_loop(0, half // step, chunk, state, unroll=COLUMN_UNROLL)
        more = (side == 0) & (flags[BUFFERS + number] != 0)

        @pl.when(more)
        def _():
            for cut, top, total in zip(cuts, tops, totals):
                top_ref[:, cut] = top
                total_ref[:, cut] = total

        @pl.when(jnp.logical_not(more))
        def _():
            slot = flags[2 * BUFFERS + number]
            for q, (top, total) in enumerate(zip(tops, totals)):
                greatest = jnp.max(top, axis=0, keepdims=True)
                total = jnp.sum(total * jnp.exp(top - greatest), axis=0, keepdims=True)
                out[slot, q : q + 1, :] = greatest + jnp.log(total)

    each_listed(flags, body)


WHOLE = pl.BlockSpec(memory_space=pltpu.VMEM)
SCALARS = pl.BlockSpec(memory_space=pltpu.SMEM)
PARAMS = pltpu.CompilerParams(vmem_limit_bytes=20 * 2**20)


def in_vmem(value):
    return pltpu.with_memory_space_constraint(value, pltpu.VMEM)


def in_hbm(value):
    return pltpu.with_memory_space_constraint(value, pltpu.HBM)


def call_message(scale, half_index, points, masses, initial, src):
    columns, depth = points.shape[0] // 2, points.shape[1]
    return pl.pallas_call(
        functools.partial(message_kernel, scale),
        out_shape=[
            pltpu.VMEM((columns + TAIL, depth), jnp.bfloat16),
            pltpu.VMEM(src.shape, jnp.bfloat16),
        ],
        in_specs=[SCALARS] + [pl.BlockSpec(memory_space=pltpu.HBM)] * 4,
        out_specs=[WHOLE] * 2,
        scratch_shapes=[
            pltpu.VMEM((columns, depth), jnp.bfloat16),
            pltpu.VMEM((2 * columns // 128, 128), jnp.float32),
            pltpu.VMEM((2 * columns // 128, 128), jnp.float32),
            pltpu.SemaphoreType.DMA((4,)),
        ],
        compiler_params=PARAMS,
        name="message",
    )(half_index.reshape(1), *map(in_hbm, (points, masses.reshape(-1, 128), initial.reshape(-1, 128), src)))


def call_first(numbers, first, last, flags, sources, targets, state):
    half, depth = sources[0].shape
    rows, columns, count = 2 * half, targets[0].shape[0] - TAIL, len(numbers)
    out_shape = [
        pltpu.VMEM((BUFFERS, rows, columns), jnp.float32),
        pltpu.VMEM((BUFFERS, columns // 128, 128), jnp.float32),
        pltpu.VMEM((rows, 128), jnp.float32),
        pltpu.VMEM((rows, 128), jnp.float32),
    ]
    if last:
        out_shape.append(jax.ShapeDtypeStruct((rows // 128, 128), jnp.float32))
    operands = [flags, *sources, *targets]
    aliases = {}
    if not first:
        aliases = {len(operands) + i: i for i in range(4)}
        operands += [in_vmem(value) for value in state]
    return pl.pallas_call(
        functools.partial(first_kernel, numbers, first, last),
        out_shape=out_shape,
        in_specs=[SCALARS] + [WHOLE] * (len(operands) - 1),
        out_specs=[WHOLE] * len(out_shape),
        scratch_shapes=[
            pltpu.VMEM((2, half, depth), jnp.bfloat16),
            pltpu.VMEM((count, columns, depth), jnp.bfloat16),
            pltpu.VMEM((count, columns // 128, 128), jnp.float32),
        ],
        input_output_aliases=aliases,
        compiler_params=PARAMS,
        cost_estimate=pl.CostEstimate(
            flops=2 * count * rows * columns * depth,
            bytes_accessed=count * rows * columns,
            transcendentals=count * rows * columns,
        ),
        name="first_rows",
    )(*operands)


def call_rows(flags, cross, masses, sums):
    rows = cross.shape[1]
    return pl.pallas_call(
        row_kernel,
        out_shape=jax.ShapeDtypeStruct((rows // 128, 128), jnp.float32),
        in_specs=[SCALARS] + [WHOLE] * 3,
        out_specs=WHOLE,
        scratch_shapes=[pltpu.VMEM((rows, 128), jnp.float32)] * 2,
        compiler_params=PARAMS,
        name="rows",
    )(flags, in_vmem(cross), in_vmem(masses), sums)


def call_columns(twice, flags, cross, weights):
    rows, columns = cross.shape[1:]
    return pl.pallas_call(
        functools.partial(column_kernel, twice),
        out_shape=jax.ShapeDtypeStruct((BUFFERS, columns // 128, 128), jnp.float32),
        in_specs=[SCALARS] + [WHOLE] * 2,
        out_specs=WHOLE,
        scratch_shapes=[pltpu.VMEM((rows, 128), jnp.float32)]
        + [pltpu.VMEM((8, columns), jnp.float32)] * 2,
        compiler_params=PARAMS,
        name="columns",
    )(flags, in_vmem(cross), weights)


def fill_rows(value, before, after):
    return jnp.pad(value, ((before, after), (0, 0), (0, 0)), constant_values=NEG_FILL)


def local(src_points, src_log_mass, tgt_points, tgt_log_mass, initial_potential, pair_list, pair_count):
    block = lax.axis_index("blk")
    rep = lax.axis_index("rep")
    blocks = lax.axis_size("blk")
    core = block % 2
    half_index = (rep % 2) ^ ((block // SEGMENT) % 2)
    rows = src_points.shape[0]
    width = tgt_points.shape[0]
    columns = width // 2

    mate = send(src_points, diagonal, blocks)
    message, own = call_message(
        1.0 / EPS_START, half_index, tgt_points, tgt_log_mass, initial_potential, src_points
    )

    before = send(message, along(2, blocks), blocks)
    after = send(message, along(-2, blocks), blocks)
    third = send(message, by_core(-3, 3, blocks), blocks)
    tied, mate = lax.optimization_barrier((message, mate))
    beside = send(tied, sibling, blocks)
    sources = [own, mate]
    groups = ((0, 1), (2, 3, 4), (5, 6, 7))

    even_slots = (3, 4, 1, 5, 0, 2, 6, 7)
    odd_slots = (4, 3, 2, 6, 7, 1, 5, 0)
    slots = jnp.where(core == 0, jnp.array(even_slots, jnp.int32), jnp.array(odd_slots, jnp.int32))
    names = (block - core - 3 + slots) % blocks

    def kept(source_block):
        row_names = pair_list[source_block]
        in_use = jnp.arange(row_names.shape[0], dtype=jnp.int32) < pair_count[source_block]
        return jnp.any((row_names[None, :] == names[:, None]) & in_use[None, :], axis=1).astype(jnp.int32)

    kept_pairs = jnp.stack([kept(block), kept(block + 1 - 2 * core)])
    entries = jnp.arange(2 * BUFFERS, dtype=jnp.int32)
    listed = kept_pairs.T.reshape(-1)
    rank = jnp.sum(jnp.where(entries[None, :] < entries[:, None], listed[None, :], 0), axis=1)
    order = jnp.sum(
        jnp.where((rank[:, None] == entries[None, :]) & (listed[:, None] != 0), entries[:, None], 0), axis=0
    )
    total = jnp.broadcast_to(jnp.sum(listed), (BUFFERS,))
    flags = jnp.concatenate([kept_pairs.reshape(-1), slots, total, order])

    state = call_first(groups[0], True, False, flags, sources, [message, beside], ())
    state, arrived = lax.optimization_barrier((state, (before, after, third)))
    passed_on = [send(value, sibling, blocks) for value in arrived]
    state = call_first(groups[1], False, False, flags, sources, arrived, state)
    *state, last = call_first(groups[2], False, True, flags, sources, passed_on, state)
    cross, window_masses = state[:2]
    part = last.reshape(-1)

    for sweep in range(ITERS):
        epsilon = EPS_START * 0.5**sweep
        if sweep == 0:
            got = send(jnp.concatenate([part, src_log_mass]), diagonal, blocks)
            both_masses = jnp.concatenate([src_log_mass, got[2 * rows :]])
        else:
            part = call_rows(flags, cross, window_masses, column_sums).reshape(-1)
            got = send(part, diagonal, blocks)
        row_sums = log_merge(part, jnp.concatenate([got[rows : 2 * rows], got[:rows]]))
        weighted = (both_masses - row_sums).reshape(2 * rows // 128, 128)
        part = call_columns(sweep > 0, flags, cross, weighted)
        chip = log_merge(
            part,
            send(part, sibling, blocks),
            send(part, lambda b, r: (b, r ^ 2), blocks),
            send(part, lambda b, r: (b ^ 1, r ^ 2), blocks),
        )
        forward = core == 0
        if sweep + 1 < ITERS:
            got = []
            for n in (1, 2, 3):
                kept_rows = 8 - 2 * n
                out = jnp.where(forward, chip[2 * n :], chip[:kept_rows])
                out = send(out, by_core(2 * n, -2 * n, blocks), blocks)
                got.append(
                    jnp.where(forward, fill_rows(out, 0, 2 * n), fill_rows(out, 2 * n, 0))
                )
            side = log_merge(*got)
            column_sums = log_merge(chip, side, send(side, sibling, blocks))
        else:
            near = jnp.where(forward, chip[5:7], chip[1:3])
            near = send(near, by_core(2, -2, blocks), blocks)
            far = jnp.where(forward, chip[7], chip[0])
            far = send(far, by_core(4, -4, blocks), blocks)
            empty = jnp.full_like(far, NEG_FILL)
            far = jnp.where(forward, jnp.stack([far, empty]), jnp.stack([empty, far]))
            side = log_merge(near, far)
            column_sums = log_merge(chip[3:5], side, send(side, sibling, blocks))
            mine = jnp.where(core == 0, column_sums[0], column_sums[1]).reshape(columns)
            other = send(mine, lambda b, r: (b, r ^ 1), blocks)
            whole = jnp.where(
                half_index == 0, jnp.concatenate([mine, other]), jnp.concatenate([other, mine])
            )
            source_pot = half_norms(src_points) - epsilon * row_sums[:rows]
            target_pot = half_norms(tgt_points) - epsilon * whole
    return source_pot, target_pot


def solution(mesh):
    in_specs = (
        P(("blk", "rep"), None),
        P(("blk", "rep")),
        P("blk", None),
        P("blk"),
        P("blk"),
        P(),
        P(),
    )
    out_specs = (P(("blk", "rep")), P("blk"))
    return jax.shard_map(local, mesh=mesh, in_specs=in_specs, out_specs=out_specs, check_vma=False)
```

```python
import functools

import jax
import jax.numpy as jnp
from jax import lax
from jax.experimental import pallas as pl
from jax.experimental.pallas import tpu as pltpu
from jax.sharding import PartitionSpec as P

ITERS = 2
EPS_START = 0.5
NEG_FILL = -1e30
ROW_UNROLL = 8
COLUMN_UNROLL = 4
BUFFERS = 8
REPS = 4
SEGMENT = 8
TAIL = 16


def send(value, place, blocks):
    pairs = []
    for block in range(blocks):
        for rep in range(REPS):
            to_block, to_rep = place(block, rep)
            pairs.append((block * REPS + rep, to_block % blocks * REPS + to_rep))
    return lax.ppermute(value, ("blk", "rep"), pairs)


def along(steps, blocks):
    def place(block, rep):
        target = (block + steps) % blocks
        return target, rep if (target // SEGMENT - block // SEGMENT) % 2 == 0 else REPS - 1 - rep

    return place


def by_core(even_steps, odd_steps, blocks):
    even, odd = along(even_steps, blocks), along(odd_steps, blocks)
    return lambda block, rep: even(block, rep) if block % 2 == 0 else odd(block, rep)


def sibling(block, rep):
    return block ^ 1, rep


def diagonal(block, rep):
    return block ^ 1, rep ^ 1


def half_norms(points):
    widened = points.astype(jnp.float32)
    return 0.5 * jnp.sum(widened * widened, axis=1)


def terms(vector):
    parts = []
    for _ in range(3):
        parts.append(vector.astype(jnp.bfloat16).astype(jnp.float32))
        vector = vector - parts[-1]
    return parts


def log_merge(*parts):
    top = functools.reduce(jnp.maximum, parts)
    return top + jnp.log(sum(jnp.exp(part - top) for part in parts))


def spread_rows(vector_ref, bias_ref):
    for q in range(bias_ref.shape[0] // 128):
        row = vector_ref[q : q + 1, :]
        bias_ref[q * 128 : (q + 1) * 128, :] = jnp.broadcast_to(row, (128, 128)).T


def fold(value, combine):
    rows = value.shape[0]
    while rows > 8:
        rows //= 2
        value = combine(value[:rows], value[rows:])
    return value


def row_update(cross_ref, index, bias, twice, side, half, top_ref, total_ref):
    step = 64

    def chunk(r, _):
        at = pl.ds(pl.multiple_of(side * half + r * step, step), step)
        scores = []
        for q, term in enumerate(bias):
            part = cross_ref[index, at, q * 128 : (q + 1) * 128]
            scores.append((part + part if twice else part) + term)
        old = top_ref[at, :]
        top = jnp.maximum(old, functools.reduce(jnp.maximum, scores))
        total = functools.reduce(jnp.add, [jnp.exp(part - top) for part in scores])
        total_ref[at, :] = total_ref[at, :] * jnp.exp(old - top) + total
        top_ref[at, :] = top
        return 0

    lax.fori_loop(0, half // step, chunk, 0, unroll=ROW_UNROLL)


def row_finish(top_ref, total_ref, out):
    for q in range(out.shape[0]):
        top = top_ref[q * 128 : (q + 1) * 128, :].T
        greatest = jnp.max(top, axis=0, keepdims=True)
        total = total_ref[q * 128 : (q + 1) * 128, :].T * jnp.exp(top - greatest)
        out[q : q + 1, :] = greatest + jnp.log(jnp.sum(total, axis=0, keepdims=True))


def each_listed(flags, body):
    def unit(u, _):
        entry = flags[4 * BUFFERS + u]
        body(lax.div(entry, 2), lax.rem(entry, 2))
        return 0

    lax.fori_loop(0, flags[3 * BUFFERS], unit, 0)


def each_kept(flags, first, count, body):
    def unit(u, _):
        number, side = first + lax.div(u, 2), lax.rem(u, 2)

        @pl.when(flags[side * BUFFERS + number] != 0)
        def _():
            body(number, side)

        return 0

    lax.fori_loop(0, 2 * count, unit, 0)


def message_kernel(scale, half, points, masses, initial, src, out, src_out, block_ref, mass_ref, initial_ref, sems):
    columns, depth = block_ref.shape
    src_copy = pltpu.make_async_copy(src, src_out, sems.at[1])
    copy = pltpu.make_async_copy(
        points.at[pl.ds(pl.multiple_of(half[0] * columns, columns), columns), :], block_ref, sems.at[0]
    )
    small = [
        pltpu.make_async_copy(masses, mass_ref, sems.at[2]),
        pltpu.make_async_copy(initial, initial_ref, sems.at[3]),
    ]
    for start in (copy, *small, src_copy):
        start.start()
    copy.wait()
    value = block_ref[...].astype(jnp.float32)
    out[:columns, :] = (value * scale).astype(jnp.bfloat16)
    squares = value * value
    high = squares.astype(jnp.bfloat16)
    low = (squares - high.astype(jnp.float32)).astype(jnp.bfloat16)
    ones = jnp.ones((8, depth), jnp.bfloat16)
    norms = sum(
        lax.dot_general(ones, part, (((1,), (1,)), ((), ())), preferred_element_type=jnp.float32)
        for part in (high, low)
    )
    count = columns // 128
    norms = jnp.concatenate([norms[0:1, q * 128 : (q + 1) * 128] for q in range(count)], axis=0)

    def pick(ref):
        return jnp.where(half[0] == 0, ref[:count, :], ref[count:, :])

    for copy in small:
        copy.wait()
    mass = pick(mass_ref)
    bias = mass + (pick(initial_ref) - 0.5 * norms) * scale
    rows = [jnp.concatenate(pair, axis=1) for pair in zip(terms(bias), terms(mass))]
    rows.append(jnp.zeros((TAIL - 3 * count, 256), jnp.float32))
    out[columns:, :] = jnp.concatenate(rows, axis=0).astype(jnp.bfloat16)
    src_copy.wait()


def first_kernel(numbers, first, last, flags, *refs):
    sources, targets = refs[:2], refs[2 : 2 + len(numbers)]
    refs = refs[2 + len(numbers) :]
    if not first:
        refs = refs[4:]
    cross, masses, top_ref, total_ref = refs[:4]
    src_ref, tgt_ref, bias_ref = refs[-3:]
    if first:
        top_ref[...] = jnp.full(top_ref.shape, NEG_FILL, jnp.float32)
        total_ref[...] = jnp.zeros(total_ref.shape, jnp.float32)
    half = sources[0].shape[0]
    width = cross.shape[2]
    for side, src in enumerate(sources):
        src_ref[side] = src[...]
    for k, number in enumerate(numbers):
        tgt_ref[k] = targets[k][:width, :]
        tail = targets[k][width:, :].astype(jnp.float32)
        count = width // 128
        vectors = tail[:count] + tail[count : 2 * count] + tail[2 * count : 3 * count]
        bias_ref[k] = vectors[:, :128]
        masses[number] = vectors[:, 128:]

    def body(number, side):
        k = number - numbers[0]
        for c in range(0, width, 256):
            for r in range(0, half, 256):
                at = pl.ds(pl.multiple_of(side * half + r, 256), 256)
                cross[number, at, c : c + 256] = lax.dot_general(
                    src_ref[side, r : r + 256, :],
                    tgt_ref[k, c : c + 256, :],
                    (((1,), (1,)), ((), ())),
                    preferred_element_type=jnp.float32,
                )
        bias = [bias_ref[k, q : q + 1, :] for q in range(width // 128)]
        row_update(cross, number, bias, False, side, half, top_ref, total_ref)

    each_kept(flags, numbers[0], len(numbers), body)
    if last:
        row_finish(top_ref, total_ref, refs[4])


def row_kernel(flags, cross, masses, sums, out, top_ref, total_ref):
    top_ref[...] = jnp.full(top_ref.shape, NEG_FILL, jnp.float32)
    total_ref[...] = jnp.zeros(total_ref.shape, jnp.float32)
    half = top_ref.shape[0] // 2

    def body(number, side):
        slot = flags[2 * BUFFERS + number]
        bias = [
            masses[number, q : q + 1, :] - 2.0 * sums[slot, q : q + 1, :] for q in range(masses.shape[1])
        ]
        row_update(cross, number, bias, True, side, half, top_ref, total_ref)

    each_listed(flags, body)
    row_finish(top_ref, total_ref, out)


def column_kernel(twice, flags, cross, weights, out, bias, top_ref, total_ref):
    out[...] = jnp.full(out.shape, NEG_FILL, jnp.float32)
    spread_rows(weights, bias)
    half = bias.shape[0] // 2
    pieces = cross.shape[2] // 128
    step = 128

    def body(number, side):
        def chunk(r, state):
            at = pl.ds(pl.multiple_of(side * half + r * step, step), step)
            weight = bias[at, :]
            tops, totals = [], []
            for q in range(pieces):
                part = cross[number, at, q * 128 : (q + 1) * 128]
                scores = (part + part if twice else part) + weight
                top = jnp.maximum(state[0][q], fold(scores, jnp.maximum))
                total = jnp.sum(jnp.exp(scores.reshape(-1, 8, 128) - top[None]), axis=0)
                totals.append(state[1][q] * jnp.exp(state[0][q] - top) + total)
                tops.append(top)
            return tuple(tops), tuple(totals)

        going = (side == 1) & (flags[number] != 0)
        cuts = [slice(q * 128, (q + 1) * 128) for q in range(pieces)]
        state = (
            tuple(jnp.where(going, top_ref[:, cut], NEG_FILL) for cut in cuts),
            tuple(jnp.where(going, total_ref[:, cut], 0.0) for cut in cuts),
        )
        tops, totals = lax.fori_loop(0, half // step, chunk, state, unroll=COLUMN_UNROLL)
        more = (side == 0) & (flags[BUFFERS + number] != 0)

        @pl.when(more)
        def _():
            for cut, top, total in zip(cuts, tops, totals):
                top_ref[:, cut] = top
                total_ref[:, cut] = total

        @pl.when(jnp.logical_not(more))
        def _():
            slot = flags[2 * BUFFERS + number]
            for q, (top, total) in enumerate(zip(tops, totals)):
                greatest = jnp.max(top, axis=0, keepdims=True)
                total = jnp.sum(total * jnp.exp(top - greatest), axis=0, keepdims=True)
                out[slot, q : q + 1, :] = greatest + jnp.log(total)

    each_listed(flags, body)


WHOLE = pl.BlockSpec(memory_space=pltpu.VMEM)
SCALARS = pl.BlockSpec(memory_space=pltpu.SMEM)
PARAMS = pltpu.CompilerParams(vmem_limit_bytes=20 * 2**20)


def in_vmem(value):
    return pltpu.with_memory_space_constraint(value, pltpu.VMEM)


def in_hbm(value):
    return pltpu.with_memory_space_constraint(value, pltpu.HBM)


def call_message(scale, half_index, points, masses, initial, src):
    columns, depth = points.shape[0] // 2, points.shape[1]
    return pl.pallas_call(
        functools.partial(message_kernel, scale),
        out_shape=[
            pltpu.VMEM((columns + TAIL, depth), jnp.bfloat16),
            pltpu.VMEM(src.shape, jnp.bfloat16),
        ],
        in_specs=[SCALARS] + [pl.BlockSpec(memory_space=pltpu.HBM)] * 4,
        out_specs=[WHOLE] * 2,
        scratch_shapes=[
            pltpu.VMEM((columns, depth), jnp.bfloat16),
            pltpu.VMEM((2 * columns // 128, 128), jnp.float32),
            pltpu.VMEM((2 * columns // 128, 128), jnp.float32),
            pltpu.SemaphoreType.DMA((4,)),
        ],
        compiler_params=PARAMS,
        name="message",
    )(half_index.reshape(1), *map(in_hbm, (points, masses.reshape(-1, 128), initial.reshape(-1, 128), src)))


def call_first(numbers, first, last, flags, sources, targets, state):
    half, depth = sources[0].shape
    rows, columns, count = 2 * half, targets[0].shape[0] - TAIL, len(numbers)
    out_shape = [
        pltpu.VMEM((BUFFERS, rows, columns), jnp.float32),
        pltpu.VMEM((BUFFERS, columns // 128, 128), jnp.float32),
        pltpu.VMEM((rows, 128), jnp.float32),
        pltpu.VMEM((rows, 128), jnp.float32),
    ]
    if last:
        out_shape.append(jax.ShapeDtypeStruct((rows // 128, 128), jnp.float32))
    operands = [flags, *sources, *targets]
    aliases = {}
    if not first:
        aliases = {len(operands) + i: i for i in range(4)}
        operands += [in_vmem(value) for value in state]
    return pl.pallas_call(
        functools.partial(first_kernel, numbers, first, last),
        out_shape=out_shape,
        in_specs=[SCALARS] + [WHOLE] * (len(operands) - 1),
        out_specs=[WHOLE] * len(out_shape),
        scratch_shapes=[
            pltpu.VMEM((2, half, depth), jnp.bfloat16),
            pltpu.VMEM((count, columns, depth), jnp.bfloat16),
            pltpu.VMEM((count, columns // 128, 128), jnp.float32),
        ],
        input_output_aliases=aliases,
        compiler_params=PARAMS,
        cost_estimate=pl.CostEstimate(
            flops=2 * count * rows * columns * depth,
            bytes_accessed=count * rows * columns,
            transcendentals=count * rows * columns,
        ),
        name="first_rows",
    )(*operands)


def call_rows(flags, cross, masses, sums):
    rows = cross.shape[1]
    return pl.pallas_call(
        row_kernel,
        out_shape=jax.ShapeDtypeStruct((rows // 128, 128), jnp.float32),
        in_specs=[SCALARS] + [WHOLE] * 3,
        out_specs=WHOLE,
        scratch_shapes=[pltpu.VMEM((rows, 128), jnp.float32)] * 2,
        compiler_params=PARAMS,
        name="rows",
    )(flags, in_vmem(cross), in_vmem(masses), sums)


def call_columns(twice, flags, cross, weights):
    rows, columns = cross.shape[1:]
    return pl.pallas_call(
        functools.partial(column_kernel, twice),
        out_shape=jax.ShapeDtypeStruct((BUFFERS, columns // 128, 128), jnp.float32),
        in_specs=[SCALARS] + [WHOLE] * 2,
        out_specs=WHOLE,
        scratch_shapes=[pltpu.VMEM((rows, 128), jnp.float32)]
        + [pltpu.VMEM((8, columns), jnp.float32)] * 2,
        compiler_params=PARAMS,
        name="columns",
    )(flags, in_vmem(cross), weights)


def fill_rows(value, before, after):
    return jnp.pad(value, ((before, after), (0, 0), (0, 0)), constant_values=NEG_FILL)


def local(src_points, src_log_mass, tgt_points, tgt_log_mass, initial_potential, pair_list, pair_count):
    block = lax.axis_index("blk")
    rep = lax.axis_index("rep")
    blocks = lax.axis_size("blk")
    core = block % 2
    half_index = (rep % 2) ^ ((block // SEGMENT) % 2)
    rows = src_points.shape[0]
    width = tgt_points.shape[0]
    columns = width // 2

    message, own = call_message(
        1.0 / EPS_START, half_index, tgt_points, tgt_log_mass, initial_potential, src_points
    )
    mate = send(src_points, diagonal, blocks)

    before = send(message, along(2, blocks), blocks)
    after = send(message, along(-2, blocks), blocks)
    third = send(message, by_core(-3, 3, blocks), blocks)
    tied, mate = lax.optimization_barrier((message, mate))
    beside = send(tied, sibling, blocks)
    sources = [own, mate]
    groups = ((0, 1), (2, 3, 4), (5, 6, 7))

    even_slots = (3, 4, 1, 5, 0, 2, 6, 7)
    odd_slots = (4, 3, 2, 6, 7, 1, 5, 0)
    slots = jnp.where(core == 0, jnp.array(even_slots, jnp.int32), jnp.array(odd_slots, jnp.int32))
    names = (block - core - 3 + slots) % blocks

    def kept(source_block):
        row_names = pair_list[source_block]
        in_use = jnp.arange(row_names.shape[0], dtype=jnp.int32) < pair_count[source_block]
        return jnp.any((row_names[None, :] == names[:, None]) & in_use[None, :], axis=1).astype(jnp.int32)

    kept_pairs = jnp.stack([kept(block), kept(block + 1 - 2 * core)])
    entries = jnp.arange(2 * BUFFERS, dtype=jnp.int32)
    listed = kept_pairs.T.reshape(-1)
    rank = jnp.sum(jnp.where(entries[None, :] < entries[:, None], listed[None, :], 0), axis=1)
    order = jnp.sum(
        jnp.where((rank[:, None] == entries[None, :]) & (listed[:, None] != 0), entries[:, None], 0), axis=0
    )
    total = jnp.broadcast_to(jnp.sum(listed), (BUFFERS,))
    flags = jnp.concatenate([kept_pairs.reshape(-1), slots, total, order])

    state = call_first(groups[0], True, False, flags, sources, [message, beside], ())
    state, arrived = lax.optimization_barrier((state, (before, after, third)))
    passed_on = [send(value, sibling, blocks) for value in arrived]
    state = call_first(groups[1], False, False, flags, sources, arrived, state)
    *state, last = call_first(groups[2], False, True, flags, sources, passed_on, state)
    cross, window_masses = state[:2]
    part = last.reshape(-1)

    for sweep in range(ITERS):
        epsilon = EPS_START * 0.5**sweep
        if sweep == 0:
            got = send(jnp.concatenate([part, src_log_mass]), diagonal, blocks)
            both_masses = jnp.concatenate([src_log_mass, got[2 * rows :]])
        else:
            part = call_rows(flags, cross, window_masses, column_sums).reshape(-1)
            got = send(part, diagonal, blocks)
        row_sums = log_merge(part, jnp.concatenate([got[rows : 2 * rows], got[:rows]]))
        weighted = (both_masses - row_sums).reshape(2 * rows // 128, 128)
        part = call_columns(sweep > 0, flags, cross, weighted)
        chip = log_merge(
            part,
            send(part, sibling, blocks),
            send(part, lambda b, r: (b, r ^ 2), blocks),
            send(part, lambda b, r: (b ^ 1, r ^ 2), blocks),
        )
        forward = core == 0
        if sweep + 1 < ITERS:
            got = []
            for n in (1, 2, 3):
                kept_rows = 8 - 2 * n
                out = jnp.where(forward, chip[2 * n :], chip[:kept_rows])
                out = send(out, by_core(2 * n, -2 * n, blocks), blocks)
                got.append(
                    jnp.where(forward, fill_rows(out, 0, 2 * n), fill_rows(out, 2 * n, 0))
                )
            side = log_merge(*got)
            column_sums = log_merge(chip, side, send(side, sibling, blocks))
        else:
            near = jnp.where(forward, chip[5:7], chip[1:3])
            near = send(near, by_core(2, -2, blocks), blocks)
            far = jnp.where(forward, chip[7], chip[0])
            far = send(far, by_core(4, -4, blocks), blocks)
            empty = jnp.full_like(far, NEG_FILL)
            far = jnp.where(forward, jnp.stack([far, empty]), jnp.stack([empty, far]))
            side = log_merge(jnp.where(forward, chip[3:5], jnp.full_like(near, NEG_FILL)), near, far)
            over_core = send(side, sibling, blocks)
            over_half = send(side, lambda b, r: (b, r ^ 1), blocks)
            over_both = send(side, diagonal, blocks)
            mine = log_merge(side, over_core)
            other = log_merge(over_half, over_both)
            mine = jnp.where(core == 0, mine[0], mine[1]).reshape(columns)
            other = jnp.where(core == 0, other[0], other[1]).reshape(columns)
            whole = jnp.where(
                half_index == 0, jnp.concatenate([mine, other]), jnp.concatenate([other, mine])
            )
            source_pot = half_norms(src_points) - epsilon * row_sums[:rows]
            target_pot = half_norms(tgt_points) - epsilon * whole
    return source_pot, target_pot


def solution(mesh):
    in_specs = (
        P(("blk", "rep"), None),
        P(("blk", "rep")),
        P("blk", None),
        P("blk"),
        P("blk"),
        P(),
        P(),
    )
    out_specs = (P(("blk", "rep")), P("blk"))
    return jax.shard_map(local, mesh=mesh, in_specs=in_specs, out_specs=out_specs, check_vma=False)
```

```python
import functools

import jax
import jax.numpy as jnp
from jax import lax
from jax.experimental import pallas as pl
from jax.experimental.pallas import tpu as pltpu
from jax.sharding import PartitionSpec as P

ITERS = 2
EPS_START = 0.5
NEG_FILL = -1e30
ROW_UNROLL = 8
COLUMN_UNROLL = 4
BUFFERS = 8
REPS = 4
SEGMENT = 8
TAIL = 16


def send(value, place, blocks):
    pairs = []
    for block in range(blocks):
        for rep in range(REPS):
            target = place(block, rep)
            if target is not None:
                pairs.append((block * REPS + rep, target[0] % blocks * REPS + target[1]))
    return lax.ppermute(value, ("blk", "rep"), pairs)


def crosses(one, other, blocks):
    return one % blocks // SEGMENT != other % blocks // SEGMENT


def along(steps, blocks, crossing=None):
    def place(block, rep):
        target = block + steps
        if crossing not in (None, crosses(block, target, blocks)):
            return None
        return target, REPS - 1 - rep if crosses(block, target, blocks) else rep

    return place


def by_core(even_steps, odd_steps, blocks, crossing=None):
    even, odd = along(even_steps, blocks, crossing), along(odd_steps, blocks, crossing)
    return lambda block, rep: even(block, rep) if block % 2 == 0 else odd(block, rep)


def sibling(block, rep):
    return block ^ 1, rep


def diagonal(block, rep):
    return block ^ 1, rep ^ 2


def half_norms(points):
    widened = points.astype(jnp.float32)
    return 0.5 * jnp.sum(widened * widened, axis=1)


def terms(vector):
    parts = []
    for _ in range(3):
        parts.append(vector.astype(jnp.bfloat16).astype(jnp.float32))
        vector = vector - parts[-1]
    return parts


def log_merge(*parts):
    top = functools.reduce(jnp.maximum, parts)
    return top + jnp.log(sum(jnp.exp(part - top) for part in parts))


def spread_rows(vector_ref, bias_ref):
    for q in range(bias_ref.shape[0] // 128):
        row = vector_ref[q : q + 1, :]
        bias_ref[q * 128 : (q + 1) * 128, :] = jnp.broadcast_to(row, (128, 128)).T


def fold(value, combine):
    rows = value.shape[0]
    while rows > 8:
        rows //= 2
        value = combine(value[:rows], value[rows:])
    return value


def row_update(cross_ref, index, bias, twice, side, half, top_ref, total_ref):
    step = 64

    def chunk(r, _):
        at = pl.ds(pl.multiple_of(side * half + r * step, step), step)
        scores = []
        for q, term in enumerate(bias):
            part = cross_ref[index, at, q * 128 : (q + 1) * 128]
            scores.append((part + part if twice else part) + term)
        old = top_ref[at, :]
        top = jnp.maximum(old, functools.reduce(jnp.maximum, scores))
        total = functools.reduce(jnp.add, [jnp.exp(part - top) for part in scores])
        total_ref[at, :] = total_ref[at, :] * jnp.exp(old - top) + total
        top_ref[at, :] = top
        return 0

    lax.fori_loop(0, half // step, chunk, 0, unroll=ROW_UNROLL)


def row_finish(top_ref, total_ref, out):
    for q in range(out.shape[0]):
        top = top_ref[q * 128 : (q + 1) * 128, :].T
        greatest = jnp.max(top, axis=0, keepdims=True)
        total = total_ref[q * 128 : (q + 1) * 128, :].T * jnp.exp(top - greatest)
        out[q : q + 1, :] = greatest + jnp.log(jnp.sum(total, axis=0, keepdims=True))


def each_listed(flags, body):
    def unit(u, _):
        entry = flags[4 * BUFFERS + u]
        body(lax.div(entry, 2), lax.rem(entry, 2))
        return 0

    lax.fori_loop(0, flags[3 * BUFFERS], unit, 0)


def each_kept(flags, first, count, body):
    def unit(u, _):
        number, side = first + lax.div(u, 2), lax.rem(u, 2)

        @pl.when(flags[side * BUFFERS + number] != 0)
        def _():
            body(number, side)

        return 0

    lax.fori_loop(0, 2 * count, unit, 0)


def message_kernel(
    scale, half, points, masses, initial, src, out, quarter, src_out, block_ref, mass_ref, initial_ref, sems
):
    columns, depth = block_ref.shape
    src_copy = pltpu.make_async_copy(src, src_out, sems.at[1])
    copy = pltpu.make_async_copy(
        points.at[pl.ds(pl.multiple_of(half[0] * columns, columns), columns), :], block_ref, sems.at[0]
    )
    small = [
        pltpu.make_async_copy(masses, mass_ref, sems.at[2]),
        pltpu.make_async_copy(initial, initial_ref, sems.at[3]),
    ]
    for start in (copy, *small, src_copy):
        start.start()
    copy.wait()
    value = block_ref[...].astype(jnp.float32)
    out[:columns, :] = (value * scale).astype(jnp.bfloat16)
    squares = value * value
    high = squares.astype(jnp.bfloat16)
    low = (squares - high.astype(jnp.float32)).astype(jnp.bfloat16)
    ones = jnp.ones((8, depth), jnp.bfloat16)
    norms = sum(
        lax.dot_general(ones, part, (((1,), (1,)), ((), ())), preferred_element_type=jnp.float32)
        for part in (high, low)
    )
    count = columns // 128
    norms = jnp.concatenate([norms[0:1, q * 128 : (q + 1) * 128] for q in range(count)], axis=0)

    def pick(ref):
        return jnp.where(half[0] == 0, ref[:count, :], ref[count:, :])

    for copy in small:
        copy.wait()
    mass = pick(mass_ref)
    bias = mass + (pick(initial_ref) - 0.5 * norms) * scale
    rows = [jnp.concatenate(pair, axis=1) for pair in zip(terms(bias), terms(mass))]
    rows.append(jnp.zeros((TAIL - 3 * count, 256), jnp.float32))
    tail = jnp.concatenate(rows, axis=0).astype(jnp.bfloat16)
    out[columns:, :] = tail
    quarter[columns // 2 :, :] = tail
    for q in range(2):

        @pl.when(half[1] == q)
        def _(q=q):
            quarter[: columns // 2, :] = out[q * columns // 2 : (q + 1) * columns // 2, :]

    src_copy.wait()


def arrive_kernel(where, *refs):
    count = len(refs) // 4
    for d in range(count):
        whole, first, second, out = refs[d::count]
        half = first.shape[0] - TAIL

        @pl.when(where[d] == 0)
        def _(whole=whole, out=out):
            out[...] = whole[...]

        @pl.when(where[d] != 0)
        def _(first=first, second=second, out=out):
            out[2 * half :, :] = first[half:, :]
            for q in range(2):

                @pl.when(where[count] == q)
                def _(q=q):
                    out[q * half : (q + 1) * half, :] = first[:half, :]
                    out[(1 - q) * half : (2 - q) * half, :] = second[:half, :]


def first_kernel(numbers, first, last, flags, *refs):
    sources, targets = refs[:2], refs[2 : 2 + len(numbers)]
    refs = refs[2 + len(numbers) :]
    if not first:
        refs = refs[4:]
    cross, masses, top_ref, total_ref = refs[:4]
    src_ref, tgt_ref, bias_ref = refs[-3:]
    if first:
        top_ref[...] = jnp.full(top_ref.shape, NEG_FILL, jnp.float32)
        total_ref[...] = jnp.zeros(total_ref.shape, jnp.float32)
    half = sources[0].shape[0]
    width = cross.shape[2]
    for side, src in enumerate(sources):
        src_ref[side] = src[...]
    for k, number in enumerate(numbers):
        tgt_ref[k] = targets[k][:width, :]
        tail = targets[k][width:, :].astype(jnp.float32)
        count = width // 128
        vectors = tail[:count] + tail[count : 2 * count] + tail[2 * count : 3 * count]
        bias_ref[k] = vectors[:, :128]
        masses[number] = vectors[:, 128:]

    def body(number, side):
        k = number - numbers[0]
        for c in range(0, width, 256):
            for r in range(0, half, 256):
                at = pl.ds(pl.multiple_of(side * half + r, 256), 256)
                cross[number, at, c : c + 256] = lax.dot_general(
                    src_ref[side, r : r + 256, :],
                    tgt_ref[k, c : c + 256, :],
                    (((1,), (1,)), ((), ())),
                    preferred_element_type=jnp.float32,
                )
        bias = [bias_ref[k, q : q + 1, :] for q in range(width // 128)]
        row_update(cross, number, bias, False, side, half, top_ref, total_ref)

    each_kept(flags, numbers[0], len(numbers), body)
    if last:
        row_finish(top_ref, total_ref, refs[4])


def row_kernel(flags, cross, masses, sums, out, top_ref, total_ref):
    top_ref[...] = jnp.full(top_ref.shape, NEG_FILL, jnp.float32)
    total_ref[...] = jnp.zeros(total_ref.shape, jnp.float32)
    half = top_ref.shape[0] // 2

    def body(number, side):
        slot = flags[2 * BUFFERS + number]
        bias = [
            masses[number, q : q + 1, :] - 2.0 * sums[slot, q : q + 1, :] for q in range(masses.shape[1])
        ]
        row_update(cross, number, bias, True, side, half, top_ref, total_ref)

    each_listed(flags, body)
    row_finish(top_ref, total_ref, out)


def column_kernel(twice, flags, cross, weights, out, bias, top_ref, total_ref):
    out[...] = jnp.full(out.shape, NEG_FILL, jnp.float32)
    spread_rows(weights, bias)
    half = bias.shape[0] // 2
    pieces = cross.shape[2] // 128
    step = 128

    def body(number, side):
        def chunk(r, state):
            at = pl.ds(pl.multiple_of(side * half + r * step, step), step)
            weight = bias[at, :]
            tops, totals = [], []
            for q in range(pieces):
                part = cross[number, at, q * 128 : (q + 1) * 128]
                scores = (part + part if twice else part) + weight
                top = jnp.maximum(state[0][q], fold(scores, jnp.maximum))
                total = jnp.sum(jnp.exp(scores.reshape(-1, 8, 128) - top[None]), axis=0)
                totals.append(state[1][q] * jnp.exp(state[0][q] - top) + total)
                tops.append(top)
            return tuple(tops), tuple(totals)

        going = (side == 1) & (flags[number] != 0)
        cuts = [slice(q * 128, (q + 1) * 128) for q in range(pieces)]
        state = (
            tuple(jnp.where(going, top_ref[:, cut], NEG_FILL) for cut in cuts),
            tuple(jnp.where(going, total_ref[:, cut], 0.0) for cut in cuts),
        )
        tops, totals = lax.fori_loop(0, half // step, chunk, state, unroll=COLUMN_UNROLL)
        more = (side == 0) & (flags[BUFFERS + number] != 0)

        @pl.when(more)
        def _():
            for cut, top, total in zip(cuts, tops, totals):
                top_ref[:, cut] = top
                total_ref[:, cut] = total

        @pl.when(jnp.logical_not(more))
        def _():
            slot = flags[2 * BUFFERS + number]
            for q, (top, total) in enumerate(zip(tops, totals)):
                greatest = jnp.max(top, axis=0, keepdims=True)
                total = jnp.sum(total * jnp.exp(top - greatest), axis=0, keepdims=True)
                out[slot, q : q + 1, :] = greatest + jnp.log(total)

    each_listed(flags, body)


WHOLE = pl.BlockSpec(memory_space=pltpu.VMEM)
SCALARS = pl.BlockSpec(memory_space=pltpu.SMEM)
PARAMS = pltpu.CompilerParams(vmem_limit_bytes=20 * 2**20)


def in_vmem(value):
    return pltpu.with_memory_space_constraint(value, pltpu.VMEM)


def in_hbm(value):
    return pltpu.with_memory_space_constraint(value, pltpu.HBM)


def call_message(scale, half_index, points, masses, initial, src):
    columns, depth = points.shape[0] // 2, points.shape[1]
    return pl.pallas_call(
        functools.partial(message_kernel, scale),
        out_shape=[
            pltpu.VMEM((columns + TAIL, depth), jnp.bfloat16),
            pltpu.VMEM((columns // 2 + TAIL, depth), jnp.bfloat16),
            pltpu.VMEM(src.shape, jnp.bfloat16),
        ],
        in_specs=[SCALARS] + [pl.BlockSpec(memory_space=pltpu.HBM)] * 4,
        out_specs=[WHOLE] * 3,
        scratch_shapes=[
            pltpu.VMEM((columns, depth), jnp.bfloat16),
            pltpu.VMEM((2 * columns // 128, 128), jnp.float32),
            pltpu.VMEM((2 * columns // 128, 128), jnp.float32),
            pltpu.SemaphoreType.DMA((4,)),
        ],
        compiler_params=PARAMS,
        name="message",
    )(half_index, *map(in_hbm, (points, masses.reshape(-1, 128), initial.reshape(-1, 128), src)))


def call_arrive(where, wholes, firsts, seconds):
    return pl.pallas_call(
        arrive_kernel,
        out_shape=[pltpu.VMEM(whole.shape, whole.dtype) for whole in wholes],
        in_specs=[SCALARS] + [WHOLE] * (3 * len(wholes)),
        out_specs=[WHOLE] * len(wholes),
        compiler_params=PARAMS,
        name="arrive",
    )(where, *wholes, *firsts, *seconds)


def call_first(numbers, first, last, flags, sources, targets, state):
    half, depth = sources[0].shape
    rows, columns, count = 2 * half, targets[0].shape[0] - TAIL, len(numbers)
    out_shape = [
        pltpu.VMEM((BUFFERS, rows, columns), jnp.float32),
        pltpu.VMEM((BUFFERS, columns // 128, 128), jnp.float32),
        pltpu.VMEM((rows, 128), jnp.float32),
        pltpu.VMEM((rows, 128), jnp.float32),
    ]
    if last:
        out_shape.append(jax.ShapeDtypeStruct((rows // 128, 128), jnp.float32))
    operands = [flags, *sources, *targets]
    aliases = {}
    if not first:
        aliases = {len(operands) + i: i for i in range(4)}
        operands += [in_vmem(value) for value in state]
    return pl.pallas_call(
        functools.partial(first_kernel, numbers, first, last),
        out_shape=out_shape,
        in_specs=[SCALARS] + [WHOLE] * (len(operands) - 1),
        out_specs=[WHOLE] * len(out_shape),
        scratch_shapes=[
            pltpu.VMEM((2, half, depth), jnp.bfloat16),
            pltpu.VMEM((count, columns, depth), jnp.bfloat16),
            pltpu.VMEM((count, columns // 128, 128), jnp.float32),
        ],
        input_output_aliases=aliases,
        compiler_params=PARAMS,
        cost_estimate=pl.CostEstimate(
            flops=2 * count * rows * columns * depth,
            bytes_accessed=count * rows * columns,
            transcendentals=count * rows * columns,
        ),
        name="first_rows",
    )(*operands)


def call_rows(flags, cross, masses, sums):
    rows = cross.shape[1]
    return pl.pallas_call(
        row_kernel,
        out_shape=jax.ShapeDtypeStruct((rows // 128, 128), jnp.float32),
        in_specs=[SCALARS] + [WHOLE] * 3,
        out_specs=WHOLE,
        scratch_shapes=[pltpu.VMEM((rows, 128), jnp.float32)] * 2,
        compiler_params=PARAMS,
        name="rows",
    )(flags, in_vmem(cross), in_vmem(masses), sums)


def call_columns(twice, flags, cross, weights):
    rows, columns = cross.shape[1:]
    return pl.pallas_call(
        functools.partial(column_kernel, twice),
        out_shape=jax.ShapeDtypeStruct((BUFFERS, columns // 128, 128), jnp.float32),
        in_specs=[SCALARS] + [WHOLE] * 2,
        out_specs=WHOLE,
        scratch_shapes=[pltpu.VMEM((rows, 128), jnp.float32)]
        + [pltpu.VMEM((8, columns), jnp.float32)] * 2,
        compiler_params=PARAMS,
        name="columns",
    )(flags, in_vmem(cross), weights)


def fill_rows(value, before, after):
    return jnp.pad(value, ((before, after), (0, 0), (0, 0)), constant_values=NEG_FILL)


def local(src_points, src_log_mass, tgt_points, tgt_log_mass, initial_potential, pair_list, pair_count):
    block = lax.axis_index("blk")
    rep = lax.axis_index("rep")
    blocks = lax.axis_size("blk")
    core = block % 2
    half_index = (rep // 2) ^ ((block // SEGMENT) % 2)
    rows = src_points.shape[0]
    width = tgt_points.shape[0]
    columns = width // 2

    message, quarter, own = call_message(
        1.0 / EPS_START, jnp.stack([half_index, rep % 2]), tgt_points, tgt_log_mass, initial_potential, src_points
    )
    mate = send(src_points, diagonal, blocks)

    routes = ((2, 2), (-2, -2), (-3, 3))

    def either(*places):
        return lambda b, r: next((place(b, r) for place in places if place(b, r)), None)

    crossing = [by_core(*steps, blocks, True) for steps in routes]
    crossed = [send(quarter, either(*crossing[:2]), blocks), send(quarter, crossing[2], blocks)]
    wholes = [send(message, by_core(*steps, blocks, False), blocks) for steps in routes]

    def handed_on(*origins):
        def place(b, r):
            return (b, r ^ 1) if any(crosses(b, b + origin[b % 2], blocks) for origin in origins) else None

        return place

    handed = [
        send(crossed[0], handed_on((-2, -2), (2, 2)), blocks),
        send(crossed[1], handed_on((-3, 3)), blocks),
    ]
    firsts, seconds = [[pieces[0], pieces[0], pieces[1]] for pieces in (crossed, handed)]
    origins = (block - 2, block + 2, block - 3 + 6 * core)
    where = jnp.stack([crosses(block, origin, blocks).astype(jnp.int32) for origin in origins] + [1 - rep % 2])
    tied, mate = lax.optimization_barrier((message, mate))
    beside = send(tied, sibling, blocks)
    sources = [own, mate]
    groups = ((0, 1), (2, 3, 4), (5, 6, 7))

    even_slots = (3, 4, 1, 5, 0, 2, 6, 7)
    odd_slots = (4, 3, 2, 6, 7, 1, 5, 0)
    slots = jnp.where(core == 0, jnp.array(even_slots, jnp.int32), jnp.array(odd_slots, jnp.int32))
    names = (block - core - 3 + slots) % blocks

    def kept(source_block):
        row_names = pair_list[source_block]
        in_use = jnp.arange(row_names.shape[0], dtype=jnp.int32) < pair_count[source_block]
        return jnp.any((row_names[None, :] == names[:, None]) & in_use[None, :], axis=1).astype(jnp.int32)

    kept_pairs = jnp.stack([kept(block), kept(block + 1 - 2 * core)])
    entries = jnp.arange(2 * BUFFERS, dtype=jnp.int32)
    listed = kept_pairs.T.reshape(-1)
    rank = jnp.sum(jnp.where(entries[None, :] < entries[:, None], listed[None, :], 0), axis=1)
    order = jnp.sum(
        jnp.where((rank[:, None] == entries[None, :]) & (listed[:, None] != 0), entries[:, None], 0), axis=0
    )
    total = jnp.broadcast_to(jnp.sum(listed), (BUFFERS,))
    flags = jnp.concatenate([kept_pairs.reshape(-1), slots, total, order])

    state = call_first(groups[0], True, False, flags, sources, [message, beside], ())
    state, where = lax.optimization_barrier((state, where))
    arrived = call_arrive(where, wholes, firsts, seconds)
    passed_on = [send(value, sibling, blocks) for value in arrived]
    state = call_first(groups[1], False, False, flags, sources, arrived, state)
    *state, last = call_first(groups[2], False, True, flags, sources, passed_on, state)
    cross, window_masses = state[:2]
    part = last.reshape(-1)

    for sweep in range(ITERS):
        epsilon = EPS_START * 0.5**sweep
        if sweep == 0:
            got = send(jnp.concatenate([part, src_log_mass]), diagonal, blocks)
            both_masses = jnp.concatenate([src_log_mass, got[2 * rows :]])
        else:
            part = call_rows(flags, cross, window_masses, column_sums).reshape(-1)
            got = send(part, diagonal, blocks)
        row_sums = log_merge(part, jnp.concatenate([got[rows : 2 * rows], got[:rows]]))
        weighted = (both_masses - row_sums).reshape(2 * rows // 128, 128)
        part = call_columns(sweep > 0, flags, cross, weighted)
        chip = log_merge(
            part,
            send(part, sibling, blocks),
            send(part, lambda b, r: (b, r ^ 1), blocks),
            send(part, lambda b, r: (b ^ 1, r ^ 1), blocks),
        )
        forward = core == 0
        if sweep + 1 < ITERS:
            got = []
            for n in (1, 2, 3):
                kept_rows = 8 - 2 * n
                out = jnp.where(forward, chip[2 * n :], chip[:kept_rows])
                out = send(out, by_core(2 * n, -2 * n, blocks), blocks)
                got.append(
                    jnp.where(forward, fill_rows(out, 0, 2 * n), fill_rows(out, 2 * n, 0))
                )
            side = log_merge(*got)
            column_sums = log_merge(chip, side, send(side, sibling, blocks))
        else:
            near = jnp.where(forward, chip[5:7], chip[1:3])
            near = send(near, by_core(2, -2, blocks), blocks)
            far = jnp.where(forward, chip[7], chip[0])
            far = send(far, by_core(4, -4, blocks), blocks)
            empty = jnp.full_like(far, NEG_FILL)
            far = jnp.where(forward, jnp.stack([far, empty]), jnp.stack([empty, far]))
            side = log_merge(jnp.where(forward, chip[3:5], jnp.full_like(near, NEG_FILL)), near, far)
            over_core = send(side, sibling, blocks)
            over_half = send(side, lambda b, r: (b, r ^ 2), blocks)
            over_both = send(side, diagonal, blocks)
            mine = log_merge(side, over_core)
            other = log_merge(over_half, over_both)
            mine = jnp.where(core == 0, mine[0], mine[1]).reshape(columns)
            other = jnp.where(core == 0, other[0], other[1]).reshape(columns)
            whole = jnp.where(
                half_index == 0, jnp.concatenate([mine, other]), jnp.concatenate([other, mine])
            )
            source_pot = half_norms(src_points) - epsilon * row_sums[:rows]
            target_pot = half_norms(tgt_points) - epsilon * whole
    return source_pot, target_pot


def solution(mesh):
    in_specs = (
        P(("blk", "rep"), None),
        P(("blk", "rep")),
        P("blk", None),
        P("blk"),
        P("blk"),
        P(),
        P(),
    )
    out_specs = (P(("blk", "rep")), P("blk"))
    return jax.shard_map(local, mesh=mesh, in_specs=in_specs, out_specs=out_specs, check_vma=False)
```

```python
import functools

import jax
import jax.numpy as jnp
from jax import lax
from jax.experimental import pallas as pl
from jax.experimental.pallas import tpu as pltpu
from jax.sharding import PartitionSpec as P

ITERS = 2
EPS_START = 0.5
NEG_FILL = -1e30
ROW_UNROLL = 8
COLUMN_UNROLL = 4
BUFFERS = 8
REPS = 4
SEGMENT = 8
TAIL = 16


def send(value, place, blocks):
    pairs = []
    for block in range(blocks):
        for rep in range(REPS):
            to_block, to_rep = place(block, rep)
            pairs.append((block * REPS + rep, to_block % blocks * REPS + to_rep))
    return lax.ppermute(value, ("blk", "rep"), pairs)


def along(steps, blocks):
    def place(block, rep):
        target = (block + steps) % blocks
        return target, rep if (target // SEGMENT - block // SEGMENT) % 2 == 0 else REPS - 1 - rep

    return place


def by_core(even_steps, odd_steps, blocks):
    even, odd = along(even_steps, blocks), along(odd_steps, blocks)
    return lambda block, rep: even(block, rep) if block % 2 == 0 else odd(block, rep)


def sibling(block, rep):
    return block ^ 1, rep


def diagonal(block, rep):
    return block ^ 1, rep ^ 1


def half_norms(points):
    widened = points.astype(jnp.float32)
    return 0.5 * jnp.sum(widened * widened, axis=1)


def terms(vector):
    parts = []
    for _ in range(3):
        parts.append(vector.astype(jnp.bfloat16).astype(jnp.float32))
        vector = vector - parts[-1]
    return parts


def log_merge(*parts):
    top = functools.reduce(jnp.maximum, parts)
    return top + jnp.log(sum(jnp.exp(part - top) for part in parts))


def spread_rows(vector_ref, bias_ref):
    for q in range(bias_ref.shape[0] // 128):
        row = vector_ref[q : q + 1, :]
        bias_ref[q * 128 : (q + 1) * 128, :] = jnp.broadcast_to(row, (128, 128)).T


def fold(value, combine):
    rows = value.shape[0]
    while rows > 8:
        rows //= 2
        value = combine(value[:rows], value[rows:])
    return value


def row_update(cross_ref, index, bias, twice, side, half, top_ref, total_ref):
    step = 64

    def chunk(r, _):
        at = pl.ds(pl.multiple_of(side * half + r * step, step), step)
        scores = []
        for q, term in enumerate(bias):
            part = cross_ref[index, at, q * 128 : (q + 1) * 128]
            scores.append((part + part if twice else part) + term)
        old = top_ref[at, :]
        top = jnp.maximum(old, functools.reduce(jnp.maximum, scores))
        total = functools.reduce(jnp.add, [jnp.exp(part - top) for part in scores])
        total_ref[at, :] = total_ref[at, :] * jnp.exp(old - top) + total
        top_ref[at, :] = top
        return 0

    lax.fori_loop(0, half // step, chunk, 0, unroll=ROW_UNROLL)


def row_finish(top_ref, total_ref, out):
    for q in range(out.shape[0]):
        top = top_ref[q * 128 : (q + 1) * 128, :].T
        greatest = jnp.max(top, axis=0, keepdims=True)
        total = total_ref[q * 128 : (q + 1) * 128, :].T * jnp.exp(top - greatest)
        out[q : q + 1, :] = greatest + jnp.log(jnp.sum(total, axis=0, keepdims=True))


def each_listed(flags, body):
    def unit(u, _):
        entry = flags[4 * BUFFERS + u]
        body(lax.div(entry, 2), lax.rem(entry, 2))
        return 0

    lax.fori_loop(0, flags[3 * BUFFERS], unit, 0)


def each_kept(flags, first, count, body):
    def unit(u, _):
        number, side = first + lax.div(u, 2), lax.rem(u, 2)

        @pl.when(flags[side * BUFFERS + number] != 0)
        def _():
            body(number, side)

        return 0

    lax.fori_loop(0, 2 * count, unit, 0)


def message_kernel(scale, half, points, masses, initial, src, out, src_out, block_ref, mass_ref, initial_ref, sems):
    columns, depth = block_ref.shape
    src_copy = pltpu.make_async_copy(src, src_out, sems.at[1])
    copy = pltpu.make_async_copy(
        points.at[pl.ds(pl.multiple_of(half[0] * columns, columns), columns), :], block_ref, sems.at[0]
    )
    small = [
        pltpu.make_async_copy(masses, mass_ref, sems.at[2]),
        pltpu.make_async_copy(initial, initial_ref, sems.at[3]),
    ]
    for start in (copy, *small, src_copy):
        start.start()
    copy.wait()
    value = block_ref[...].astype(jnp.float32)
    out[:columns, :] = (value * scale).astype(jnp.bfloat16)
    squares = value * value
    high = squares.astype(jnp.bfloat16)
    low = (squares - high.astype(jnp.float32)).astype(jnp.bfloat16)
    ones = jnp.ones((8, depth), jnp.bfloat16)
    norms = sum(
        lax.dot_general(ones, part, (((1,), (1,)), ((), ())), preferred_element_type=jnp.float32)
        for part in (high, low)
    )
    count = columns // 128
    norms = jnp.concatenate([norms[0:1, q * 128 : (q + 1) * 128] for q in range(count)], axis=0)

    def pick(ref):
        return jnp.where(half[0] == 0, ref[:count, :], ref[count:, :])

    for copy in small:
        copy.wait()
    mass = pick(mass_ref)
    bias = mass + (pick(initial_ref) - 0.5 * norms) * scale
    rows = [jnp.concatenate(pair, axis=1) for pair in zip(terms(bias), terms(mass))]
    rows.append(jnp.zeros((TAIL - 3 * count, 256), jnp.float32))
    out[columns:, :] = jnp.concatenate(rows, axis=0).astype(jnp.bfloat16)
    src_copy.wait()


def first_kernel(numbers, first, last, flags, *refs):
    sources, targets = refs[:2], refs[2 : 2 + len(numbers)]
    refs = refs[2 + len(numbers) :]
    if not first:
        refs = refs[4:]
    cross, masses, top_ref, total_ref = refs[:4]
    src_ref, tgt_ref, bias_ref = refs[-3:]
    if first:
        top_ref[...] = jnp.full(top_ref.shape, NEG_FILL, jnp.float32)
        total_ref[...] = jnp.zeros(total_ref.shape, jnp.float32)
    half = sources[0].shape[0]
    width = cross.shape[2]
    for side, src in enumerate(sources):
        src_ref[side] = src[...]
    for k, number in enumerate(numbers):
        tgt_ref[k] = targets[k][:width, :]
        tail = targets[k][width:, :].astype(jnp.float32)
        count = width // 128
        vectors = tail[:count] + tail[count : 2 * count] + tail[2 * count : 3 * count]
        bias_ref[k] = vectors[:, :128]
        masses[number] = vectors[:, 128:]

    def body(number, side):
        k = number - numbers[0]
        for c in range(0, width, 256):
            for r in range(0, half, 256):
                at = pl.ds(pl.multiple_of(side * half + r, 256), 256)
                cross[number, at, c : c + 256] = lax.dot_general(
                    src_ref[side, r : r + 256, :],
                    tgt_ref[k, c : c + 256, :],
                    (((1,), (1,)), ((), ())),
                    preferred_element_type=jnp.float32,
                )
        bias = [bias_ref[k, q : q + 1, :] for q in range(width // 128)]
        row_update(cross, number, bias, False, side, half, top_ref, total_ref)

    each_kept(flags, numbers[0], len(numbers), body)
    if last:
        row_finish(top_ref, total_ref, refs[4])


def row_kernel(flags, cross, masses, sums, out, top_ref, total_ref):
    top_ref[...] = jnp.full(top_ref.shape, NEG_FILL, jnp.float32)
    total_ref[...] = jnp.zeros(total_ref.shape, jnp.float32)
    half = top_ref.shape[0] // 2

    def body(number, side):
        slot = flags[2 * BUFFERS + number]
        bias = [
            masses[number, q : q + 1, :] - 2.0 * sums[slot, q : q + 1, :] for q in range(masses.shape[1])
        ]
        row_update(cross, number, bias, True, side, half, top_ref, total_ref)

    each_listed(flags, body)
    row_finish(top_ref, total_ref, out)


def column_kernel(twice, flags, cross, weights, out, bias, top_ref, total_ref):
    out[...] = jnp.full(out.shape, NEG_FILL, jnp.float32)
    spread_rows(weights, bias)
    half = bias.shape[0] // 2
    pieces = cross.shape[2] // 128
    step = 128

    def body(number, side):
        def chunk(r, state):
            at = pl.ds(pl.multiple_of(side * half + r * step, step), step)
            weight = bias[at, :]
            tops, totals = [], []
            for q in range(pieces):
                part = cross[number, at, q * 128 : (q + 1) * 128]
                scores = (part + part if twice else part) + weight
                top = jnp.maximum(state[0][q], fold(scores, jnp.maximum))
                total = jnp.sum(jnp.exp(scores.reshape(-1, 8, 128) - top[None]), axis=0)
                totals.append(state[1][q] * jnp.exp(state[0][q] - top) + total)
                tops.append(top)
            return tuple(tops), tuple(totals)

        going = (side == 1) & (flags[number] != 0)
        cuts = [slice(q * 128, (q + 1) * 128) for q in range(pieces)]
        state = (
            tuple(jnp.where(going, top_ref[:, cut], NEG_FILL) for cut in cuts),
            tuple(jnp.where(going, total_ref[:, cut], 0.0) for cut in cuts),
        )
        tops, totals = lax.fori_loop(0, half // step, chunk, state, unroll=COLUMN_UNROLL)
        more = (side == 0) & (flags[BUFFERS + number] != 0)

        @pl.when(more)
        def _():
            for cut, top, total in zip(cuts, tops, totals):
                top_ref[:, cut] = top
                total_ref[:, cut] = total

        @pl.when(jnp.logical_not(more))
        def _():
            slot = flags[2 * BUFFERS + number]
            for q, (top, total) in enumerate(zip(tops, totals)):
                greatest = jnp.max(top, axis=0, keepdims=True)
                total = jnp.sum(total * jnp.exp(top - greatest), axis=0, keepdims=True)
                out[slot, q : q + 1, :] = greatest + jnp.log(total)

    each_listed(flags, body)


WHOLE = pl.BlockSpec(memory_space=pltpu.VMEM)
SCALARS = pl.BlockSpec(memory_space=pltpu.SMEM)
PARAMS = pltpu.CompilerParams(vmem_limit_bytes=20 * 2**20)


def in_vmem(value):
    return pltpu.with_memory_space_constraint(value, pltpu.VMEM)


def in_hbm(value):
    return pltpu.with_memory_space_constraint(value, pltpu.HBM)


def call_message(scale, half_index, points, masses, initial, src):
    columns, depth = points.shape[0] // 2, points.shape[1]
    return pl.pallas_call(
        functools.partial(message_kernel, scale),
        out_shape=[
            pltpu.VMEM((columns + TAIL, depth), jnp.bfloat16),
            pltpu.VMEM(src.shape, jnp.bfloat16),
        ],
        in_specs=[SCALARS] + [pl.BlockSpec(memory_space=pltpu.HBM)] * 4,
        out_specs=[WHOLE] * 2,
        scratch_shapes=[
            pltpu.VMEM((columns, depth), jnp.bfloat16),
            pltpu.VMEM((2 * columns // 128, 128), jnp.float32),
            pltpu.VMEM((2 * columns // 128, 128), jnp.float32),
            pltpu.SemaphoreType.DMA((4,)),
        ],
        compiler_params=PARAMS,
        name="message",
    )(half_index.reshape(1), *map(in_hbm, (points, masses.reshape(-1, 128), initial.reshape(-1, 128), src)))


def call_first(numbers, first, last, flags, sources, targets, state):
    half, depth = sources[0].shape
    rows, columns, count = 2 * half, targets[0].shape[0] - TAIL, len(numbers)
    out_shape = [
        pltpu.VMEM((BUFFERS, rows, columns), jnp.float32),
        pltpu.VMEM((BUFFERS, columns // 128, 128), jnp.float32),
        pltpu.VMEM((rows, 128), jnp.float32),
        pltpu.VMEM((rows, 128), jnp.float32),
    ]
    if last:
        out_shape.append(jax.ShapeDtypeStruct((rows // 128, 128), jnp.float32))
    operands = [flags, *sources, *targets]
    aliases = {}
    if not first:
        aliases = {len(operands) + i: i for i in range(4)}
        operands += [in_vmem(value) for value in state]
    return pl.pallas_call(
        functools.partial(first_kernel, numbers, first, last),
        out_shape=out_shape,
        in_specs=[SCALARS] + [WHOLE] * (len(operands) - 1),
        out_specs=[WHOLE] * len(out_shape),
        scratch_shapes=[
            pltpu.VMEM((2, half, depth), jnp.bfloat16),
            pltpu.VMEM((count, columns, depth), jnp.bfloat16),
            pltpu.VMEM((count, columns // 128, 128), jnp.float32),
        ],
        input_output_aliases=aliases,
        compiler_params=PARAMS,
        cost_estimate=pl.CostEstimate(
            flops=2 * count * rows * columns * depth,
            bytes_accessed=count * rows * columns,
            transcendentals=count * rows * columns,
        ),
        name="first_rows",
    )(*operands)


def call_rows(flags, cross, masses, sums):
    rows = cross.shape[1]
    return pl.pallas_call(
        row_kernel,
        out_shape=jax.ShapeDtypeStruct((rows // 128, 128), jnp.float32),
        in_specs=[SCALARS] + [WHOLE] * 3,
        out_specs=WHOLE,
        scratch_shapes=[pltpu.VMEM((rows, 128), jnp.float32)] * 2,
        compiler_params=PARAMS,
        name="rows",
    )(flags, in_vmem(cross), in_vmem(masses), sums)


def call_columns(twice, flags, cross, weights):
    rows, columns = cross.shape[1:]
    return pl.pallas_call(
        functools.partial(column_kernel, twice),
        out_shape=jax.ShapeDtypeStruct((BUFFERS, columns // 128, 128), jnp.float32),
        in_specs=[SCALARS] + [WHOLE] * 2,
        out_specs=WHOLE,
        scratch_shapes=[pltpu.VMEM((rows, 128), jnp.float32)]
        + [pltpu.VMEM((8, columns), jnp.float32)] * 2,
        compiler_params=PARAMS,
        name="columns",
    )(flags, in_vmem(cross), weights)


def fill_rows(value, before, after):
    return jnp.pad(value, ((before, after), (0, 0), (0, 0)), constant_values=NEG_FILL)


def local(src_points, src_log_mass, tgt_points, tgt_log_mass, initial_potential, pair_list, pair_count):
    block = lax.axis_index("blk")
    rep = lax.axis_index("rep")
    blocks = lax.axis_size("blk")
    core = block % 2
    half_index = (rep % 2) ^ ((block // SEGMENT) % 2)
    rows = src_points.shape[0]
    width = tgt_points.shape[0]
    columns = width // 2

    mate = send(src_points, diagonal, blocks)
    message, own = call_message(
        1.0 / EPS_START, half_index, tgt_points, tgt_log_mass, initial_potential, src_points
    )

    before = send(message, along(2, blocks), blocks)
    after = send(message, along(-2, blocks), blocks)
    third = send(message, by_core(-3, 3, blocks), blocks)
    tied, mate = lax.optimization_barrier((message, mate))
    beside = send(tied, sibling, blocks)
    sources = [own, mate]
    groups = ((0, 1), (2, 3), (4, 5, 6), (7,))

    even_slots = (3, 4, 1, 5, 2, 6, 0, 7)
    odd_slots = (4, 3, 2, 6, 1, 5, 7, 0)
    slots = jnp.where(core == 0, jnp.array(even_slots, jnp.int32), jnp.array(odd_slots, jnp.int32))
    names = (block - core - 3 + slots) % blocks

    def kept(source_block):
        row_names = pair_list[source_block]
        in_use = jnp.arange(row_names.shape[0], dtype=jnp.int32) < pair_count[source_block]
        return jnp.any((row_names[None, :] == names[:, None]) & in_use[None, :], axis=1).astype(jnp.int32)

    kept_pairs = jnp.stack([kept(block), kept(block + 1 - 2 * core)])
    entries = jnp.arange(2 * BUFFERS, dtype=jnp.int32)
    listed = kept_pairs.T.reshape(-1)
    rank = jnp.sum(jnp.where(entries[None, :] < entries[:, None], listed[None, :], 0), axis=1)
    order = jnp.sum(
        jnp.where((rank[:, None] == entries[None, :]) & (listed[:, None] != 0), entries[:, None], 0), axis=0
    )
    total = jnp.broadcast_to(jnp.sum(listed), (BUFFERS,))
    flags = jnp.concatenate([kept_pairs.reshape(-1), slots, total, order])

    state = call_first(groups[0], True, False, flags, sources, [message, beside], ())
    state, near = lax.optimization_barrier((state, [before, after]))
    near_beside = [send(value, sibling, blocks) for value in near]
    state = call_first(groups[1], False, False, flags, sources, near, state)
    state, third = lax.optimization_barrier((state, third))
    third_beside = send(third, sibling, blocks)
    state = call_first(groups[2], False, False, flags, sources, [*near_beside, third], state)
    *state, last = call_first(groups[3], False, True, flags, sources, [third_beside], state)
    cross, window_masses = state[:2]
    part = last.reshape(-1)

    for sweep in range(ITERS):
        epsilon = EPS_START * 0.5**sweep
        if sweep == 0:
            got = send(jnp.concatenate([part, src_log_mass]), diagonal, blocks)
            both_masses = jnp.concatenate([src_log_mass, got[2 * rows :]])
        else:
            part = call_rows(flags, cross, window_masses, column_sums).reshape(-1)
            got = send(part, diagonal, blocks)
        row_sums = log_merge(part, jnp.concatenate([got[rows : 2 * rows], got[:rows]]))
        weighted = (both_masses - row_sums).reshape(2 * rows // 128, 128)
        part = call_columns(sweep > 0, flags, cross, weighted)
        chip = log_merge(
            part,
            send(part, sibling, blocks),
            send(part, lambda b, r: (b, r ^ 2), blocks),
            send(part, lambda b, r: (b ^ 1, r ^ 2), blocks),
        )
        forward = core == 0
        if sweep + 1 < ITERS:
            got = []
            for n in (1, 2, 3):
                kept_rows = 8 - 2 * n
                out = jnp.where(forward, chip[2 * n :], chip[:kept_rows])
                out = send(out, by_core(2 * n, -2 * n, blocks), blocks)
                got.append(
                    jnp.where(forward, fill_rows(out, 0, 2 * n), fill_rows(out, 2 * n, 0))
                )
            side = log_merge(*got)
            column_sums = log_merge(chip, side, send(side, sibling, blocks))
        else:
            near = jnp.where(forward, chip[5:7], chip[1:3])
            near = send(near, by_core(2, -2, blocks), blocks)
            far = jnp.where(forward, chip[7], chip[0])
            far = send(far, by_core(4, -4, blocks), blocks)
            empty = jnp.full_like(far, NEG_FILL)
            far = jnp.where(forward, jnp.stack([far, empty]), jnp.stack([empty, far]))
            side = log_merge(near, far)
            column_sums = log_merge(chip[3:5], side, send(side, sibling, blocks))
            mine = jnp.where(core == 0, column_sums[0], column_sums[1]).reshape(columns)
            other = send(mine, lambda b, r: (b, r ^ 1), blocks)
            whole = jnp.where(
                half_index == 0, jnp.concatenate([mine, other]), jnp.concatenate([other, mine])
            )
            source_pot = half_norms(src_points) - epsilon * row_sums[:rows]
            target_pot = half_norms(tgt_points) - epsilon * whole
    return source_pot, target_pot


def solution(mesh):
    in_specs = (
        P(("blk", "rep"), None),
        P(("blk", "rep")),
        P("blk", None),
        P("blk"),
        P("blk"),
        P(),
        P(),
    )
    out_specs = (P(("blk", "rep")), P("blk"))
    return jax.shard_map(local, mesh=mesh, in_specs=in_specs, out_specs=out_specs, check_vma=False)
```

```python
import functools

import jax
import jax.numpy as jnp
from jax import lax
from jax.experimental import pallas as pl
from jax.experimental.pallas import tpu as pltpu
from jax.sharding import PartitionSpec as P

ITERS = 2
EPS_START = 0.5
NEG_FILL = -1e30
ROW_UNROLL = 8
COLUMN_UNROLL = 4
BUFFERS = 8
REPS = 4
SEGMENT = 8
TAIL = 16


def send(value, place, blocks):
    pairs = []
    for block in range(blocks):
        for rep in range(REPS):
            to_block, to_rep = place(block, rep)
            pairs.append((block * REPS + rep, to_block % blocks * REPS + to_rep))
    return lax.ppermute(value, ("blk", "rep"), pairs)


def along(steps, blocks):
    def place(block, rep):
        target = (block + steps) % blocks
        return target, rep if (target // SEGMENT - block // SEGMENT) % 2 == 0 else REPS - 1 - rep

    return place


def by_core(even_steps, odd_steps, blocks):
    even, odd = along(even_steps, blocks), along(odd_steps, blocks)
    return lambda block, rep: even(block, rep) if block % 2 == 0 else odd(block, rep)


def sibling(block, rep):
    return block ^ 1, rep


def diagonal(block, rep):
    return block ^ 1, rep ^ 1


def half_norms(points):
    widened = points.astype(jnp.float32)
    return 0.5 * jnp.sum(widened * widened, axis=1)


def terms(vector):
    parts = []
    for _ in range(3):
        parts.append(vector.astype(jnp.bfloat16).astype(jnp.float32))
        vector = vector - parts[-1]
    return parts


def log_merge(*parts):
    top = functools.reduce(jnp.maximum, parts)
    return top + jnp.log(sum(jnp.exp(part - top) for part in parts))


def spread_rows(vector_ref, bias_ref):
    for q in range(bias_ref.shape[0] // 128):
        row = vector_ref[q : q + 1, :]
        bias_ref[q * 128 : (q + 1) * 128, :] = jnp.broadcast_to(row, (128, 128)).T


def fold(value, combine):
    rows = value.shape[0]
    while rows > 8:
        rows //= 2
        value = combine(value[:rows], value[rows:])
    return value


def row_update(cross_ref, index, bias, twice, side, half, top_ref, total_ref):
    step = 64

    def chunk(r, _):
        at = pl.ds(pl.multiple_of(side * half + r * step, step), step)
        scores = []
        for q, term in enumerate(bias):
            part = cross_ref[index, at, q * 128 : (q + 1) * 128]
            scores.append((part + part if twice else part) + term)
        old = top_ref[at, :]
        top = jnp.maximum(old, functools.reduce(jnp.maximum, scores))
        total = functools.reduce(jnp.add, [jnp.exp(part - top) for part in scores])
        total_ref[at, :] = total_ref[at, :] * jnp.exp(old - top) + total
        top_ref[at, :] = top
        return 0

    lax.fori_loop(0, half // step, chunk, 0, unroll=ROW_UNROLL)


def row_finish(top_ref, total_ref, out):
    for q in range(out.shape[0]):
        top = top_ref[q * 128 : (q + 1) * 128, :].T
        greatest = jnp.max(top, axis=0, keepdims=True)
        total = total_ref[q * 128 : (q + 1) * 128, :].T * jnp.exp(top - greatest)
        out[q : q + 1, :] = greatest + jnp.log(jnp.sum(total, axis=0, keepdims=True))


def each_listed(flags, body):
    def unit(u, _):
        entry = flags[4 * BUFFERS + u]
        body(lax.div(entry, 2), lax.rem(entry, 2))
        return 0

    lax.fori_loop(0, flags[3 * BUFFERS], unit, 0)


def each_kept(flags, first, count, body):
    def unit(u, _):
        number, side = first + lax.div(u, 2), lax.rem(u, 2)

        @pl.when(flags[side * BUFFERS + number] != 0)
        def _():
            body(number, side)

        return 0

    lax.fori_loop(0, 2 * count, unit, 0)


def message_kernel(scale, half, points, masses, initial, src, out, src_out, block_ref, mass_ref, initial_ref, sems):
    columns, depth = block_ref.shape
    src_copy = pltpu.make_async_copy(src, src_out, sems.at[1])
    copy = pltpu.make_async_copy(
        points.at[pl.ds(pl.multiple_of(half[0] * columns, columns), columns), :], block_ref, sems.at[0]
    )
    small = [
        pltpu.make_async_copy(masses, mass_ref, sems.at[2]),
        pltpu.make_async_copy(initial, initial_ref, sems.at[3]),
    ]
    for start in (copy, *small, src_copy):
        start.start()
    copy.wait()
    value = block_ref[...].astype(jnp.float32)
    out[:columns, :] = (value * scale).astype(jnp.bfloat16)
    squares = value * value
    high = squares.astype(jnp.bfloat16)
    low = (squares - high.astype(jnp.float32)).astype(jnp.bfloat16)
    ones = jnp.ones((8, depth), jnp.bfloat16)
    norms = sum(
        lax.dot_general(ones, part, (((1,), (1,)), ((), ())), preferred_element_type=jnp.float32)
        for part in (high, low)
    )
    count = columns // 128
    norms = jnp.concatenate([norms[0:1, q * 128 : (q + 1) * 128] for q in range(count)], axis=0)

    def pick(ref):
        return jnp.where(half[0] == 0, ref[:count, :], ref[count:, :])

    for copy in small:
        copy.wait()
    mass = pick(mass_ref)
    bias = mass + (pick(initial_ref) - 0.5 * norms) * scale
    rows = [jnp.concatenate(pair, axis=1) for pair in zip(terms(bias), terms(mass))]
    rows.append(jnp.zeros((TAIL - 3 * count, 256), jnp.float32))
    out[columns:, :] = jnp.concatenate(rows, axis=0).astype(jnp.bfloat16)
    src_copy.wait()


def first_kernel(numbers, first, last, flags, *refs):
    sources, targets = refs[:2], refs[2 : 2 + len(numbers)]
    refs = refs[2 + len(numbers) :]
    if not first:
        refs = refs[4:]
    cross, masses, top_ref, total_ref = refs[:4]
    src_ref, tgt_ref, bias_ref = refs[-3:]
    if first:
        top_ref[...] = jnp.full(top_ref.shape, NEG_FILL, jnp.float32)
        total_ref[...] = jnp.zeros(total_ref.shape, jnp.float32)
    half = sources[0].shape[0]
    width = cross.shape[2]
    for side, src in enumerate(sources):
        src_ref[side] = src[...]
    for k, number in enumerate(numbers):
        tgt_ref[k] = targets[k][:width, :]
        tail = targets[k][width:, :].astype(jnp.float32)
        count = width // 128
        vectors = tail[:count] + tail[count : 2 * count] + tail[2 * count : 3 * count]
        bias_ref[k] = vectors[:, :128]
        masses[number] = vectors[:, 128:]

    def body(number, side):
        k = number - numbers[0]
        for c in range(0, width, 256):
            for r in range(0, half, 256):
                at = pl.ds(pl.multiple_of(side * half + r, 256), 256)
                cross[number, at, c : c + 256] = lax.dot_general(
                    src_ref[side, r : r + 256, :],
                    tgt_ref[k, c : c + 256, :],
                    (((1,), (1,)), ((), ())),
                    preferred_element_type=jnp.float32,
                )
        bias = [bias_ref[k, q : q + 1, :] for q in range(width // 128)]
        row_update(cross, number, bias, False, side, half, top_ref, total_ref)

    each_kept(flags, numbers[0], len(numbers), body)
    if last:
        row_finish(top_ref, total_ref, refs[4])


def row_kernel(flags, cross, masses, sums, out, top_ref, total_ref):
    top_ref[...] = jnp.full(top_ref.shape, NEG_FILL, jnp.float32)
    total_ref[...] = jnp.zeros(total_ref.shape, jnp.float32)
    half = top_ref.shape[0] // 2

    def body(number, side):
        slot = flags[2 * BUFFERS + number]
        bias = [
            masses[number, q : q + 1, :] - 2.0 * sums[slot, q : q + 1, :] for q in range(masses.shape[1])
        ]
        row_update(cross, number, bias, True, side, half, top_ref, total_ref)

    each_listed(flags, body)
    row_finish(top_ref, total_ref, out)


def column_kernel(twice, flags, cross, weights, out, bias, top_ref, total_ref):
    out[...] = jnp.full(out.shape, NEG_FILL, jnp.float32)
    spread_rows(weights, bias)
    half = bias.shape[0] // 2
    pieces = cross.shape[2] // 128
    step = 128

    def body(number, side):
        def chunk(r, state):
            at = pl.ds(pl.multiple_of(side * half + r * step, step), step)
            weight = bias[at, :]
            tops, totals = [], []
            for q in range(pieces):
                part = cross[number, at, q * 128 : (q + 1) * 128]
                scores = (part + part if twice else part) + weight
                top = jnp.maximum(state[0][q], fold(scores, jnp.maximum))
                total = jnp.sum(jnp.exp(scores.reshape(-1, 8, 128) - top[None]), axis=0)
                totals.append(state[1][q] * jnp.exp(state[0][q] - top) + total)
                tops.append(top)
            return tuple(tops), tuple(totals)

        going = (side == 1) & (flags[number] != 0)
        cuts = [slice(q * 128, (q + 1) * 128) for q in range(pieces)]
        state = (
            tuple(jnp.where(going, top_ref[:, cut], NEG_FILL) for cut in cuts),
            tuple(jnp.where(going, total_ref[:, cut], 0.0) for cut in cuts),
        )
        tops, totals = lax.fori_loop(0, half // step, chunk, state, unroll=COLUMN_UNROLL)
        more = (side == 0) & (flags[BUFFERS + number] != 0)

        @pl.when(more)
        def _():
            for cut, top, total in zip(cuts, tops, totals):
                top_ref[:, cut] = top
                total_ref[:, cut] = total

        @pl.when(jnp.logical_not(more))
        def _():
            slot = flags[2 * BUFFERS + number]
            for q, (top, total) in enumerate(zip(tops, totals)):
                greatest = jnp.max(top, axis=0, keepdims=True)
                total = jnp.sum(total * jnp.exp(top - greatest), axis=0, keepdims=True)
                out[slot, q : q + 1, :] = greatest + jnp.log(total)

    each_listed(flags, body)


WHOLE = pl.BlockSpec(memory_space=pltpu.VMEM)
SCALARS = pl.BlockSpec(memory_space=pltpu.SMEM)
PARAMS = pltpu.CompilerParams(vmem_limit_bytes=20 * 2**20)


def in_vmem(value):
    return pltpu.with_memory_space_constraint(value, pltpu.VMEM)


def in_hbm(value):
    return pltpu.with_memory_space_constraint(value, pltpu.HBM)


def call_message(scale, half_index, points, masses, initial, src):
    columns, depth = points.shape[0] // 2, points.shape[1]
    return pl.pallas_call(
        functools.partial(message_kernel, scale),
        out_shape=[
            pltpu.VMEM((columns + TAIL, depth), jnp.bfloat16),
            pltpu.VMEM(src.shape, jnp.bfloat16),
        ],
        in_specs=[SCALARS] + [pl.BlockSpec(memory_space=pltpu.HBM)] * 4,
        out_specs=[WHOLE] * 2,
        scratch_shapes=[
            pltpu.VMEM((columns, depth), jnp.bfloat16),
            pltpu.VMEM((2 * columns // 128, 128), jnp.float32),
            pltpu.VMEM((2 * columns // 128, 128), jnp.float32),
            pltpu.SemaphoreType.DMA((4,)),
        ],
        compiler_params=PARAMS,
        name="message",
    )(half_index.reshape(1), *map(in_hbm, (points, masses.reshape(-1, 128), initial.reshape(-1, 128), src)))


def call_first(numbers, first, last, flags, sources, targets, state):
    half, depth = sources[0].shape
    rows, columns, count = 2 * half, targets[0].shape[0] - TAIL, len(numbers)
    out_shape = [
        pltpu.VMEM((BUFFERS, rows, columns), jnp.float32),
        pltpu.VMEM((BUFFERS, columns // 128, 128), jnp.float32),
        pltpu.VMEM((rows, 128), jnp.float32),
        pltpu.VMEM((rows, 128), jnp.float32),
    ]
    if last:
        out_shape.append(jax.ShapeDtypeStruct((rows // 128, 128), jnp.float32))
    operands = [flags, *sources, *targets]
    aliases = {}
    if not first:
        aliases = {len(operands) + i: i for i in range(4)}
        operands += [in_vmem(value) for value in state]
    return pl.pallas_call(
        functools.partial(first_kernel, numbers, first, last),
        out_shape=out_shape,
        in_specs=[SCALARS] + [WHOLE] * (len(operands) - 1),
        out_specs=[WHOLE] * len(out_shape),
        scratch_shapes=[
            pltpu.VMEM((2, half, depth), jnp.bfloat16),
            pltpu.VMEM((count, columns, depth), jnp.bfloat16),
            pltpu.VMEM((count, columns // 128, 128), jnp.float32),
        ],
        input_output_aliases=aliases,
        compiler_params=PARAMS,
        cost_estimate=pl.CostEstimate(
            flops=2 * count * rows * columns * depth,
            bytes_accessed=count * rows * columns,
            transcendentals=count * rows * columns,
        ),
        name="first_rows",
    )(*operands)


def call_rows(flags, cross, masses, sums):
    rows = cross.shape[1]
    return pl.pallas_call(
        row_kernel,
        out_shape=jax.ShapeDtypeStruct((rows // 128, 128), jnp.float32),
        in_specs=[SCALARS] + [WHOLE] * 3,
        out_specs=WHOLE,
        scratch_shapes=[pltpu.VMEM((rows, 128), jnp.float32)] * 2,
        compiler_params=PARAMS,
        name="rows",
    )(flags, in_vmem(cross), in_vmem(masses), sums)


def call_columns(twice, flags, cross, weights):
    rows, columns = cross.shape[1:]
    return pl.pallas_call(
        functools.partial(column_kernel, twice),
        out_shape=jax.ShapeDtypeStruct((BUFFERS, columns // 128, 128), jnp.float32),
        in_specs=[SCALARS] + [WHOLE] * 2,
        out_specs=WHOLE,
        scratch_shapes=[pltpu.VMEM((rows, 128), jnp.float32)]
        + [pltpu.VMEM((8, columns), jnp.float32)] * 2,
        compiler_params=PARAMS,
        name="columns",
    )(flags, in_vmem(cross), weights)


def fill_rows(value, before, after):
    return jnp.pad(value, ((before, after), (0, 0), (0, 0)), constant_values=NEG_FILL)


def local(src_points, src_log_mass, tgt_points, tgt_log_mass, initial_potential, pair_list, pair_count):
    block = lax.axis_index("blk")
    rep = lax.axis_index("rep")
    blocks = lax.axis_size("blk")
    core = block % 2
    half_index = (rep % 2) ^ ((block // SEGMENT) % 2)
    rows = src_points.shape[0]
    width = tgt_points.shape[0]
    columns = width // 2

    mate = send(src_points, diagonal, blocks)
    message, own = call_message(
        1.0 / EPS_START, half_index, tgt_points, tgt_log_mass, initial_potential, src_points
    )

    before = send(message, along(2, blocks), blocks)
    after = send(message, along(-2, blocks), blocks)
    third = send(message, by_core(-3, 3, blocks), blocks)
    tied, mate = lax.optimization_barrier((message, mate))
    beside = send(tied, sibling, blocks)
    sources = [own, mate]
    groups = ((0, 1), (2, 3), (4, 5, 6), (7,))

    even_slots = (3, 4, 1, 5, 2, 6, 0, 7)
    odd_slots = (4, 3, 2, 6, 1, 5, 7, 0)
    slots = jnp.where(core == 0, jnp.array(even_slots, jnp.int32), jnp.array(odd_slots, jnp.int32))
    names = (block - core - 3 + slots) % blocks

    def kept(source_block):
        row_names = pair_list[source_block]
        in_use = jnp.arange(row_names.shape[0], dtype=jnp.int32) < pair_count[source_block]
        return jnp.any((row_names[None, :] == names[:, None]) & in_use[None, :], axis=1).astype(jnp.int32)

    kept_pairs = jnp.stack([kept(block), kept(block + 1 - 2 * core)])
    entries = jnp.arange(2 * BUFFERS, dtype=jnp.int32)
    listed = kept_pairs.T.reshape(-1)
    rank = jnp.sum(jnp.where(entries[None, :] < entries[:, None], listed[None, :], 0), axis=1)
    order = jnp.sum(
        jnp.where((rank[:, None] == entries[None, :]) & (listed[:, None] != 0), entries[:, None], 0), axis=0
    )
    total = jnp.broadcast_to(jnp.sum(listed), (BUFFERS,))
    flags = jnp.concatenate([kept_pairs.reshape(-1), slots, total, order])

    state = call_first(groups[0], True, False, flags, sources, [message, beside], ())
    state, near = lax.optimization_barrier((state, [before, after]))
    near_beside = [send(value, sibling, blocks) for value in near]
    state = call_first(groups[1], False, False, flags, sources, near, state)
    state, third = lax.optimization_barrier((state, third))
    third_beside = send(third, sibling, blocks)
    state = call_first(groups[2], False, False, flags, sources, [*near_beside, third], state)
    *state, last = call_first(groups[3], False, True, flags, sources, [third_beside], state)
    cross, window_masses = state[:2]
    part = last.reshape(-1)

    for sweep in range(ITERS):
        epsilon = EPS_START * 0.5**sweep
        if sweep == 0:
            got = send(jnp.concatenate([part, src_log_mass]), diagonal, blocks)
            both_masses = jnp.concatenate([src_log_mass, got[2 * rows :]])
        else:
            part = call_rows(flags, cross, window_masses, column_sums).reshape(-1)
            got = send(part, diagonal, blocks)
        row_sums = log_merge(part, jnp.concatenate([got[rows : 2 * rows], got[:rows]]))
        weighted = (both_masses - row_sums).reshape(2 * rows // 128, 128)
        part = call_columns(sweep > 0, flags, cross, weighted)
        chip = log_merge(
            part,
            send(part, sibling, blocks),
            send(part, lambda b, r: (b, r ^ 2), blocks),
            send(part, lambda b, r: (b ^ 1, r ^ 2), blocks),
        )
        forward = core == 0
        if sweep + 1 < ITERS:
            got = []
            for n in (1, 2, 3):
                kept_rows = 8 - 2 * n
                out = jnp.where(forward, chip[2 * n :], chip[:kept_rows])
                out = send(out, by_core(2 * n, -2 * n, blocks), blocks)
                got.append(
                    jnp.where(forward, fill_rows(out, 0, 2 * n), fill_rows(out, 2 * n, 0))
                )
            side = log_merge(*got)
            column_sums = log_merge(chip, side, send(side, sibling, blocks))
        else:
            near = jnp.where(forward, chip[5:7], chip[1:3])
            near = send(near, by_core(2, -2, blocks), blocks)
            far = jnp.where(forward, chip[7], chip[0])
            far = send(far, by_core(4, -4, blocks), blocks)
            empty = jnp.full_like(far, NEG_FILL)
            far = jnp.where(forward, jnp.stack([far, empty]), jnp.stack([empty, far]))
            side = log_merge(jnp.where(forward, chip[3:5], jnp.full_like(near, NEG_FILL)), near, far)
            over_core = send(side, sibling, blocks)
            over_half = send(side, lambda b, r: (b, r ^ 1), blocks)
            over_both = send(side, diagonal, blocks)
            mine = log_merge(side, over_core)
            other = log_merge(over_half, over_both)
            mine = jnp.where(core == 0, mine[0], mine[1]).reshape(columns)
            other = jnp.where(core == 0, other[0], other[1]).reshape(columns)
            whole = jnp.where(
                half_index == 0, jnp.concatenate([mine, other]), jnp.concatenate([other, mine])
            )
            source_pot = half_norms(src_points) - epsilon * row_sums[:rows]
            target_pot = half_norms(tgt_points) - epsilon * whole
    return source_pot, target_pot


def solution(mesh):
    in_specs = (
        P(("blk", "rep"), None),
        P(("blk", "rep")),
        P("blk", None),
        P("blk"),
        P("blk"),
        P(),
        P(),
    )
    out_specs = (P(("blk", "rep")), P("blk"))
    return jax.shard_map(local, mesh=mesh, in_specs=in_specs, out_specs=out_specs, check_vma=False)
```

```python
import functools

import jax
import jax.numpy as jnp
from jax import lax
from jax.experimental import pallas as pl
from jax.experimental.pallas import tpu as pltpu
from jax.sharding import PartitionSpec as P

ITERS = 2
EPS_START = 0.5
NEG_FILL = -1e30
ROW_UNROLL = 8
COLUMN_UNROLL = 4
BUFFERS = 8
REPS = 4
SEGMENT = 8
TAIL = 16


def send(value, place, blocks):
    pairs = []
    for block in range(blocks):
        for rep in range(REPS):
            to_block, to_rep = place(block, rep)
            pairs.append((block * REPS + rep, to_block % blocks * REPS + to_rep))
    return lax.ppermute(value, ("blk", "rep"), pairs)


def along(steps, blocks):
    def place(block, rep):
        target = (block + steps) % blocks
        return target, rep if (target // SEGMENT - block // SEGMENT) % 2 == 0 else REPS - 1 - rep

    return place


def by_core(even_steps, odd_steps, blocks):
    even, odd = along(even_steps, blocks), along(odd_steps, blocks)
    return lambda block, rep: even(block, rep) if block % 2 == 0 else odd(block, rep)


def sibling(block, rep):
    return block ^ 1, rep


def diagonal(block, rep):
    return block ^ 1, rep ^ 1


def half_norms(points):
    widened = points.astype(jnp.float32)
    return 0.5 * jnp.sum(widened * widened, axis=1)


def terms(vector):
    parts = []
    for _ in range(3):
        parts.append(vector.astype(jnp.bfloat16).astype(jnp.float32))
        vector = vector - parts[-1]
    return parts


def log_merge(*parts):
    top = functools.reduce(jnp.maximum, parts)
    return top + jnp.log(sum(jnp.exp(part - top) for part in parts))


def spread_rows(vector_ref, bias_ref):
    for q in range(bias_ref.shape[0] // 128):
        row = vector_ref[q : q + 1, :]
        bias_ref[q * 128 : (q + 1) * 128, :] = jnp.broadcast_to(row, (128, 128)).T


def fold(value, combine):
    rows = value.shape[0]
    while rows > 8:
        rows //= 2
        value = combine(value[:rows], value[rows:])
    return value


def row_update(cross_ref, index, bias, twice, side, half, top_ref, total_ref):
    step = 64

    def chunk(r, _):
        at = pl.ds(pl.multiple_of(side * half + r * step, step), step)
        scores = []
        for q, term in enumerate(bias):
            part = cross_ref[index, at, q * 128 : (q + 1) * 128]
            scores.append((part + part if twice else part) + term)
        old = top_ref[at, :]
        top = jnp.maximum(old, functools.reduce(jnp.maximum, scores))
        total = functools.reduce(jnp.add, [jnp.exp(part - top) for part in scores])
        total_ref[at, :] = total_ref[at, :] * jnp.exp(old - top) + total
        top_ref[at, :] = top
        return 0

    lax.fori_loop(0, half // step, chunk, 0, unroll=ROW_UNROLL)


def row_finish(top_ref, total_ref, out):
    for q in range(out.shape[0]):
        top = top_ref[q * 128 : (q + 1) * 128, :].T
        greatest = jnp.max(top, axis=0, keepdims=True)
        total = total_ref[q * 128 : (q + 1) * 128, :].T * jnp.exp(top - greatest)
        out[q : q + 1, :] = greatest + jnp.log(jnp.sum(total, axis=0, keepdims=True))


def each_listed(flags, body):
    def unit(u, _):
        entry = flags[4 * BUFFERS + u]
        body(lax.div(entry, 2), lax.rem(entry, 2))
        return 0

    lax.fori_loop(0, flags[3 * BUFFERS], unit, 0)


def each_kept(flags, first, count, body):
    def unit(u, _):
        number, side = first + lax.div(u, 2), lax.rem(u, 2)

        @pl.when(flags[side * BUFFERS + number] != 0)
        def _():
            body(number, side)

        return 0

    lax.fori_loop(0, 2 * count, unit, 0)


def list_kept(blocks, slots, block, core, pair_list, pair_count, flags):
    sources = (block, block + 1 - 2 * core)
    entries = pair_list.shape[0]
    lists = [[pair_list[j, source] for j in range(entries)] for source in sources]
    counts = [pair_count[source] for source in sources]
    total = jnp.int32(0)
    for u in range(2 * BUFFERS):
        flags[4 * BUFFERS + u] = jnp.int32(0)
    for number in range(BUFFERS):
        slot = jnp.where(core == 0, jnp.int32(slots[0][number]), jnp.int32(slots[1][number]))
        name = lax.rem(block - core - 3 + slot + blocks, jnp.int32(blocks))
        flags[2 * BUFFERS + number] = slot
        for side in range(2):
            kept = jnp.int32(0)
            for j in range(entries):
                same = (lists[side][j] == name) & (j < counts[side])
                kept = jnp.where(same, jnp.int32(1), kept)
            flags[side * BUFFERS + number] = kept
            flags[4 * BUFFERS + total] = jnp.int32(2 * number + side)
            total = total + kept
    for number in range(BUFFERS):
        flags[3 * BUFFERS + number] = total


def message_kernel(
    scale,
    blocks,
    slots,
    half,
    points,
    masses,
    initial,
    src,
    pair_list,
    pair_count,
    out,
    src_out,
    flags,
    block_ref,
    mass_ref,
    initial_ref,
    list_ref,
    count_ref,
    sems,
):
    columns, depth = block_ref.shape
    src_copy = pltpu.make_async_copy(src, src_out, sems.at[1])
    copy = pltpu.make_async_copy(
        points.at[pl.ds(pl.multiple_of(half[0] * columns, columns), columns), :], block_ref, sems.at[0]
    )
    small = [
        pltpu.make_async_copy(masses, mass_ref, sems.at[2]),
        pltpu.make_async_copy(initial, initial_ref, sems.at[3]),
    ]
    pairs = [
        pltpu.make_async_copy(pair_list, list_ref, sems.at[4]),
        pltpu.make_async_copy(pair_count, count_ref, sems.at[5]),
    ]
    for start in (copy, *pairs, *small, src_copy):
        start.start()
    for pair in pairs:
        pair.wait()
    list_kept(blocks, slots, half[1], half[2], list_ref, count_ref, flags)
    copy.wait()
    value = block_ref[...].astype(jnp.float32)
    out[:columns, :] = (value * scale).astype(jnp.bfloat16)
    squares = value * value
    high = squares.astype(jnp.bfloat16)
    low = (squares - high.astype(jnp.float32)).astype(jnp.bfloat16)
    ones = jnp.ones((8, depth), jnp.bfloat16)
    norms = sum(
        lax.dot_general(ones, part, (((1,), (1,)), ((), ())), preferred_element_type=jnp.float32)
        for part in (high, low)
    )
    count = columns // 128
    norms = jnp.concatenate([norms[0:1, q * 128 : (q + 1) * 128] for q in range(count)], axis=0)

    def pick(ref):
        return jnp.where(half[0] == 0, ref[:count, :], ref[count:, :])

    for copy in small:
        copy.wait()
    mass = pick(mass_ref)
    bias = mass + (pick(initial_ref) - 0.5 * norms) * scale
    rows = [jnp.concatenate(pair, axis=1) for pair in zip(terms(bias), terms(mass))]
    rows.append(jnp.zeros((TAIL - 3 * count, 256), jnp.float32))
    out[columns:, :] = jnp.concatenate(rows, axis=0).astype(jnp.bfloat16)
    src_copy.wait()


def first_kernel(numbers, first, last, flags, *refs):
    sources, targets = refs[:2], refs[2 : 2 + len(numbers)]
    refs = refs[2 + len(numbers) :]
    if not first:
        refs = refs[4:]
    cross, masses, top_ref, total_ref = refs[:4]
    src_ref, tgt_ref, bias_ref = refs[-3:]
    if first:
        top_ref[...] = jnp.full(top_ref.shape, NEG_FILL, jnp.float32)
        total_ref[...] = jnp.zeros(total_ref.shape, jnp.float32)
    half = sources[0].shape[0]
    width = cross.shape[2]
    for side, src in enumerate(sources):
        src_ref[side] = src[...]
    for k, number in enumerate(numbers):
        tgt_ref[k] = targets[k][:width, :]
        tail = targets[k][width:, :].astype(jnp.float32)
        count = width // 128
        vectors = tail[:count] + tail[count : 2 * count] + tail[2 * count : 3 * count]
        bias_ref[k] = vectors[:, :128]
        masses[number] = vectors[:, 128:]

    def body(number, side):
        k = number - numbers[0]
        for c in range(0, width, 256):
            for r in range(0, half, 256):
                at = pl.ds(pl.multiple_of(side * half + r, 256), 256)
                cross[number, at, c : c + 256] = lax.dot_general(
                    src_ref[side, r : r + 256, :],
                    tgt_ref[k, c : c + 256, :],
                    (((1,), (1,)), ((), ())),
                    preferred_element_type=jnp.float32,
                )
        bias = [bias_ref[k, q : q + 1, :] for q in range(width // 128)]
        row_update(cross, number, bias, False, side, half, top_ref, total_ref)

    each_kept(flags, numbers[0], len(numbers), body)
    if last:
        row_finish(top_ref, total_ref, refs[4])


def row_kernel(flags, cross, masses, sums, out, top_ref, total_ref):
    top_ref[...] = jnp.full(top_ref.shape, NEG_FILL, jnp.float32)
    total_ref[...] = jnp.zeros(total_ref.shape, jnp.float32)
    half = top_ref.shape[0] // 2

    def body(number, side):
        slot = flags[2 * BUFFERS + number]
        bias = [
            masses[number, q : q + 1, :] - 2.0 * sums[slot, q : q + 1, :] for q in range(masses.shape[1])
        ]
        row_update(cross, number, bias, True, side, half, top_ref, total_ref)

    each_listed(flags, body)
    row_finish(top_ref, total_ref, out)


def column_kernel(twice, flags, cross, weights, out, bias, top_ref, total_ref):
    out[...] = jnp.full(out.shape, NEG_FILL, jnp.float32)
    spread_rows(weights, bias)
    half = bias.shape[0] // 2
    pieces = cross.shape[2] // 128
    step = 128

    def body(number, side):
        def chunk(r, state):
            at = pl.ds(pl.multiple_of(side * half + r * step, step), step)
            weight = bias[at, :]
            tops, totals = [], []
            for q in range(pieces):
                part = cross[number, at, q * 128 : (q + 1) * 128]
                scores = (part + part if twice else part) + weight
                top = jnp.maximum(state[0][q], fold(scores, jnp.maximum))
                total = jnp.sum(jnp.exp(scores.reshape(-1, 8, 128) - top[None]), axis=0)
                totals.append(state[1][q] * jnp.exp(state[0][q] - top) + total)
                tops.append(top)
            return tuple(tops), tuple(totals)

        going = (side == 1) & (flags[number] != 0)
        cuts = [slice(q * 128, (q + 1) * 128) for q in range(pieces)]
        state = (
            tuple(jnp.where(going, top_ref[:, cut], NEG_FILL) for cut in cuts),
            tuple(jnp.where(going, total_ref[:, cut], 0.0) for cut in cuts),
        )
        tops, totals = lax.fori_loop(0, half // step, chunk, state, unroll=COLUMN_UNROLL)
        more = (side == 0) & (flags[BUFFERS + number] != 0)

        @pl.when(more)
        def _():
            for cut, top, total in zip(cuts, tops, totals):
                top_ref[:, cut] = top
                total_ref[:, cut] = total

        @pl.when(jnp.logical_not(more))
        def _():
            slot = flags[2 * BUFFERS + number]
            for q, (top, total) in enumerate(zip(tops, totals)):
                greatest = jnp.max(top, axis=0, keepdims=True)
                total = jnp.sum(total * jnp.exp(top - greatest), axis=0, keepdims=True)
                out[slot, q : q + 1, :] = greatest + jnp.log(total)

    each_listed(flags, body)


WHOLE = pl.BlockSpec(memory_space=pltpu.VMEM)
SCALARS = pl.BlockSpec(memory_space=pltpu.SMEM)
PARAMS = pltpu.CompilerParams(vmem_limit_bytes=20 * 2**20)


def in_vmem(value):
    return pltpu.with_memory_space_constraint(value, pltpu.VMEM)


def in_hbm(value):
    return pltpu.with_memory_space_constraint(value, pltpu.HBM)


def call_message(scale, blocks, slots, half, points, masses, initial, src, pair_list, pair_count):
    columns, depth = points.shape[0] // 2, points.shape[1]
    return pl.pallas_call(
        functools.partial(message_kernel, scale, blocks, slots),
        out_shape=[
            pltpu.VMEM((columns + TAIL, depth), jnp.bfloat16),
            pltpu.VMEM(src.shape, jnp.bfloat16),
            jax.ShapeDtypeStruct((6 * BUFFERS,), jnp.int32),
        ],
        in_specs=[SCALARS] + [pl.BlockSpec(memory_space=pltpu.HBM)] * 6,
        out_specs=[WHOLE] * 2 + [SCALARS],
        scratch_shapes=[
            pltpu.VMEM((columns, depth), jnp.bfloat16),
            pltpu.VMEM((2 * columns // 128, 128), jnp.float32),
            pltpu.VMEM((2 * columns // 128, 128), jnp.float32),
            pltpu.SMEM(pair_list.shape[::-1], jnp.int32),
            pltpu.SMEM(pair_count.shape, jnp.int32),
            pltpu.SemaphoreType.DMA((6,)),
        ],
        compiler_params=PARAMS,
        name="message",
    )(
        half,
        *map(in_hbm, (points, masses.reshape(-1, 128), initial.reshape(-1, 128), src, pair_list.T, pair_count)),
    )


def call_first(numbers, first, last, flags, sources, targets, state):
    half, depth = sources[0].shape
    rows, columns, count = 2 * half, targets[0].shape[0] - TAIL, len(numbers)
    out_shape = [
        pltpu.VMEM((BUFFERS, rows, columns), jnp.float32),
        pltpu.VMEM((BUFFERS, columns // 128, 128), jnp.float32),
        pltpu.VMEM((rows, 128), jnp.float32),
        pltpu.VMEM((rows, 128), jnp.float32),
    ]
    if last:
        out_shape.append(jax.ShapeDtypeStruct((rows // 128, 128), jnp.float32))
    operands = [flags, *sources, *targets]
    aliases = {}
    if not first:
        aliases = {len(operands) + i: i for i in range(4)}
        operands += [in_vmem(value) for value in state]
    return pl.pallas_call(
        functools.partial(first_kernel, numbers, first, last),
        out_shape=out_shape,
        in_specs=[SCALARS] + [WHOLE] * (len(operands) - 1),
        out_specs=[WHOLE] * len(out_shape),
        scratch_shapes=[
            pltpu.VMEM((2, half, depth), jnp.bfloat16),
            pltpu.VMEM((count, columns, depth), jnp.bfloat16),
            pltpu.VMEM((count, columns // 128, 128), jnp.float32),
        ],
        input_output_aliases=aliases,
        compiler_params=PARAMS,
        cost_estimate=pl.CostEstimate(
            flops=2 * count * rows * columns * depth,
            bytes_accessed=count * rows * columns,
            transcendentals=count * rows * columns,
        ),
        name="first_rows",
    )(*operands)


def call_rows(flags, cross, masses, sums):
    rows = cross.shape[1]
    return pl.pallas_call(
        row_kernel,
        out_shape=jax.ShapeDtypeStruct((rows // 128, 128), jnp.float32),
        in_specs=[SCALARS] + [WHOLE] * 3,
        out_specs=WHOLE,
        scratch_shapes=[pltpu.VMEM((rows, 128), jnp.float32)] * 2,
        compiler_params=PARAMS,
        name="rows",
    )(flags, in_vmem(cross), in_vmem(masses), sums)


def call_columns(twice, flags, cross, weights):
    rows, columns = cross.shape[1:]
    return pl.pallas_call(
        functools.partial(column_kernel, twice),
        out_shape=jax.ShapeDtypeStruct((BUFFERS, columns // 128, 128), jnp.float32),
        in_specs=[SCALARS] + [WHOLE] * 2,
        out_specs=WHOLE,
        scratch_shapes=[pltpu.VMEM((rows, 128), jnp.float32)]
        + [pltpu.VMEM((8, columns), jnp.float32)] * 2,
        compiler_params=PARAMS,
        name="columns",
    )(flags, in_vmem(cross), weights)


def fill_rows(value, before, after):
    return jnp.pad(value, ((before, after), (0, 0), (0, 0)), constant_values=NEG_FILL)


def local(src_points, src_log_mass, tgt_points, tgt_log_mass, initial_potential, pair_list, pair_count):
    block = lax.axis_index("blk")
    rep = lax.axis_index("rep")
    blocks = lax.axis_size("blk")
    core = block % 2
    half_index = (rep % 2) ^ ((block // SEGMENT) % 2)
    rows = src_points.shape[0]
    width = tgt_points.shape[0]
    columns = width // 2

    mate = send(src_points, diagonal, blocks)
    even_slots = (3, 4, 1, 5, 2, 6, 0, 7)
    odd_slots = (4, 3, 2, 6, 1, 5, 7, 0)
    place, forward, lower = lax.optimization_barrier(
        (jnp.stack([half_index, block, core]), core == 0, half_index == 0)
    )
    message, own, flags = call_message(
        1.0 / EPS_START,
        blocks,
        (even_slots, odd_slots),
        place,
        tgt_points,
        tgt_log_mass,
        initial_potential,
        src_points,
        pair_list,
        pair_count,
    )

    before = send(message, along(2, blocks), blocks)
    after = send(message, along(-2, blocks), blocks)
    tied, mate = lax.optimization_barrier((message, mate))
    third = send(tied, by_core(-3, 3, blocks), blocks)
    beside = send(message, sibling, blocks)
    sources = [own, mate]
    groups = ((0, 1), (2, 3), (4, 5, 6), (7,))

    state = call_first(groups[0], True, False, flags, sources, [message, beside], ())
    state, near = lax.optimization_barrier((state, [before, after]))
    near_beside = [send(value, sibling, blocks) for value in near]
    state = call_first(groups[1], False, False, flags, sources, near, state)
    state, third = lax.optimization_barrier((state, third))
    third_beside = send(third, sibling, blocks)
    state = call_first(groups[2], False, False, flags, sources, [*near_beside, third], state)
    *state, last = call_first(groups[3], False, True, flags, sources, [third_beside], state)
    cross, window_masses = state[:2]
    part = last.reshape(-1)

    for sweep in range(ITERS):
        epsilon = EPS_START * 0.5**sweep
        if sweep == 0:
            got = send(jnp.concatenate([part, src_log_mass]), diagonal, blocks)
            both_masses = jnp.concatenate([src_log_mass, got[2 * rows :]])
        else:
            part = call_rows(flags, cross, window_masses, column_sums).reshape(-1)
            got = send(part, diagonal, blocks)
        row_sums = log_merge(part, jnp.concatenate([got[rows : 2 * rows], got[:rows]]))
        weighted = (both_masses - row_sums).reshape(2 * rows // 128, 128)
        part = call_columns(sweep > 0, flags, cross, weighted)
        chip = log_merge(
            part,
            send(part, sibling, blocks),
            send(part, lambda b, r: (b, r ^ 2), blocks),
            send(part, lambda b, r: (b ^ 1, r ^ 2), blocks),
        )
        if sweep + 1 < ITERS:
            got = []
            for n in (1, 2, 3):
                kept_rows = 8 - 2 * n
                out = jnp.where(forward, chip[2 * n :], chip[:kept_rows])
                out = send(out, by_core(2 * n, -2 * n, blocks), blocks)
                got.append(
                    jnp.where(forward, fill_rows(out, 0, 2 * n), fill_rows(out, 2 * n, 0))
                )
            side = log_merge(*got)
            column_sums = log_merge(chip, side, send(side, sibling, blocks))
        else:
            near = jnp.where(forward, chip[5:7], chip[1:3])
            near = send(near, by_core(2, -2, blocks), blocks)
            far = jnp.where(forward, chip[7], chip[0])
            far = send(far, by_core(4, -4, blocks), blocks)
            empty = jnp.full_like(far, NEG_FILL)
            far = jnp.where(forward, jnp.stack([far, empty]), jnp.stack([empty, far]))
            side = log_merge(jnp.where(forward, chip[3:5], jnp.full_like(near, NEG_FILL)), near, far)
            over_core = send(side, sibling, blocks)
            over_half = send(side, lambda b, r: (b, r ^ 1), blocks)
            over_both = send(side, diagonal, blocks)
            mine = log_merge(side, over_core)
            other = log_merge(over_half, over_both)
            mine = jnp.where(forward, mine[0], mine[1]).reshape(columns)
            other = jnp.where(forward, other[0], other[1]).reshape(columns)
            whole = jnp.where(
                lower, jnp.concatenate([mine, other]), jnp.concatenate([other, mine])
            )
            part, src_points, tgt_points = lax.optimization_barrier((part, src_points, tgt_points))
            source_pot = half_norms(src_points) - epsilon * row_sums[:rows]
            target_pot = half_norms(tgt_points) - epsilon * whole
    return source_pot, target_pot


def solution(mesh):
    in_specs = (
        P(("blk", "rep"), None),
        P(("blk", "rep")),
        P("blk", None),
        P("blk"),
        P("blk"),
        P(),
        P(),
    )
    out_specs = (P(("blk", "rep")), P("blk"))
    return jax.shard_map(local, mesh=mesh, in_specs=in_specs, out_specs=out_specs, check_vma=False)
```

```python
import functools

import jax
import jax.numpy as jnp
from jax import lax
from jax.experimental import pallas as pl
from jax.experimental.pallas import tpu as pltpu
from jax.sharding import PartitionSpec as P

ITERS = 2
EPS_START = 0.5
NEG_FILL = -1e30
ROW_UNROLL = 8
COLUMN_UNROLL = 4
BUFFERS = 8
REPS = 4
SEGMENT = 8
TAIL = 16


def send(value, place, blocks):
    pairs = []
    for block in range(blocks):
        for rep in range(REPS):
            to_block, to_rep = place(block, rep)
            pairs.append((block * REPS + rep, to_block % blocks * REPS + to_rep))
    return lax.ppermute(value, ("blk", "rep"), pairs)


def along(steps, blocks):
    def place(block, rep):
        target = (block + steps) % blocks
        return target, rep if (target // SEGMENT - block // SEGMENT) % 2 == 0 else REPS - 1 - rep

    return place


def by_core(even_steps, odd_steps, blocks):
    even, odd = along(even_steps, blocks), along(odd_steps, blocks)
    return lambda block, rep: even(block, rep) if block % 2 == 0 else odd(block, rep)


def sibling(block, rep):
    return block ^ 1, rep


def diagonal(block, rep):
    return block ^ 1, rep ^ 1


def half_norms(points):
    widened = points.astype(jnp.float32)
    return 0.5 * jnp.sum(widened * widened, axis=1)


def terms(vector):
    parts = []
    for _ in range(3):
        parts.append(vector.astype(jnp.bfloat16).astype(jnp.float32))
        vector = vector - parts[-1]
    return parts


def log_merge(*parts):
    top = functools.reduce(jnp.maximum, parts)
    return top + jnp.log(sum(jnp.exp(part - top) for part in parts))


def spread_rows(vector_ref, bias_ref):
    for q in range(bias_ref.shape[0] // 128):
        row = vector_ref[q : q + 1, :]
        bias_ref[q * 128 : (q + 1) * 128, :] = jnp.broadcast_to(row, (128, 128)).T


def fold(value, combine):
    rows = value.shape[0]
    while rows > 8:
        rows //= 2
        value = combine(value[:rows], value[rows:])
    return value


def row_update(cross_ref, index, bias, twice, side, half, top_ref, total_ref):
    step = 64

    def chunk(r, _):
        at = pl.ds(pl.multiple_of(side * half + r * step, step), step)
        scores = []
        for q, term in enumerate(bias):
            part = cross_ref[index, at, q * 128 : (q + 1) * 128]
            scores.append((part + part if twice else part) + term)
        old = top_ref[at, :]
        top = jnp.maximum(old, functools.reduce(jnp.maximum, scores))
        total = functools.reduce(jnp.add, [jnp.exp(part - top) for part in scores])
        total_ref[at, :] = total_ref[at, :] * jnp.exp(old - top) + total
        top_ref[at, :] = top
        return 0

    lax.fori_loop(0, half // step, chunk, 0, unroll=ROW_UNROLL)


def row_finish(top_ref, total_ref, out):
    for q in range(out.shape[0]):
        top = top_ref[q * 128 : (q + 1) * 128, :].T
        greatest = jnp.max(top, axis=0, keepdims=True)
        total = total_ref[q * 128 : (q + 1) * 128, :].T * jnp.exp(top - greatest)
        out[q : q + 1, :] = greatest + jnp.log(jnp.sum(total, axis=0, keepdims=True))


def each_listed(flags, body):
    def unit(u, _):
        entry = flags[4 * BUFFERS + u]
        body(lax.div(entry, 2), lax.rem(entry, 2))
        return 0

    lax.fori_loop(0, flags[3 * BUFFERS], unit, 0)


def each_kept(flags, first, count, body):
    def unit(u, _):
        number, side = first + lax.div(u, 2), lax.rem(u, 2)

        @pl.when(flags[side * BUFFERS + number] != 0)
        def _():
            body(number, side)

        return 0

    lax.fori_loop(0, 2 * count, unit, 0)


def flags_kernel(blocks, slots, place, pair_list, pair_count, flags, list_ref, count_ref, sems):
    copies = [
        pltpu.make_async_copy(pair_list, list_ref, sems.at[0]),
        pltpu.make_async_copy(pair_count, count_ref, sems.at[1]),
    ]
    for copy in copies:
        copy.start()
    for copy in copies:
        copy.wait()
    pair_list, pair_count = list_ref, count_ref
    block, core = place[1], place[2]
    sources = (block, block + 1 - 2 * core)
    entries = pair_list.shape[0]
    lists = [[pair_list[j, source] for j in range(entries)] for source in sources]
    counts = [pair_count[source] for source in sources]
    total = jnp.int32(0)
    for u in range(2 * BUFFERS):
        flags[4 * BUFFERS + u] = jnp.int32(0)
    for number in range(BUFFERS):
        slot = jnp.where(core == 0, jnp.int32(slots[0][number]), jnp.int32(slots[1][number]))
        name = lax.rem(block - core - 3 + slot + blocks, jnp.int32(blocks))
        flags[2 * BUFFERS + number] = slot
        for side in range(2):
            kept = jnp.int32(0)
            for j in range(entries):
                same = (lists[side][j] == name) & (j < counts[side])
                kept = jnp.where(same, jnp.int32(1), kept)
            flags[side * BUFFERS + number] = kept
            flags[4 * BUFFERS + total] = jnp.int32(2 * number + side)
            total = total + kept
    for number in range(BUFFERS):
        flags[3 * BUFFERS + number] = total


def message_kernel(
    scale, half, points, masses, initial, src, out, src_out, block_ref, mass_ref, initial_ref, sems
):
    columns, depth = block_ref.shape
    src_copy = pltpu.make_async_copy(src, src_out, sems.at[1])
    copy = pltpu.make_async_copy(
        points.at[pl.ds(pl.multiple_of(half[0] * columns, columns), columns), :], block_ref, sems.at[0]
    )
    small = [
        pltpu.make_async_copy(masses, mass_ref, sems.at[2]),
        pltpu.make_async_copy(initial, initial_ref, sems.at[3]),
    ]
    for start in (copy, *small, src_copy):
        start.start()
    copy.wait()
    value = block_ref[...].astype(jnp.float32)
    out[:columns, :] = (value * scale).astype(jnp.bfloat16)
    squares = value * value
    high = squares.astype(jnp.bfloat16)
    low = (squares - high.astype(jnp.float32)).astype(jnp.bfloat16)
    ones = jnp.ones((8, depth), jnp.bfloat16)
    norms = sum(
        lax.dot_general(ones, part, (((1,), (1,)), ((), ())), preferred_element_type=jnp.float32)
        for part in (high, low)
    )
    count = columns // 128
    norms = jnp.concatenate([norms[0:1, q * 128 : (q + 1) * 128] for q in range(count)], axis=0)

    def pick(ref):
        return jnp.where(half[0] == 0, ref[:count, :], ref[count:, :])

    for copy in small:
        copy.wait()
    mass = pick(mass_ref)
    bias = mass + (pick(initial_ref) - 0.5 * norms) * scale
    rows = [jnp.concatenate(pair, axis=1) for pair in zip(terms(bias), terms(mass))]
    rows.append(jnp.zeros((TAIL - 3 * count, 256), jnp.float32))
    out[columns:, :] = jnp.concatenate(rows, axis=0).astype(jnp.bfloat16)
    src_copy.wait()


def first_kernel(numbers, first, last, flags, *refs):
    sources, targets = refs[:2], refs[2 : 2 + len(numbers)]
    refs = refs[2 + len(numbers) :]
    if not first:
        refs = refs[4:]
    cross, masses, top_ref, total_ref = refs[:4]
    src_ref, tgt_ref, bias_ref = refs[-3:]
    if first:
        top_ref[...] = jnp.full(top_ref.shape, NEG_FILL, jnp.float32)
        total_ref[...] = jnp.zeros(total_ref.shape, jnp.float32)
    half = sources[0].shape[0]
    width = cross.shape[2]
    for side, src in enumerate(sources):
        src_ref[side] = src[...]
    for k, number in enumerate(numbers):
        tgt_ref[k] = targets[k][:width, :]
        tail = targets[k][width:, :].astype(jnp.float32)
        count = width // 128
        vectors = tail[:count] + tail[count : 2 * count] + tail[2 * count : 3 * count]
        bias_ref[k] = vectors[:, :128]
        masses[number] = vectors[:, 128:]

    def body(number, side):
        k = number - numbers[0]
        for c in range(0, width, 256):
            for r in range(0, half, 256):
                at = pl.ds(pl.multiple_of(side * half + r, 256), 256)
                cross[number, at, c : c + 256] = lax.dot_general(
                    src_ref[side, r : r + 256, :],
                    tgt_ref[k, c : c + 256, :],
                    (((1,), (1,)), ((), ())),
                    preferred_element_type=jnp.float32,
                )
        bias = [bias_ref[k, q : q + 1, :] for q in range(width // 128)]
        row_update(cross, number, bias, False, side, half, top_ref, total_ref)

    each_kept(flags, numbers[0], len(numbers), body)
    if last:
        row_finish(top_ref, total_ref, refs[4])


def row_kernel(flags, cross, masses, sums, out, top_ref, total_ref):
    top_ref[...] = jnp.full(top_ref.shape, NEG_FILL, jnp.float32)
    total_ref[...] = jnp.zeros(total_ref.shape, jnp.float32)
    half = top_ref.shape[0] // 2

    def body(number, side):
        slot = flags[2 * BUFFERS + number]
        bias = [
            masses[number, q : q + 1, :] - 2.0 * sums[slot, q : q + 1, :] for q in range(masses.shape[1])
        ]
        row_update(cross, number, bias, True, side, half, top_ref, total_ref)

    each_listed(flags, body)
    row_finish(top_ref, total_ref, out)


def column_kernel(twice, flags, cross, weights, out, bias, top_ref, total_ref):
    out[...] = jnp.full(out.shape, NEG_FILL, jnp.float32)
    spread_rows(weights, bias)
    half = bias.shape[0] // 2
    pieces = cross.shape[2] // 128
    step = 128

    def body(number, side):
        def chunk(r, state):
            at = pl.ds(pl.multiple_of(side * half + r * step, step), step)
            weight = bias[at, :]
            tops, totals = [], []
            for q in range(pieces):
                part = cross[number, at, q * 128 : (q + 1) * 128]
                scores = (part + part if twice else part) + weight
                top = jnp.maximum(state[0][q], fold(scores, jnp.maximum))
                total = jnp.sum(jnp.exp(scores.reshape(-1, 8, 128) - top[None]), axis=0)
                totals.append(state[1][q] * jnp.exp(state[0][q] - top) + total)
                tops.append(top)
            return tuple(tops), tuple(totals)

        going = (side == 1) & (flags[number] != 0)
        cuts = [slice(q * 128, (q + 1) * 128) for q in range(pieces)]
        state = (
            tuple(jnp.where(going, top_ref[:, cut], NEG_FILL) for cut in cuts),
            tuple(jnp.where(going, total_ref[:, cut], 0.0) for cut in cuts),
        )
        tops, totals = lax.fori_loop(0, half // step, chunk, state, unroll=COLUMN_UNROLL)
        more = (side == 0) & (flags[BUFFERS + number] != 0)

        @pl.when(more)
        def _():
            for cut, top, total in zip(cuts, tops, totals):
                top_ref[:, cut] = top
                total_ref[:, cut] = total

        @pl.when(jnp.logical_not(more))
        def _():
            slot = flags[2 * BUFFERS + number]
            for q, (top, total) in enumerate(zip(tops, totals)):
                greatest = jnp.max(top, axis=0, keepdims=True)
                total = jnp.sum(total * jnp.exp(top - greatest), axis=0, keepdims=True)
                out[slot, q : q + 1, :] = greatest + jnp.log(total)

    each_listed(flags, body)


WHOLE = pl.BlockSpec(memory_space=pltpu.VMEM)
SCALARS = pl.BlockSpec(memory_space=pltpu.SMEM)
PARAMS = pltpu.CompilerParams(vmem_limit_bytes=20 * 2**20)


def in_vmem(value):
    return pltpu.with_memory_space_constraint(value, pltpu.VMEM)


def in_hbm(value):
    return pltpu.with_memory_space_constraint(value, pltpu.HBM)


def call_flags(blocks, slots, place, pair_list, pair_count):
    return pl.pallas_call(
        functools.partial(flags_kernel, blocks, slots),
        out_shape=jax.ShapeDtypeStruct((6 * BUFFERS,), jnp.int32),
        in_specs=[SCALARS] + [pl.BlockSpec(memory_space=pltpu.HBM)] * 2,
        out_specs=SCALARS,
        scratch_shapes=[
            pltpu.SMEM(pair_list.shape[::-1], jnp.int32),
            pltpu.SMEM(pair_count.shape, jnp.int32),
            pltpu.SemaphoreType.DMA((2,)),
        ],
        compiler_params=PARAMS,
        name="flags",
    )(place, in_hbm(pair_list.T), in_hbm(pair_count))


def call_message(scale, half, points, masses, initial, src):
    columns, depth = points.shape[0] // 2, points.shape[1]
    return pl.pallas_call(
        functools.partial(message_kernel, scale),
        out_shape=[
            pltpu.VMEM((columns + TAIL, depth), jnp.bfloat16),
            pltpu.VMEM(src.shape, jnp.bfloat16),
        ],
        in_specs=[SCALARS] + [pl.BlockSpec(memory_space=pltpu.HBM)] * 4,
        out_specs=[WHOLE] * 2,
        scratch_shapes=[
            pltpu.VMEM((columns, depth), jnp.bfloat16),
            pltpu.VMEM((2 * columns // 128, 128), jnp.float32),
            pltpu.VMEM((2 * columns // 128, 128), jnp.float32),
            pltpu.SemaphoreType.DMA((4,)),
        ],
        compiler_params=PARAMS,
        name="message",
    )(
        half,
        *map(in_hbm, (points, masses.reshape(-1, 128), initial.reshape(-1, 128), src)),
    )


def call_first(numbers, first, last, flags, sources, targets, state):
    half, depth = sources[0].shape
    rows, columns, count = 2 * half, targets[0].shape[0] - TAIL, len(numbers)
    out_shape = [
        pltpu.VMEM((BUFFERS, rows, columns), jnp.float32),
        pltpu.VMEM((BUFFERS, columns // 128, 128), jnp.float32),
        pltpu.VMEM((rows, 128), jnp.float32),
        pltpu.VMEM((rows, 128), jnp.float32),
    ]
    if last:
        out_shape.append(jax.ShapeDtypeStruct((rows // 128, 128), jnp.float32))
    operands = [flags, *sources, *targets]
    aliases = {}
    if not first:
        aliases = {len(operands) + i: i for i in range(4)}
        operands += [in_vmem(value) for value in state]
    return pl.pallas_call(
        functools.partial(first_kernel, numbers, first, last),
        out_shape=out_shape,
        in_specs=[SCALARS] + [WHOLE] * (len(operands) - 1),
        out_specs=[WHOLE] * len(out_shape),
        scratch_shapes=[
            pltpu.VMEM((2, half, depth), jnp.bfloat16),
            pltpu.VMEM((count, columns, depth), jnp.bfloat16),
            pltpu.VMEM((count, columns // 128, 128), jnp.float32),
        ],
        input_output_aliases=aliases,
        compiler_params=PARAMS,
        cost_estimate=pl.CostEstimate(
            flops=2 * count * rows * columns * depth,
            bytes_accessed=count * rows * columns,
            transcendentals=count * rows * columns,
        ),
        name="first_rows",
    )(*operands)


def call_rows(flags, cross, masses, sums):
    rows = cross.shape[1]
    return pl.pallas_call(
        row_kernel,
        out_shape=jax.ShapeDtypeStruct((rows // 128, 128), jnp.float32),
        in_specs=[SCALARS] + [WHOLE] * 3,
        out_specs=WHOLE,
        scratch_shapes=[pltpu.VMEM((rows, 128), jnp.float32)] * 2,
        compiler_params=PARAMS,
        name="rows",
    )(flags, in_vmem(cross), in_vmem(masses), sums)


def call_columns(twice, flags, cross, weights):
    rows, columns = cross.shape[1:]
    return pl.pallas_call(
        functools.partial(column_kernel, twice),
        out_shape=jax.ShapeDtypeStruct((BUFFERS, columns // 128, 128), jnp.float32),
        in_specs=[SCALARS] + [WHOLE] * 2,
        out_specs=WHOLE,
        scratch_shapes=[pltpu.VMEM((rows, 128), jnp.float32)]
        + [pltpu.VMEM((8, columns), jnp.float32)] * 2,
        compiler_params=PARAMS,
        name="columns",
    )(flags, in_vmem(cross), weights)


def fill_rows(value, before, after):
    return jnp.pad(value, ((before, after), (0, 0), (0, 0)), constant_values=NEG_FILL)


def local(src_points, src_log_mass, tgt_points, tgt_log_mass, initial_potential, pair_list, pair_count):
    block = lax.axis_index("blk")
    rep = lax.axis_index("rep")
    blocks = lax.axis_size("blk")
    core = block % 2
    half_index = (rep % 2) ^ ((block // SEGMENT) % 2)
    rows = src_points.shape[0]
    width = tgt_points.shape[0]
    columns = width // 2

    mate = send(src_points, diagonal, blocks)
    even_slots = (3, 4, 1, 5, 2, 6, 0, 7)
    odd_slots = (4, 3, 2, 6, 1, 5, 7, 0)
    place, forward, lower = lax.optimization_barrier(
        (jnp.stack([half_index, block, core]), core == 0, half_index == 0)
    )
    message, own = call_message(
        1.0 / EPS_START,
        place,
        tgt_points,
        tgt_log_mass,
        initial_potential,
        src_points,
    )

    before = send(message, along(2, blocks), blocks)
    after = send(message, along(-2, blocks), blocks)
    tied, mate, place = lax.optimization_barrier((message, mate, place))
    flags = call_flags(blocks, (even_slots, odd_slots), place, pair_list, pair_count)
    third = send(tied, by_core(-3, 3, blocks), blocks)
    beside = send(message, sibling, blocks)
    sources = [own, mate]
    groups = ((0, 1), (2, 3), (4, 5, 6), (7,))

    state = call_first(groups[0], True, False, flags, sources, [message, beside], ())
    state, near = lax.optimization_barrier((state, [before, after]))
    near_beside = [send(value, sibling, blocks) for value in near]
    state = call_first(groups[1], False, False, flags, sources, near, state)
    state, third = lax.optimization_barrier((state, third))
    third_beside = send(third, sibling, blocks)
    state = call_first(groups[2], False, False, flags, sources, [*near_beside, third], state)
    *state, last = call_first(groups[3], False, True, flags, sources, [third_beside], state)
    cross, window_masses = state[:2]
    part = last.reshape(-1)

    for sweep in range(ITERS):
        epsilon = EPS_START * 0.5**sweep
        if sweep == 0:
            got = send(jnp.concatenate([part, src_log_mass]), diagonal, blocks)
            both_masses = jnp.concatenate([src_log_mass, got[2 * rows :]])
        else:
            part = call_rows(flags, cross, window_masses, column_sums).reshape(-1)
            got = send(part, diagonal, blocks)
        row_sums = log_merge(part, jnp.concatenate([got[rows : 2 * rows], got[:rows]]))
        weighted = (both_masses - row_sums).reshape(2 * rows // 128, 128)
        part = call_columns(sweep > 0, flags, cross, weighted)
        chip = log_merge(
            part,
            send(part, sibling, blocks),
            send(part, lambda b, r: (b, r ^ 2), blocks),
            send(part, lambda b, r: (b ^ 1, r ^ 2), blocks),
        )
        if sweep + 1 < ITERS:
            got = []
            for n in (1, 2, 3):
                kept_rows = 8 - 2 * n
                out = jnp.where(forward, chip[2 * n :], chip[:kept_rows])
                out = send(out, by_core(2 * n, -2 * n, blocks), blocks)
                got.append(
                    jnp.where(forward, fill_rows(out, 0, 2 * n), fill_rows(out, 2 * n, 0))
                )
            side = log_merge(*got)
            column_sums = log_merge(chip, side, send(side, sibling, blocks))
        else:
            near = jnp.where(forward, chip[5:7], chip[1:3])
            near = send(near, by_core(2, -2, blocks), blocks)
            far = jnp.where(forward, chip[7], chip[0])
            far = send(far, by_core(4, -4, blocks), blocks)
            empty = jnp.full_like(far, NEG_FILL)
            far = jnp.where(forward, jnp.stack([far, empty]), jnp.stack([empty, far]))
            side = log_merge(jnp.where(forward, chip[3:5], jnp.full_like(near, NEG_FILL)), near, far)
            over_core = send(side, sibling, blocks)
            over_half = send(side, lambda b, r: (b, r ^ 1), blocks)
            over_both = send(side, diagonal, blocks)
            mine = log_merge(side, over_core)
            other = log_merge(over_half, over_both)
            mine = jnp.where(forward, mine[0], mine[1]).reshape(columns)
            other = jnp.where(forward, other[0], other[1]).reshape(columns)
            whole = jnp.where(
                lower, jnp.concatenate([mine, other]), jnp.concatenate([other, mine])
            )
            part, src_points, tgt_points = lax.optimization_barrier((part, src_points, tgt_points))
            source_pot = half_norms(src_points) - epsilon * row_sums[:rows]
            target_pot = half_norms(tgt_points) - epsilon * whole
    return source_pot, target_pot


def solution(mesh):
    in_specs = (
        P(("blk", "rep"), None),
        P(("blk", "rep")),
        P("blk", None),
        P("blk"),
        P("blk"),
        P(),
        P(),
    )
    out_specs = (P(("blk", "rep")), P("blk"))
    return jax.shard_map(local, mesh=mesh, in_specs=in_specs, out_specs=out_specs, check_vma=False)
```

```python
import functools

import jax
import jax.numpy as jnp
from jax import lax
from jax.experimental import pallas as pl
from jax.experimental.pallas import tpu as pltpu
from jax.sharding import PartitionSpec as P

ITERS = 2
EPS_START = 0.5
NEG_FILL = -1e30
ROW_UNROLL = 8
COLUMN_UNROLL = 4
BUFFERS = 8
REPS = 4
SEGMENT = 8
TAIL = 16


def send(value, place, blocks):
    pairs = []
    for block in range(blocks):
        for rep in range(REPS):
            to_block, to_rep = place(block, rep)
            pairs.append((block * REPS + rep, to_block % blocks * REPS + to_rep))
    return lax.ppermute(value, ("blk", "rep"), pairs)


def along(steps, blocks):
    def place(block, rep):
        target = (block + steps) % blocks
        return target, rep if (target // SEGMENT - block // SEGMENT) % 2 == 0 else REPS - 1 - rep

    return place


def by_core(even_steps, odd_steps, blocks):
    even, odd = along(even_steps, blocks), along(odd_steps, blocks)
    return lambda block, rep: even(block, rep) if block % 2 == 0 else odd(block, rep)


def sibling(block, rep):
    return block ^ 1, rep


def diagonal(block, rep):
    return block ^ 1, rep ^ 1


def half_norms(points):
    widened = points.astype(jnp.float32)
    return 0.5 * jnp.sum(widened * widened, axis=1)


def terms(vector):
    parts = []
    for _ in range(3):
        parts.append(vector.astype(jnp.bfloat16).astype(jnp.float32))
        vector = vector - parts[-1]
    return parts


def log_merge(*parts):
    top = functools.reduce(jnp.maximum, parts)
    return top + jnp.log(sum(jnp.exp(part - top) for part in parts))


def spread_rows(vector_ref, bias_ref):
    for q in range(bias_ref.shape[0] // 128):
        row = vector_ref[q : q + 1, :]
        bias_ref[q * 128 : (q + 1) * 128, :] = jnp.broadcast_to(row, (128, 128)).T


def fold(value, combine):
    rows = value.shape[0]
    while rows > 8:
        rows //= 2
        value = combine(value[:rows], value[rows:])
    return value


def row_update(cross_ref, index, bias, twice, side, half, top_ref, total_ref):
    step = 64

    def chunk(r, _):
        at = pl.ds(pl.multiple_of(side * half + r * step, step), step)
        scores = []
        for q, term in enumerate(bias):
            part = cross_ref[index, at, q * 128 : (q + 1) * 128]
            scores.append((part + part if twice else part) + term)
        old = top_ref[at, :]
        top = jnp.maximum(old, functools.reduce(jnp.maximum, scores))
        total = functools.reduce(jnp.add, [jnp.exp(part - top) for part in scores])
        total_ref[at, :] = total_ref[at, :] * jnp.exp(old - top) + total
        top_ref[at, :] = top
        return 0

    lax.fori_loop(0, half // step, chunk, 0, unroll=ROW_UNROLL)


def row_finish(top_ref, total_ref, out):
    for q in range(out.shape[0]):
        top = top_ref[q * 128 : (q + 1) * 128, :].T
        greatest = jnp.max(top, axis=0, keepdims=True)
        total = total_ref[q * 128 : (q + 1) * 128, :].T * jnp.exp(top - greatest)
        out[q : q + 1, :] = greatest + jnp.log(jnp.sum(total, axis=0, keepdims=True))


def each_listed(flags, body):
    def unit(u, _):
        entry = flags[4 * BUFFERS + u]
        body(lax.div(entry, 2), lax.rem(entry, 2))
        return 0

    lax.fori_loop(0, flags[3 * BUFFERS], unit, 0)


def each_kept(flags, first, count, body):
    def unit(u, _):
        number, side = first + lax.div(u, 2), lax.rem(u, 2)

        @pl.when(flags[side * BUFFERS + number] != 0)
        def _():
            body(number, side)

        return 0

    lax.fori_loop(0, 2 * count, unit, 0)


def flags_kernel(blocks, slots, place, pair_list, pair_count, flags, list_ref, count_ref, sems):
    copies = [
        pltpu.make_async_copy(pair_list, list_ref, sems.at[0]),
        pltpu.make_async_copy(pair_count, count_ref, sems.at[1]),
    ]
    for copy in copies:
        copy.start()
    for copy in copies:
        copy.wait()
    pair_list, pair_count = list_ref, count_ref
    block, core = place[1], place[2]
    sources = (block, block + 1 - 2 * core)
    entries = pair_list.shape[0]
    lists = [[pair_list[j, source] for j in range(entries)] for source in sources]
    counts = [pair_count[source] for source in sources]
    total = jnp.int32(0)
    for u in range(2 * BUFFERS):
        flags[4 * BUFFERS + u] = jnp.int32(0)
    for number in range(BUFFERS):
        slot = jnp.where(core == 0, jnp.int32(slots[0][number]), jnp.int32(slots[1][number]))
        name = lax.rem(block - core - 3 + slot + blocks, jnp.int32(blocks))
        flags[2 * BUFFERS + number] = slot
        for side in range(2):
            kept = jnp.int32(0)
            for j in range(entries):
                same = (lists[side][j] == name) & (j < counts[side])
                kept = jnp.where(same, jnp.int32(1), kept)
            flags[side * BUFFERS + number] = kept
            flags[4 * BUFFERS + total] = jnp.int32(2 * number + side)
            total = total + kept
    for number in range(BUFFERS):
        flags[3 * BUFFERS + number] = total


def message_kernel(
    scale, half, points, masses, initial, src, out, src_out, block_ref, mass_ref, initial_ref, sems
):
    columns, depth = block_ref.shape
    src_copy = pltpu.make_async_copy(src, src_out, sems.at[1])
    copy = pltpu.make_async_copy(
        points.at[pl.ds(pl.multiple_of(half[0] * columns, columns), columns), :], block_ref, sems.at[0]
    )
    small = [
        pltpu.make_async_copy(masses, mass_ref, sems.at[2]),
        pltpu.make_async_copy(initial, initial_ref, sems.at[3]),
    ]
    for start in (copy, *small, src_copy):
        start.start()
    copy.wait()
    value = block_ref[...].astype(jnp.float32)
    out[:columns, :] = (value * scale).astype(jnp.bfloat16)
    squares = value * value
    high = squares.astype(jnp.bfloat16)
    low = (squares - high.astype(jnp.float32)).astype(jnp.bfloat16)
    ones = jnp.ones((8, depth), jnp.bfloat16)
    norms = sum(
        lax.dot_general(ones, part, (((1,), (1,)), ((), ())), preferred_element_type=jnp.float32)
        for part in (high, low)
    )
    count = columns // 128
    norms = jnp.concatenate([norms[0:1, q * 128 : (q + 1) * 128] for q in range(count)], axis=0)

    def pick(ref):
        return jnp.where(half[0] == 0, ref[:count, :], ref[count:, :])

    for copy in small:
        copy.wait()
    mass = pick(mass_ref)
    bias = mass + (pick(initial_ref) - 0.5 * norms) * scale
    rows = [jnp.concatenate(pair, axis=1) for pair in zip(terms(bias), terms(mass))]
    rows.append(jnp.zeros((TAIL - 3 * count, 256), jnp.float32))
    out[columns:, :] = jnp.concatenate(rows, axis=0).astype(jnp.bfloat16)
    src_copy.wait()


def first_kernel(numbers, first, last, flags, *refs):
    targets, refs = refs[: len(numbers)], refs[len(numbers) :]
    sources, refs = (refs[:2], refs[2:]) if first else ((), refs[5:])
    cross, masses, top_ref, total_ref, src_ref = refs[:5]
    tgt_ref, bias_ref = refs[-2:]
    if first:
        top_ref[...] = jnp.full(top_ref.shape, NEG_FILL, jnp.float32)
        total_ref[...] = jnp.zeros(total_ref.shape, jnp.float32)
    half = src_ref.shape[1]
    width = cross.shape[2]
    for side, src in enumerate(sources):
        src_ref[side] = src[...]
    for k, number in enumerate(numbers):
        tgt_ref[k] = targets[k][:width, :]
        tail = targets[k][width:, :].astype(jnp.float32)
        count = width // 128
        vectors = tail[:count] + tail[count : 2 * count] + tail[2 * count : 3 * count]
        bias_ref[k] = vectors[:, :128]
        masses[number] = vectors[:, 128:]

    def body(number, side):
        k = number - numbers[0]
        for c in range(0, width, 256):
            for r in range(0, half, 256):
                at = pl.ds(pl.multiple_of(side * half + r, 256), 256)
                cross[number, at, c : c + 256] = lax.dot_general(
                    src_ref[side, r : r + 256, :],
                    tgt_ref[k, c : c + 256, :],
                    (((1,), (1,)), ((), ())),
                    preferred_element_type=jnp.float32,
                )
        bias = [bias_ref[k, q : q + 1, :] for q in range(width // 128)]
        row_update(cross, number, bias, False, side, half, top_ref, total_ref)

    each_kept(flags, numbers[0], len(numbers), body)
    if last:
        row_finish(top_ref, total_ref, refs[5])


def row_kernel(flags, cross, masses, sums, out, top_ref, total_ref):
    top_ref[...] = jnp.full(top_ref.shape, NEG_FILL, jnp.float32)
    total_ref[...] = jnp.zeros(total_ref.shape, jnp.float32)
    half = top_ref.shape[0] // 2

    def body(number, side):
        slot = flags[2 * BUFFERS + number]
        bias = [
            masses[number, q : q + 1, :] - 2.0 * sums[slot, q : q + 1, :] for q in range(masses.shape[1])
        ]
        row_update(cross, number, bias, True, side, half, top_ref, total_ref)

    each_listed(flags, body)
    row_finish(top_ref, total_ref, out)


def column_kernel(twice, flags, cross, weights, out, bias, top_ref, total_ref):
    out[...] = jnp.full(out.shape, NEG_FILL, jnp.float32)
    spread_rows(weights, bias)
    half = bias.shape[0] // 2
    pieces = cross.shape[2] // 128
    step = 128

    def body(number, side):
        def chunk(r, state):
            at = pl.ds(pl.multiple_of(side * half + r * step, step), step)
            weight = bias[at, :]
            tops, totals = [], []
            for q in range(pieces):
                part = cross[number, at, q * 128 : (q + 1) * 128]
                scores = (part + part if twice else part) + weight
                top = jnp.maximum(state[0][q], fold(scores, jnp.maximum))
                total = jnp.sum(jnp.exp(scores.reshape(-1, 8, 128) - top[None]), axis=0)
                totals.append(state[1][q] * jnp.exp(state[0][q] - top) + total)
                tops.append(top)
            return tuple(tops), tuple(totals)

        going = (side == 1) & (flags[number] != 0)
        cuts = [slice(q * 128, (q + 1) * 128) for q in range(pieces)]
        state = (
            tuple(jnp.where(going, top_ref[:, cut], NEG_FILL) for cut in cuts),
            tuple(jnp.where(going, total_ref[:, cut], 0.0) for cut in cuts),
        )
        tops, totals = lax.fori_loop(0, half // step, chunk, state, unroll=COLUMN_UNROLL)
        more = (side == 0) & (flags[BUFFERS + number] != 0)

        @pl.when(more)
        def _():
            for cut, top, total in zip(cuts, tops, totals):
                top_ref[:, cut] = top
                total_ref[:, cut] = total

        @pl.when(jnp.logical_not(more))
        def _():
            slot = flags[2 * BUFFERS + number]
            for q, (top, total) in enumerate(zip(tops, totals)):
                greatest = jnp.max(top, axis=0, keepdims=True)
                total = jnp.sum(total * jnp.exp(top - greatest), axis=0, keepdims=True)
                out[slot, q : q + 1, :] = greatest + jnp.log(total)

    each_listed(flags, body)


WHOLE = pl.BlockSpec(memory_space=pltpu.VMEM)
SCALARS = pl.BlockSpec(memory_space=pltpu.SMEM)
PARAMS = pltpu.CompilerParams(vmem_limit_bytes=20 * 2**20)


def in_vmem(value):
    return pltpu.with_memory_space_constraint(value, pltpu.VMEM)


def in_hbm(value):
    return pltpu.with_memory_space_constraint(value, pltpu.HBM)


def call_flags(blocks, slots, place, pair_list, pair_count):
    return pl.pallas_call(
        functools.partial(flags_kernel, blocks, slots),
        out_shape=jax.ShapeDtypeStruct((6 * BUFFERS,), jnp.int32),
        in_specs=[SCALARS] + [pl.BlockSpec(memory_space=pltpu.HBM)] * 2,
        out_specs=SCALARS,
        scratch_shapes=[
            pltpu.SMEM(pair_list.shape[::-1], jnp.int32),
            pltpu.SMEM(pair_count.shape, jnp.int32),
            pltpu.SemaphoreType.DMA((2,)),
        ],
        compiler_params=PARAMS,
        name="flags",
    )(place, in_hbm(pair_list.T), in_hbm(pair_count))


def call_message(scale, half, points, masses, initial, src):
    columns, depth = points.shape[0] // 2, points.shape[1]
    return pl.pallas_call(
        functools.partial(message_kernel, scale),
        out_shape=[
            pltpu.VMEM((columns + TAIL, depth), jnp.bfloat16),
            pltpu.VMEM(src.shape, jnp.bfloat16),
        ],
        in_specs=[SCALARS] + [pl.BlockSpec(memory_space=pltpu.HBM)] * 4,
        out_specs=[WHOLE] * 2,
        scratch_shapes=[
            pltpu.VMEM((columns, depth), jnp.bfloat16),
            pltpu.VMEM((2 * columns // 128, 128), jnp.float32),
            pltpu.VMEM((2 * columns // 128, 128), jnp.float32),
            pltpu.SemaphoreType.DMA((4,)),
        ],
        compiler_params=PARAMS,
        name="message",
    )(
        half,
        *map(in_hbm, (points, masses.reshape(-1, 128), initial.reshape(-1, 128), src)),
    )


def call_first(numbers, first, last, flags, sources, targets, state):
    half, depth = sources[0].shape
    rows, columns, count = 2 * half, targets[0].shape[0] - TAIL, len(numbers)
    out_shape = [
        pltpu.VMEM((BUFFERS, rows, columns), jnp.float32),
        pltpu.VMEM((BUFFERS, columns // 128, 128), jnp.float32),
        pltpu.VMEM((rows, 128), jnp.float32),
        pltpu.VMEM((rows, 128), jnp.float32),
        pltpu.VMEM((2, half, depth), jnp.bfloat16),
    ]
    if last:
        out_shape.append(jax.ShapeDtypeStruct((rows // 128, 128), jnp.float32))
    operands = [flags, *targets]
    aliases = {}
    if first:
        operands += sources
    else:
        aliases = {len(operands) + i: i for i in range(5)}
        operands += [in_vmem(value) for value in state]
    return pl.pallas_call(
        functools.partial(first_kernel, numbers, first, last),
        out_shape=out_shape,
        in_specs=[SCALARS] + [WHOLE] * (len(operands) - 1),
        out_specs=[WHOLE] * len(out_shape),
        scratch_shapes=[
            pltpu.VMEM((count, columns, depth), jnp.bfloat16),
            pltpu.VMEM((count, columns // 128, 128), jnp.float32),
        ],
        input_output_aliases=aliases,
        compiler_params=PARAMS,
        cost_estimate=pl.CostEstimate(
            flops=2 * count * rows * columns * depth,
            bytes_accessed=count * rows * columns,
            transcendentals=count * rows * columns,
        ),
        name="first_rows",
    )(*operands)


def call_rows(flags, cross, masses, sums):
    rows = cross.shape[1]
    return pl.pallas_call(
        row_kernel,
        out_shape=jax.ShapeDtypeStruct((rows // 128, 128), jnp.float32),
        in_specs=[SCALARS] + [WHOLE] * 3,
        out_specs=WHOLE,
        scratch_shapes=[pltpu.VMEM((rows, 128), jnp.float32)] * 2,
        compiler_params=PARAMS,
        name="rows",
    )(flags, in_vmem(cross), in_vmem(masses), sums)


def call_columns(twice, flags, cross, weights):
    rows, columns = cross.shape[1:]
    return pl.pallas_call(
        functools.partial(column_kernel, twice),
        out_shape=jax.ShapeDtypeStruct((BUFFERS, columns // 128, 128), jnp.float32),
        in_specs=[SCALARS] + [WHOLE] * 2,
        out_specs=WHOLE,
        scratch_shapes=[pltpu.VMEM((rows, 128), jnp.float32)]
        + [pltpu.VMEM((8, columns), jnp.float32)] * 2,
        compiler_params=PARAMS,
        name="columns",
    )(flags, in_vmem(cross), weights)


def fill_rows(value, before, after):
    return jnp.pad(value, ((before, after), (0, 0), (0, 0)), constant_values=NEG_FILL)


def local(src_points, src_log_mass, tgt_points, tgt_log_mass, initial_potential, pair_list, pair_count):
    block = lax.axis_index("blk")
    rep = lax.axis_index("rep")
    blocks = lax.axis_size("blk")
    core = block % 2
    half_index = (rep % 2) ^ ((block // SEGMENT) % 2)
    rows = src_points.shape[0]
    width = tgt_points.shape[0]
    columns = width // 2

    mate = send(src_points, diagonal, blocks)
    even_slots = (3, 4, 1, 5, 2, 6, 0, 7)
    odd_slots = (4, 3, 2, 6, 1, 5, 7, 0)
    place, forward, lower = lax.optimization_barrier(
        (jnp.stack([half_index, block, core]), core == 0, half_index == 0)
    )
    message, own = call_message(
        1.0 / EPS_START,
        place,
        tgt_points,
        tgt_log_mass,
        initial_potential,
        src_points,
    )

    before = send(message, along(2, blocks), blocks)
    after = send(message, along(-2, blocks), blocks)
    tied, mate, place = lax.optimization_barrier((message, mate, place))
    flags = call_flags(blocks, (even_slots, odd_slots), place, pair_list, pair_count)
    third = send(tied, by_core(-3, 3, blocks), blocks)
    beside = send(message, sibling, blocks)
    sources = [own, mate]
    groups = ((0, 1), (2, 3), (4, 5, 6), (7,))

    state = call_first(groups[0], True, False, flags, sources, [message, beside], ())
    state, near = lax.optimization_barrier((state, [before, after]))
    near_beside = [send(value, sibling, blocks) for value in near]
    state = call_first(groups[1], False, False, flags, sources, near, state)
    state, third = lax.optimization_barrier((state, third))
    third_beside = send(third, sibling, blocks)
    state = call_first(groups[2], False, False, flags, sources, [*near_beside, third], state)
    *state, last = call_first(groups[3], False, True, flags, sources, [third_beside], state)
    cross, window_masses = state[:2]
    part = last.reshape(-1)

    for sweep in range(ITERS):
        epsilon = EPS_START * 0.5**sweep
        if sweep == 0:
            got = send(jnp.concatenate([part, src_log_mass]), diagonal, blocks)
            both_masses = jnp.concatenate([src_log_mass, got[2 * rows :]])
        else:
            part = call_rows(flags, cross, window_masses, column_sums).reshape(-1)
            got = send(part, diagonal, blocks)
        row_sums = log_merge(part, jnp.concatenate([got[rows : 2 * rows], got[:rows]]))
        weighted = (both_masses - row_sums).reshape(2 * rows // 128, 128)
        part = call_columns(sweep > 0, flags, cross, weighted)
        chip = log_merge(
            part,
            send(part, sibling, blocks),
            send(part, lambda b, r: (b, r ^ 2), blocks),
            send(part, lambda b, r: (b ^ 1, r ^ 2), blocks),
        )
        if sweep + 1 < ITERS:
            got = []
            for n in (1, 2, 3):
                kept_rows = 8 - 2 * n
                out = jnp.where(forward, chip[2 * n :], chip[:kept_rows])
                out = send(out, by_core(2 * n, -2 * n, blocks), blocks)
                got.append(
                    jnp.where(forward, fill_rows(out, 0, 2 * n), fill_rows(out, 2 * n, 0))
                )
            side = log_merge(*got)
            column_sums = log_merge(chip, side, send(side, sibling, blocks))
        else:
            near = jnp.where(forward, chip[5:7], chip[1:3])
            near = send(near, by_core(2, -2, blocks), blocks)
            far = jnp.where(forward, chip[7], chip[0])
            far = send(far, by_core(4, -4, blocks), blocks)
            empty = jnp.full_like(far, NEG_FILL)
            far = jnp.where(forward, jnp.stack([far, empty]), jnp.stack([empty, far]))
            side = log_merge(jnp.where(forward, chip[3:5], jnp.full_like(near, NEG_FILL)), near, far)
            over_core = send(side, sibling, blocks)
            over_half = send(side, lambda b, r: (b, r ^ 1), blocks)
            over_both = send(side, diagonal, blocks)
            mine = log_merge(side, over_core)
            other = log_merge(over_half, over_both)
            mine = jnp.where(forward, mine[0], mine[1]).reshape(columns)
            other = jnp.where(forward, other[0], other[1]).reshape(columns)
            whole = jnp.where(
                lower, jnp.concatenate([mine, other]), jnp.concatenate([other, mine])
            )
            part, src_points, tgt_points = lax.optimization_barrier((part, src_points, tgt_points))
            source_pot = half_norms(src_points) - epsilon * row_sums[:rows]
            target_pot = half_norms(tgt_points) - epsilon * whole
    return source_pot, target_pot


def solution(mesh):
    in_specs = (
        P(("blk", "rep"), None),
        P(("blk", "rep")),
        P("blk", None),
        P("blk"),
        P("blk"),
        P(),
        P(),
    )
    out_specs = (P(("blk", "rep")), P("blk"))
    return jax.shard_map(local, mesh=mesh, in_specs=in_specs, out_specs=out_specs, check_vma=False)
```
